256 devices in a mesh: section: 2 (over x_hi), dp: 128 (over x_lo, z, y, core).
Axes of the slice: x: 4 (x_hi: 2, x_lo: 2; x = x_hi * 2 + x_lo), y: 4, z: 8, core: 2. Of those that a mesh axis runs over, the one named last changes fastest.
Arguments:
- heat_start: float32 [4096, 32, 128], P(('section', 'dp')), may hold values from -18 to 18
- conductivity: float32 [4096, 32, 128], P(('section', 'dp')), may hold values from 0.25 to 1
- patch_z: int32 [256], P(('section', 'dp')), may hold values from 0 to 12
- patch_x: int32 [256], P(('section', 'dp')), may hold values from 0 to 24
- slot_table: int32 [256], P(('section', 'dp')), may hold values from 0 to 255, as said below
- w_stem: bfloat16 [64, 54], replicated, may hold values from -0.875 to 0.875
- w_lift: bfloat16 [64, 64], replicated, may hold values from -0.75 to 0.75
- w_down: bfloat16 [128, 1728], replicated, may hold values from -1 to 1
- w_deep: bfloat16 [128, 128], replicated, may hold values from -1 to 2
- w_merge: bfloat16 [64, 192], replicated, may hold values from -1 to 1
- w_out: bfloat16 [1, 64], replicated, may hold values from -0.75 to 0.75
Outputs:
- heat_two: float32 [4096, 32, 128], P(('section', 'dp'))
- predictions: bfloat16 [512, 4, 8, 128], P(('section', 'dp'))
- grad_pack: float32 [2048, 128], P('dp')
The draws below stay inside these ranges and needn't reach their ends.
Inputs may be any that keep to these rules, and one draw needn't show every extreme that they name: Within each section (each aligned block of 128 entries) the entries are distinct; entry s sends patch s to trainer slot_table[s] // 2 of the same section, slot slot_table[s] % 2. In each section a quarter of the trainers receive two patches, half receive one, a quarter none.
All inputs are finite; a program needn't handle non-finite values.
Results may differ from the reference program's by a relative error of at most 0.0073.
The reference program's roundings to bfloat16 on the way count: a program that leaves them out, or rounds other values in their place, can miss the bound.
Values may be sent and summed in bfloat16 or wider, within the bound.
A program may use at most 128 MiB of HBM per device.

```python
import math
from functools import partial
import jax
import jax.numpy as jnp
from jax import lax

ZD = 16
GX = 32
GY = 128
PZ = 4
PX = 8
CIN = 2
C1 = 64
C2 = 128
GROWS = 2048
SOURCES = 256
NZ = 4096
N_SECTION = 2
N_DP = 128


def draw_heat_start(key, part):
    key = jax.random.fold_in(key, 11)
    depth = jnp.arange(NZ, dtype=jnp.float32) / max(NZ - 1, 1)
    values = jax.random.uniform(key, (NZ, GX, GY), jnp.float32, -6.0, 6.0)
    rise = jnp.exp(depth * jnp.log(3.0))
    return (values * rise[:, None, None]).astype(jnp.float32)


def draw_slot_table(key, part):
    key = jax.random.fold_in(key, 7)

    def draw_section(section_key):
        key_src, key_dst = jax.random.split(section_key)
        sources = jax.random.permutation(key_src, N_DP)
        trainers = jax.random.permutation(key_dst, N_DP)
        position = jnp.argsort(sources)
        half_count = N_DP // 2
        quarter_count = N_DP // 4
        paired = trainers[position // 2]
        single = trainers[jnp.clip(quarter_count + position - half_count, 0, N_DP - 1)]
        trainer_of = jnp.where(position < half_count, paired, single)
        slot_of = jnp.where(position < half_count, position % 2, 0)
        return (2 * trainer_of + slot_of).astype(jnp.int32)
    section_keys = jax.random.split(key, N_SECTION)
    return jax.vmap(draw_section)(section_keys).reshape(-1).astype(jnp.int32)


def random_signs(key, shape):
    return jnp.where(jax.random.bernoulli(key, 0.5, shape), 1.0, -1.0).astype(jnp.float32)


def draw_w_down(key, part):
    key = jax.random.fold_in(key, 21)
    shape = (C2, 27 * C1)
    values = random_signs(key, shape)
    return (values * (27.0 * C1) ** (-0.5)).astype(jnp.bfloat16)


def draw_w_deep(key, part):
    key = jax.random.fold_in(key, 23)
    shape = (C2, C2)
    values = random_signs(key, shape)
    return (jnp.eye(C2, dtype=jnp.float32) + 0.4 * values * (1.0 * C2) ** (-0.5)).astype(jnp.bfloat16)


def draw_w_merge(key, part):
    key = jax.random.fold_in(key, 29)
    shape = (C1, C1 + C2)
    values = random_signs(key, shape)
    return (values * (1.0 * (C1 + C2)) ** (-0.5)).astype(jnp.bfloat16)


def with_ends(values, own_key, least, largest):
    longest = values.shape.index(max(values.shape))
    spots = []
    for shift in (0, 1):
        where = [jax.random.randint(jax.random.fold_in(own_key, axis), (), 0, length) for axis, length in enumerate(values.shape)]
        where[longest] = (where[longest] + shift) % values.shape[longest]
        spots.append(tuple(where))
    return values.at[spots[0]].set(least).at[spots[1]].set(largest)


def levels(key, shape, pieces, least, top_value):
    loudness = 1.0
    for dim, blocks in pieces:
        steps = jax.random.uniform(jax.random.fold_in(jax.random.fold_in(key, 6), dim), (blocks,), jnp.float32, least / len(pieces), top_value / len(pieces))
        loudness = loudness * jnp.repeat(jnp.exp(steps), shape[dim] // blocks).reshape((-1,) + (1,) * (len(shape) - 1 - dim))
    return loudness


def centred(key, dims, deviation, reach, kind=jnp.bfloat16):
    array = deviation * jax.random.normal(key, dims, jnp.float32)
    return jnp.clip(array, min=-reach, max=reach).astype(kind)


def setup_inputs(seed: int = 0) -> dict:
    arg_keys = jax.random.split(jax.random.key(seed), 12)
    return {
        "heat_start": draw_heat_start(jax.random.fold_in(arg_keys[11], 71), 0),
        "conductivity": jnp.clip(jnp.exp(math.log(1.0) - 1.3862944 * jax.random.uniform(arg_keys[1], (NZ, GX, GY), jnp.float32) ** levels(arg_keys[1], (NZ, GX, GY), ((0, 256),), -0.2, 0.2)), 0.25, 1.0),
        "patch_z": with_ends(jax.random.randint(arg_keys[2], (SOURCES,), 0, ZD - PZ + 1), jax.random.fold_in(arg_keys[2], 1), 0, ZD - PZ).astype(jnp.int32),
        "patch_x": with_ends(jax.random.randint(arg_keys[3], (SOURCES,), 0, GX - PX + 1), jax.random.fold_in(arg_keys[3], 1), 0, GX - PX).astype(jnp.int32),
        "slot_table": draw_slot_table(jax.random.fold_in(arg_keys[11], 71), 0),
        "w_stem": centred(arg_keys[5], (C1, 27 * CIN), (27 * CIN) ** -0.5, 0.875),
        "w_lift": centred(arg_keys[6], (C1, C1), C1 ** -0.5, 0.75),
        "w_down": draw_w_down(jax.random.fold_in(arg_keys[11], 71), 0),
        "w_deep": draw_w_deep(jax.random.fold_in(arg_keys[11], 71), 0),
        "w_merge": draw_w_merge(jax.random.fold_in(arg_keys[11], 71), 0),
        "w_out": centred(arg_keys[10], (1, C1), C1 ** -0.5, 0.75),
    }


TIME_STEP = 0.15

def advance(heat_ext, cond_ext):
    interior = heat_ext[1:-1]
    cond_mid = cond_ext[1:-1]
    padded_u = jnp.pad(interior, ((0, 0), (1, 1), (1, 1)))
    padded_k = jnp.pad(cond_mid, ((0, 0), (1, 1), (1, 1)))
    net_flux = 0.5 * (cond_mid + cond_ext[2:]) * (heat_ext[2:] - interior)
    net_flux = net_flux + 0.5 * (cond_mid + cond_ext[:-2]) * (heat_ext[:-2] - interior)
    net_flux = net_flux + 0.5 * (cond_mid + padded_k[:, 2:, 1:-1]) * (padded_u[:, 2:, 1:-1] - interior)
    net_flux = net_flux + 0.5 * (cond_mid + padded_k[:, :-2, 1:-1]) * (padded_u[:, :-2, 1:-1] - interior)
    net_flux = net_flux + 0.5 * (cond_mid + padded_k[:, 1:-1, 2:]) * (padded_u[:, 1:-1, 2:] - interior)
    net_flux = net_flux + 0.5 * (cond_mid + padded_k[:, 1:-1, :-2]) * (padded_u[:, 1:-1, :-2] - interior)
    return interior + TIME_STEP * net_flux

def conv_cube(activity, kernel):
    depth_z, width_x, width_y = (activity.shape[2], activity.shape[3], activity.shape[4])
    padded = jnp.pad(activity, ((0, 0), (0, 0), (1, 1), (1, 1), (1, 1)))
    shifted = [padded[:, :, offset_z:offset_z + depth_z, offset_x:offset_x + width_x, offset_y:offset_y + width_y] for offset_z in range(3) for offset_x in range(3) for offset_y in range(3)]
    columns = jnp.concatenate(shifted, axis=0)
    result = jnp.dot(kernel, columns.reshape(columns.shape[0], -1), preferred_element_type=jnp.float32)
    return result.reshape((kernel.shape[0],) + activity.shape[1:])

def pointwise(kernel, activity):
    result = jnp.dot(kernel, activity.reshape(activity.shape[0], -1), preferred_element_type=jnp.float32)
    return result.reshape((kernel.shape[0],) + activity.shape[1:])

def network_loss(weights, batch_data, loss_scale):
    w_stem, w_lift, w_down, w_deep, w_merge, w_out = weights
    inputs = jnp.transpose(batch_data[:, :2], (1, 0, 2, 3, 4))
    target = batch_data[:, 2].astype(jnp.float32)
    level_one = jax.nn.silu(conv_cube(inputs, w_stem)).astype(jnp.bfloat16)
    level_two = jax.nn.silu(pointwise(w_lift, level_one)).astype(jnp.bfloat16)
    channels, batch_size, depth_z, width_x, width_y = level_two.shape
    stored = lax.optimization_barrier(level_two).astype(jnp.float32)
    pooled = stored.reshape(channels, batch_size, depth_z // 2, 2, width_x // 2, 2, width_y).mean(axis=(3, 5)).astype(jnp.bfloat16)
    coarse = jax.nn.silu(conv_cube(pooled, w_down)).astype(jnp.bfloat16)
    deeper = jax.nn.silu(pointwise(w_deep, coarse)).astype(jnp.bfloat16)
    lifted = jnp.repeat(jnp.repeat(deeper, 2, axis=2), 2, axis=3)
    joined = jnp.concatenate([level_two, lifted], axis=0)
    merged = jax.nn.silu(pointwise(w_merge, joined)).astype(jnp.bfloat16)
    predicted = pointwise(w_out, merged)[0]
    misfit = predicted - target
    loss_value = 0.5 * jnp.sum(misfit * misfit) * loss_scale
    return (loss_value, predicted)

def train_slots(weights, batch_data, loss_scale):
    loss_value, pullback, predicted = jax.vjp(partial(network_loss, batch_data=batch_data, loss_scale=loss_scale), weights, has_aux=True)
    gradients = pullback(jnp.ones((), jnp.float32))[0]
    return (gradients, predicted)

def pack_grads(gradients, row_count):
    flattened = jnp.concatenate([grad_piece.astype(jnp.float32).reshape(-1) for grad_piece in gradients])
    flattened = jnp.pad(flattened, (0, row_count * 128 - flattened.shape[0]))
    return flattened.reshape(row_count, 128)

def reference(heat_start, conductivity, patch_z, patch_x, slot_table, w_stem, w_lift, w_down, w_deep, w_merge, w_out):
    weights = (w_stem, w_lift, w_down, w_deep, w_merge, w_out)
    cond_ext = jnp.pad(conductivity, ((1, 1), (0, 0), (0, 0)))
    heat_one = advance(jnp.pad(heat_start, ((1, 1), (0, 0), (0, 0))), cond_ext)
    heat_two = advance(jnp.pad(heat_one, ((1, 1), (0, 0), (0, 0))), cond_ext)
    sources = patch_z.shape[0]
    starts_z = (jnp.arange(sources, dtype=jnp.int32) * ZD + patch_z).astype(jnp.int32)
    stacked = jnp.stack([heat_one, conductivity, heat_two])

    def cut_patch(start_z, start_x):
        zero_index = jnp.zeros((), jnp.int32)
        return lax.dynamic_slice(stacked, (zero_index, start_z, start_x.astype(jnp.int32), zero_index), (3, PZ, PX, GY))
    patches = jax.vmap(cut_patch)(starts_z, patch_x).astype(jnp.bfloat16)
    section_of = jnp.arange(sources, dtype=jnp.int32) // N_DP
    slot_index = section_of * 2 * N_DP + slot_table
    slot_data = jnp.zeros((2 * sources, 3, PZ, PX, GY), jnp.bfloat16).at[slot_index].set(patches)
    grouped = slot_data.reshape(sources, 2, 3, PZ, PX, GY)
    loss_scale = 1.0 / (sources * PZ * PX * GY)

    def trainer_step(running, slot_group):
        gradients, predicted = train_slots(weights, slot_group, loss_scale)
        return (running + pack_grads(gradients, GROWS), predicted.astype(jnp.bfloat16))
    running, predictions = lax.scan(trainer_step, jnp.zeros((GROWS, 128), jnp.float32), grouped)
    return (heat_two, predictions.reshape(2 * sources, PZ, PX, GY), running)
```

```python
import functools

import jax
import jax.numpy as jnp
from jax import lax
from jax.experimental import pallas as pl
from jax.experimental.pallas import tpu as pltpu
from jax.sharding import PartitionSpec as P

MESH = pl.DeviceIdType.MESH
TIME_STEP = 0.15
GY = 128
PZ = 4
PX = 8
C1 = 64
C2 = 128
GROWS = 2048
LINE = 8
F32 = jnp.float32
BF16 = jnp.bfloat16
VMEM = pl.BlockSpec(memory_space=pltpu.VMEM)
SMEM = pl.BlockSpec(memory_space=pltpu.SMEM)


def rounded(x):
    return x.astype(BF16).astype(F32)


def heat_kernel(
    n_sec, n_dp, pz_ref, px_ref, u_ref, k_ref, out_ref, patch_ref, ulo, klo, uhi, khi, h1, send, recv
):
    total = n_sec * n_dp
    depth = u_ref.shape[0]
    me = lax.axis_index("section") * n_dp + lax.axis_index("dp")
    after = lax.rem(me + 1, total)
    before = lax.rem(me + total - 1, total)

    def place(i):
        return (lax.div(i, n_dp), lax.rem(i, n_dp))

    barrier = pltpu.get_barrier_semaphore()
    for peer in (before, after):
        pl.semaphore_signal(barrier, inc=1, device_id=place(peer), device_id_type=MESH)
    pl.semaphore_wait(barrier, 2)
    plan = (
        (u_ref.at[pl.ds(depth - 2, 2)], ulo, after),
        (k_ref.at[pl.ds(depth - 2, 2)], klo, after),
        (u_ref.at[pl.ds(0, 2)], uhi, before),
        (k_ref.at[pl.ds(0, 2)], khi, before),
    )
    copies = []
    for i, (src, dst, peer) in enumerate(plan):
        copy = pltpu.make_async_remote_copy(
            src_ref=src,
            dst_ref=dst,
            send_sem=send.at[i],
            recv_sem=recv.at[i],
            device_id=place(peer),
            device_id_type=MESH,
        )
        copy.start()
        copies.append(copy)

    rows, lanes = u_ref.shape[1:]
    row = lax.broadcasted_iota(jnp.int32, (rows, lanes), 0)
    lane = lax.broadcasted_iota(jnp.int32, (rows, lanes), 1)

    def step(up, uc, un, kp, kc, kn):
        flux = (kc + kn) * (un - uc) + (kc + kp) * (up - uc)
        for axis, place_, size in ((0, row, rows), (1, lane, lanes)):
            last = place_ == size - 1
            first = place_ == 0
            u_next = jnp.where(last, 0.0, pltpu.roll(uc, size - 1, axis))
            k_next = jnp.where(last, 0.0, pltpu.roll(kc, size - 1, axis))
            face = (kc + k_next) * (u_next - uc)
            back = jnp.where(first, kc * uc, pltpu.roll(face, 1, axis))
            flux = flux + (face - back)
        return uc + (0.5 * TIME_STEP) * flux

    def interior(z, carry):
        h1[z + 1] = step(u_ref[z - 1], u_ref[z], u_ref[z + 1], k_ref[z - 1], k_ref[z], k_ref[z + 1])
        return carry

    lax.fori_loop(1, depth - 1, interior, 0)
    for copy in copies:
        copy.wait_recv()
    has_lo = (me > 0).astype(F32)
    has_hi = (me < total - 1).astype(F32)
    ul = [ulo[0] * has_lo, ulo[1] * has_lo]
    kl = [klo[0] * has_lo, klo[1] * has_lo]
    uh = [uhi[0] * has_hi, uhi[1] * has_hi]
    kh = [khi[0] * has_hi, khi[1] * has_hi]
    end = depth - 1
    h1[0] = has_lo * step(ul[0], ul[1], u_ref[0], kl[0], kl[1], k_ref[0])
    h1[1] = step(ul[1], u_ref[0], u_ref[1], kl[1], k_ref[0], k_ref[1])
    h1[depth] = step(u_ref[end - 1], u_ref[end], uh[0], k_ref[end - 1], k_ref[end], kh[0])
    h1[depth + 1] = has_hi * step(u_ref[end], uh[0], uh[1], k_ref[end], kh[0], kh[1])

    out_ref[0] = step(h1[0], h1[1], h1[2], kl[1], k_ref[0], k_ref[1])
    out_ref[end] = step(h1[end], h1[depth], h1[depth + 1], k_ref[end - 1], k_ref[end], kh[0])

    def second(z, carry):
        out_ref[z] = step(h1[z], h1[z + 1], h1[z + 2], k_ref[z - 1], k_ref[z], k_ref[z + 1])
        return carry

    lax.fori_loop(1, depth - 1, second, 0)
    pz = pz_ref[0]
    px = px_ref[0]
    for z in range(PZ):
        patch_ref[0, z] = h1[1 + pz + z, pl.ds(px, PX), :]
        patch_ref[1, z] = k_ref[pz + z, pl.ds(px, PX), :]
        patch_ref[2, z] = out_ref[pz + z, pl.ds(px, PX), :]
    for copy in copies:
        copy.wait_send()


def heat_steps(n_sec, n_dp, heat, cond, patch_z, patch_x):
    layers = (2,) + heat.shape[1:]
    return pl.pallas_call(
        functools.partial(heat_kernel, n_sec, n_dp),
        out_shape=(
            jax.ShapeDtypeStruct(heat.shape, F32),
            jax.ShapeDtypeStruct((3, PZ, PX, GY), F32),
        ),
        in_specs=[SMEM, SMEM, VMEM, VMEM],
        out_specs=(VMEM, VMEM),
        scratch_shapes=[
            pltpu.VMEM(layers, F32),
            pltpu.VMEM(layers, F32),
            pltpu.VMEM(layers, F32),
            pltpu.VMEM(layers, F32),
            pltpu.VMEM((heat.shape[0] + 2,) + heat.shape[1:], F32),
            pltpu.SemaphoreType.DMA((4,)),
            pltpu.SemaphoreType.DMA((4,)),
        ],
        compiler_params=pltpu.CompilerParams(
            collective_id=0, has_side_effects=True, vmem_limit_bytes=16 * 2**20
        ),
        name="heat",
    )(patch_z, patch_x, heat, cond)


NT = (((1,), (1,)), ((), ()))
NN = (((1,), (0,)), ((), ()))


def mm(a, b, dims=NN):
    return lax.dot_general(a, b, dims, preferred_element_type=F32)


def silu_and_slope(z):
    s = 0.5 * jnp.tanh(0.5 * z) + 0.5
    value = z * s
    return value, s + value * (1.0 - s)


def block(x, b):
    return x[:, b * GY : (b + 1) * GY]


def train_kernel(
    scale,
    slot_ref,
    patch_ref,
    w_stem,
    w_lift,
    w_down,
    w_deep,
    w_merge,
    w_out,
    pred_ref,
    grad_ref,
    tall,
    cols,
    l1,
    l2,
    g1,
    g2,
    dl2,
    colsd,
    colsz,
    wback,
    pack,
    pair,
):
    plane = PX * GY
    cells = PZ * plane
    small = cells // 4
    row8 = lax.broadcasted_iota(jnp.int32, (PX, GY), 0)
    lane8 = lax.broadcasted_iota(jnp.int32, (PX, GY), 1)
    lane64 = lax.broadcasted_iota(jnp.int32, (C1, GY), 1)

    tall[...] = jnp.zeros_like(tall)
    for channel in range(2):
        for dx in range(3):
            for dy in range(3):
                shifted = []
                for z in range(PZ):
                    v = rounded(patch_ref[channel, z])
                    if dx == 0:
                        v = jnp.where(row8 == 0, 0.0, pltpu.roll(v, 1, 0))
                    elif dx == 2:
                        v = jnp.where(row8 == PX - 1, 0.0, pltpu.roll(v, PX - 1, 0))
                    if dy == 0:
                        v = jnp.where(lane8 == 0, 0.0, pltpu.roll(v, 1, 1))
                    elif dy == 2:
                        v = jnp.where(lane8 == GY - 1, 0.0, pltpu.roll(v, GY - 1, 1))
                    shifted.append(v)
                for dz in range(3):
                    r = ((dz * 3 + dx) * 3 + dy) * 2 + channel
                    for z in range(PZ):
                        if 0 <= z + dz - 1 < PZ:
                            tall[pl.ds(z * PX * C1 + r, PX, stride=C1), :] = shifted[z + dz - 1]
    for b in range(PZ * PX):
        cols[:, b * GY : (b + 1) * GY] = tall[b * C1 : (b + 1) * C1, :].astype(BF16)

    stem = w_stem[...]
    lift = w_lift[...]
    taps = stem.shape[1]
    pooled = []
    for zz in range(PZ // 2):
        rows = []
        for z in (2 * zz, 2 * zz + 1):
            here = slice(z * plane, (z + 1) * plane)
            value, slope = silu_and_slope(mm(stem, cols[0:taps, here]))
            g1[:, here] = slope
            one = value.astype(BF16)
            l1[:, here] = one
            value, slope = silu_and_slope(mm(lift, one))
            g2[:, here] = slope
            two = value.astype(BF16)
            l2[:, here] = two
            rows.append(two.astype(F32))
        both = rows[0] + rows[1]
        for xx in range(PX // 2):
            pooled.append(rounded((block(both, 2 * xx) + block(both, 2 * xx + 1)) * 0.25))

    hz, hx = PZ // 2, PX // 2
    shifted = []
    for dy in range(3):
        if dy == 0:
            part = [jnp.where(lane64 == 0, 0.0, pltpu.roll(v, 1, 1)) for v in pooled]
        elif dy == 1:
            part = pooled
        else:
            part = [jnp.where(lane64 == GY - 1, 0.0, pltpu.roll(v, GY - 1, 1)) for v in pooled]
        shifted.append([v.astype(BF16) for v in part])
    nothing = jnp.zeros((C1, GY), BF16)
    for dz in range(3):
        for dx in range(3):
            for dy in range(3):
                r = ((dz * 3 + dx) * 3 + dy) * C1
                for z in range(hz):
                    for x in range(hx):
                        sz, sx = z + dz - 1, x + dx - 1
                        inside = 0 <= sz < hz and 0 <= sx < hx
                        b = z * hx + x
                        colsd[r : r + C1, b * GY : (b + 1) * GY] = (
                            shifted[dy][sz * hx + sx] if inside else nothing
                        )
    depth = 27 * C1
    colsd[depth : depth + C1, :] = jnp.zeros((C1, small), BF16)
    value, slope_down = silu_and_slope(mm(w_down[...], colsd[0:depth, :]))
    coarse = value.astype(BF16)
    value, slope_deep = silu_and_slope(mm(w_deep[...], coarse))
    deeper = value.astype(BF16)
    merge_fine = w_merge[:, 0:C1]
    merge_coarse = w_merge[:, C1 : C1 + C2]
    lifted = mm(merge_coarse, deeper)

    out_row = w_out[...].astype(F32)
    eye = lax.broadcasted_iota(jnp.int32, (C1, C1), 0) == lax.broadcasted_iota(jnp.int32, (C1, C1), 1)
    out_col = jnp.sum(jnp.where(eye, jnp.broadcast_to(out_row, (C1, C1)), 0.0), axis=1, keepdims=True)
    out8 = jnp.broadcast_to(out_row, (8, C1)).astype(BF16)
    fine_t = merge_fine.astype(F32).T.astype(BF16)
    d_fine = jnp.zeros((C1, GY), F32)
    d_out = jnp.zeros((8, GY), F32)
    gathered = [None] * (hz * hx)
    for z in range(PZ):
        here = slice(z * plane, (z + 1) * plane)
        two = l2[:, here]
        added = [block(lifted, (z // 2) * hx + x // 2) for x in range(PX)]
        value, slope = silu_and_slope(mm(merge_fine, two) + jnp.concatenate(added, axis=1))
        merged = value.astype(BF16)
        wide = mm(out8, merged)
        predicted = jnp.zeros((PX, GY), F32)
        for x in range(PX):
            predicted = jnp.where(row8 == x, block(wide, x), predicted)
        pred_ref[z * PX : (z + 1) * PX, :] = predicted
        misfit = (predicted - rounded(patch_ref[2, z])) * scale
        d_wide = jnp.concatenate(
            [jnp.broadcast_to(misfit[x : x + 1, :], (8, GY)) for x in range(PX)], axis=1
        ).astype(BF16)
        d_out = d_out + mm(d_wide, jnp.concatenate([merged, merged], axis=0), NT)
        d_merged = jnp.concatenate([out_col * misfit[x : x + 1, :] for x in range(PX)], axis=1)
        dz = rounded(d_merged) * slope
        for x in range(PX):
            b = (z // 2) * hx + x // 2
            gathered[b] = block(dz, x) if gathered[b] is None else gathered[b] + block(dz, x)
        dz = dz.astype(BF16)
        d_fine = d_fine + mm(dz, jnp.concatenate([two, two], axis=0), NT)
        dl2[:, here] = rounded(mm(fine_t, dz))

    d_lifted = jnp.concatenate(gathered, axis=1).astype(BF16)
    d_coarse_merge = mm(d_lifted, deeper, NT)
    d_deeper = mm(merge_coarse.astype(F32).T.astype(BF16), d_lifted)
    dz_deep = (rounded(d_deeper) * slope_deep).astype(BF16)
    d_deep = mm(dz_deep, coarse, NT)
    d_coarse = mm(w_deep[...].astype(F32).T.astype(BF16), dz_deep)
    dz_down = (rounded(d_coarse) * slope_down).astype(BF16)

    r_ = lax.broadcasted_iota(jnp.int32, (C2, C2), 0)
    c_ = lax.broadcasted_iota(jnp.int32, (C2, C2), 1)
    parted = jnp.where(r_ < C1, 2 * r_, 2 * r_ - (C2 - 1)) == c_
    dz_parted = mm(parted.astype(BF16), dz_down).astype(BF16)
    base = 27 + 32
    chunks = [mm(dz_parted, colsd[j * C2 : (j + 1) * C2, :], NT) for j in range(14)]
    low = lane64 < C1
    for j in range(13):
        pack[pl.ds(base + j, C1, stride=27), :] = chunks[j][0:C1]
        pack[pl.ds(base + 14 + j, C1, stride=27), :] = pltpu.roll(
            jnp.where(low, chunks[j + 1][C1:C2], chunks[j][C1:C2]), C1, 1
        )
    pack[pl.ds(base + 13, C1, stride=27), :] = jnp.where(
        low, chunks[13][0:C1], pltpu.roll(chunks[0][C1:C2], C1, 1)
    )

    blank = jnp.zeros((C2, GY), BF16)
    for dz in range(3):
        for dx in range(3):
            j = dz * 3 + dx
            wback[:, j * C2 : (j + 1) * C2] = (
                w_down[:, j * 3 * C1 : (j + 1) * 3 * C1].astype(F32).T.astype(BF16)
            )
            for z in range(hz):
                for x in range(hx):
                    sz, sx = z - (dz - 1), x - (dx - 1)
                    inside = 0 <= sz < hz and 0 <= sx < hx
                    b = z * hx + x
                    colsz[j * C2 : (j + 1) * C2, b * GY : (b + 1) * GY] = (
                        block(dz_down, sz * hx + sx) if inside else blank
                    )
    d_shifted = mm(wback[...], colsz[...])
    d_pooled = []
    for b in range(hz * hx):
        whole = block(d_shifted, b)
        total = whole[C1 : 2 * C1]
        total = total + jnp.where(lane64 == GY - 1, 0.0, pltpu.roll(whole[0:C1], GY - 1, 1))
        total = total + jnp.where(lane64 == 0, 0.0, pltpu.roll(whole[2 * C1 : 3 * C1], 1, 1))
        d_pooled.append(rounded(total) * 0.25)

    lift_t = lift.astype(F32).T.astype(BF16)
    d_lift = jnp.zeros((C1, GY), F32)
    d_stem = jnp.zeros((C1, C1), F32)
    for z in range(PZ):
        here = slice(z * plane, (z + 1) * plane)
        spread = jnp.concatenate([d_pooled[(z // 2) * hx + x // 2] for x in range(PX)], axis=1)
        dz = ((dl2[:, here] + spread) * g2[:, here]).astype(BF16)
        one = l1[:, here]
        d_lift = d_lift + mm(dz, jnp.concatenate([one, one], axis=0), NT)
        d_one = rounded(mm(lift_t, dz))
        dz = (d_one * g1[:, here]).astype(BF16)
        d_stem = d_stem + mm(dz, cols[:, here], NT)

    pair[:, 0:C1] = d_stem
    pair[:, C1:GY] = jnp.zeros((C1, GY - C1), F32)
    turned = pair[...]
    source = lax.broadcasted_iota(jnp.int32, (C1, GY), 0)
    for bit in range(6):
        moved = pltpu.roll(turned, (taps << bit) % GY, 1)
        turned = jnp.where((source >> bit) % 2 == 1, moved, turned)
    begin = source * taps
    kept = turned.astype(BF16)
    wraps = lane64 < begin % GY
    stay = jnp.where(wraps, 0.0, turned).astype(BF16)
    over = jnp.where(wraps, turned, 0.0).astype(BF16)
    target_row = lax.broadcasted_iota(jnp.int32, (32, C1), 0)
    owner = lax.broadcasted_iota(jnp.int32, (32, C1), 1) * taps // GY
    del kept
    stem_rows = mm((target_row == owner).astype(BF16), stay)
    stem_rows = stem_rows + mm((target_row == owner + 1).astype(BF16), over)
    pack[0:27, :] = stem_rows[0:27, :]

    low32 = lax.broadcasted_iota(jnp.int32, (32, GY), 1) < C1
    pair[...] = d_lift
    pack[27 : 27 + 32, :] = jnp.where(low32, pair[pl.ds(0, 32, stride=2), :], pair[pl.ds(1, 32, stride=2), :])

    base = 27 + 32 + 27 * C1
    pack[base : base + C2, :] = d_deep
    base = base + C2
    fine_even_odd = []
    pair[...] = d_fine
    fine_even_odd = [pair[pl.ds(i, 32, stride=2), :] for i in range(2)]
    pair[...] = d_coarse_merge
    coarse_even_odd = [pair[pl.ds(i, 32, stride=2), :] for i in range(2)]
    half = pltpu.roll(coarse_even_odd[0], C1, 1)
    pack[pl.ds(base, 32, stride=3), :] = jnp.where(low32, fine_even_odd[0], half)
    pack[pl.ds(base + 1, 32, stride=3), :] = jnp.where(low32, half, fine_even_odd[1])
    pack[pl.ds(base + 2, 32, stride=3), :] = coarse_even_odd[1]
    base = base + 96
    pack[base : base + 1, :] = jnp.where(lane8[0:1] < C1, d_out[0:1, :], 0.0)
    pack[base + 1 : GROWS, :] = jnp.zeros((GROWS - base - 1, GY), F32)

    per = grad_ref.shape[2]
    for lo in range(grad_ref.shape[0]):
        for hi in range(grad_ref.shape[1]):
            start = (hi * grad_ref.shape[0] + lo) * per
            grad_ref[lo, hi] = pack[start : start + per, :].astype(BF16)
    pred_ref[PZ * PX : PZ * PX + 16, :] = jnp.full((16, GY), slot_ref[0].astype(F32))


def train(scale, n_hi, n_lo, slot, patch, weights):
    cells = PZ * PX * GY
    small = cells // 4
    return pl.pallas_call(
        functools.partial(train_kernel, scale),
        out_shape=(
            jax.ShapeDtypeStruct((PZ * PX + 16, GY), F32),
            jax.ShapeDtypeStruct((n_lo, n_hi, GROWS // (n_lo * n_hi), GY), BF16),
        ),
        in_specs=[SMEM] + [VMEM] * 7,
        out_specs=(VMEM, VMEM),
        scratch_shapes=[
            pltpu.VMEM((PZ * PX * C1, GY), F32),
            pltpu.VMEM((C1, cells), BF16),
            pltpu.VMEM((C1, cells), BF16),
            pltpu.VMEM((C1, cells), BF16),
            pltpu.VMEM((C1, cells), F32),
            pltpu.VMEM((C1, cells), F32),
            pltpu.VMEM((C1, cells), F32),
            pltpu.VMEM((28 * C1, small), BF16),
            pltpu.VMEM((9 * C2, small), BF16),
            pltpu.VMEM((3 * C1, 9 * C2), BF16),
            pltpu.VMEM((GROWS, GY), F32),
            pltpu.VMEM((C1, GY), F32),
        ],
        compiler_params=pltpu.CompilerParams(vmem_limit_bytes=48 * 2**20),
        name="train",
    )(slot, patch, *weights)


def share_kernel(
    n_sec,
    n_hi,
    n_lo,
    g_ref,
    p_ref,
    pred_out,
    grad_out,
    packet,
    buf1,
    acc,
    buf2,
    pbuf,
    q_ref,
    qbuf,
    s1,
    r1,
    s2,
    r2,
    s3,
    r3,
    s4,
    r4,
):
    sec = lax.axis_index("section")
    dp = lax.axis_index("dp")
    hi = lax.div(dp, n_lo)
    lo = lax.rem(dp, n_lo)
    across = n_sec * n_hi
    mine = sec * n_hi + hi

    def in_line(d):
        peer = lax.rem(lo + d, n_lo)
        return peer, (sec, hi * n_lo + peer)

    def in_column(d):
        peer = lax.rem(mine + d, across)
        return peer, (lax.div(peer, n_hi), lax.rem(peer, n_hi) * n_lo + lo)

    def in_part(d):
        peer = lax.rem(hi + d, n_hi)
        return peer, (sec, peer * n_lo + lo)

    barrier = pltpu.get_barrier_semaphore()
    for d in range(1, n_lo):
        pl.semaphore_signal(barrier, inc=1, device_id=in_line(d)[1], device_id_type=MESH)
    for d in range(1, across):
        pl.semaphore_signal(barrier, inc=1, device_id=in_column(d)[1], device_id_type=MESH)
    packet[...] = p_ref[...].astype(BF16)
    pl.semaphore_wait(barrier, n_lo - 1 + across - 1)

    def send(src, dst, ssem, rsem, device):
        copy = pltpu.make_async_remote_copy(
            src_ref=src, dst_ref=dst, send_sem=ssem, recv_sem=rsem, device_id=device, device_id_type=MESH
        )
        copy.start()
        return copy

    grads = []
    for d in range(1, n_lo):
        peer, device = in_line(d)
        grads.append(send(g_ref.at[peer], buf1.at[d - 1], s1.at[d - 1], r1.at[d - 1], device))
    packets = []
    for d in range(1, n_hi):
        peer, device = in_part(d)
        packets.append(send(packet, pbuf.at[d], s3.at[d - 1], r3.at[d - 1], device))
    pbuf[0] = packet[...]
    for copy in grads:
        copy.wait_recv()

    def add_line(h, carry):
        value = g_ref[lo, h].astype(F32)
        for d in range(n_lo - 1):
            value = value + buf1[d, h].astype(F32)
        acc[h] = value
        return carry

    lax.fori_loop(0, n_hi, add_line, 0)
    partials = []
    for d in range(1, across):
        peer, device = in_column(d)
        partials.append(
            send(acc.at[lax.rem(peer, n_hi)], buf2.at[mine], s2.at[d - 1], r2.at[d - 1], device)
        )
    buf2[mine] = acc[hi]

    for copy in packets:
        copy.wait_recv()
    cells = PZ * PX

    def route(q, carry):
        wanted = (hi * (2 * n_lo) + q).astype(F32)
        value = jnp.zeros((cells, GY), F32)
        for src in range(n_hi):
            named = pbuf[src, cells : cells + 16, :].astype(F32)
            named = jnp.concatenate([named] * (cells // 16), axis=0)
            value = value + jnp.where(named == wanted, pbuf[src, 0:cells, :].astype(F32), 0.0)
        q_ref[q] = value.astype(BF16)
        return carry

    lax.fori_loop(0, 2 * n_lo, route, 0)
    routed = []
    for d in range(1, n_lo):
        peer, device = in_line(d)
        routed.append(send(q_ref.at[pl.ds(2 * peer, 2)], qbuf.at[d - 1], s4.at[d - 1], r4.at[d - 1], device))

    for copy in partials:
        copy.wait_recv()

    def add_column(t, total):
        return total + buf2[t]

    grad_out[...] = lax.fori_loop(1, across, add_column, buf2[0])

    for copy in routed:
        copy.wait_recv()
    for s in range(2):
        value = q_ref[2 * lo + s].astype(F32)
        for d in range(n_lo - 1):
            value = value + qbuf[d, s].astype(F32)
        for z in range(PZ):
            pred_out[s, z] = value[z * PX : (z + 1) * PX].astype(BF16)
    for copy in grads + packets + partials + routed:
        copy.wait_send()


def share(n_sec, n_hi, n_lo, grads, preds):
    per = grads.shape[2]
    across = n_sec * n_hi
    dma = pltpu.SemaphoreType.DMA
    return pl.pallas_call(
        functools.partial(share_kernel, n_sec, n_hi, n_lo),
        out_shape=(
            jax.ShapeDtypeStruct((2, PZ, PX, GY), BF16),
            jax.ShapeDtypeStruct((per, GY), F32),
        ),
        in_specs=[VMEM, VMEM],
        out_specs=(VMEM, VMEM),
        scratch_shapes=[
            pltpu.VMEM((PZ * PX + 16, GY), BF16),
            pltpu.VMEM((n_lo - 1, n_hi, per, GY), BF16),
            pltpu.VMEM((n_hi, per, GY), F32),
            pltpu.VMEM((across, per, GY), F32),
            pltpu.VMEM((n_hi, PZ * PX + 16, GY), BF16),
            pltpu.VMEM((2 * n_lo, PZ * PX, GY), BF16),
            pltpu.VMEM((n_lo - 1, 2, PZ * PX, GY), BF16),
            dma((n_lo - 1,)),
            dma((n_lo - 1,)),
            dma((across - 1,)),
            dma((across - 1,)),
            dma((n_hi - 1,)),
            dma((n_hi - 1,)),
            dma((n_lo - 1,)),
            dma((n_lo - 1,)),
        ],
        compiler_params=pltpu.CompilerParams(
            collective_id=1, has_side_effects=True, vmem_limit_bytes=16 * 2**20
        ),
        name="share",
    )(grads, preds)


def local(
    n_sec,
    n_dp,
    heat_start,
    conductivity,
    patch_z,
    patch_x,
    slot_table,
    w_stem,
    w_lift,
    w_down,
    w_deep,
    w_merge,
    w_out,
):
    n_lo = LINE
    n_hi = n_dp // n_lo
    weights = (w_stem, w_lift, w_down, w_deep, w_merge, w_out)
    heat_two, patch = heat_steps(n_sec, n_dp, heat_start, conductivity, patch_z, patch_x)
    scale = 1.0 / (n_sec * n_dp * PZ * PX * GY)
    preds, grads = train(scale, n_hi, n_lo, slot_table, patch, weights)
    predictions, grad_pack = share(n_sec, n_hi, n_lo, grads, preds)
    return heat_two, predictions, grad_pack


def solution(mesh):
    n_sec, n_dp = mesh.shape["section"], mesh.shape["dp"]
    both = ("section", "dp")
    return jax.shard_map(
        functools.partial(local, n_sec, n_dp),
        mesh=mesh,
        in_specs=(P(both, None, None), P(both, None, None), P(both), P(both), P(both)) + (P(),) * 6,
        out_specs=(P(both, None, None), P(both, None, None, None), P("dp", None)),
        check_vma=False,
    )
```

```python
import functools

import jax
import jax.numpy as jnp
from jax import lax
from jax.experimental import pallas as pl
from jax.experimental.pallas import tpu as pltpu
from jax.sharding import PartitionSpec as P

MESH = pl.DeviceIdType.MESH
TIME_STEP = 0.15
GY = 128
PZ = 4
PX = 8
C1 = 64
C2 = 128
GROWS = 2048
LINE = 8
F32 = jnp.float32
BF16 = jnp.bfloat16
VMEM = pl.BlockSpec(memory_space=pltpu.VMEM)
SMEM = pl.BlockSpec(memory_space=pltpu.SMEM)
HBM = pl.BlockSpec(memory_space=pltpu.HBM)


def rounded(x):
    return x.astype(BF16).astype(F32)


NT = (((1,), (1,)), ((), ()))
NN = (((1,), (0,)), ((), ()))


def mm(a, b, dims=NN):
    return lax.dot_general(a, b, dims, preferred_element_type=F32)


def heat_kernel(
    n_sec,
    n_dp,
    pz_ref,
    px_ref,
    u_hbm,
    k_hbm,
    stem_hbm,
    lift_hbm,
    down_hbm,
    deep_hbm,
    merge_hbm,
    proj_hbm,
    out_ref,
    patch_ref,
    stem_ref,
    lift_ref,
    lift_t,
    down_ref,
    down_back,
    deep_ref,
    deep_t,
    fine_ref,
    fine_t,
    coarse_ref,
    coarse_t,
    proj_ref,
    proj_col,
    v_stem,
    v_down,
    v_merge,
    v_proj,
    u_ref,
    k_ref,
    ulo,
    klo,
    uhi,
    khi,
    h1,
    load,
    send,
    recv,
):
    total = n_sec * n_dp
    depth = u_ref.shape[0]
    me = lax.axis_index("section") * n_dp + lax.axis_index("dp")
    after = lax.rem(me + 1, total)
    before = lax.rem(me + total - 1, total)

    def place(i):
        return (lax.div(i, n_dp), lax.rem(i, n_dp))

    barrier = pltpu.get_barrier_semaphore()
    for peer in (before, after):
        pl.semaphore_signal(barrier, inc=1, device_id=place(peer), device_id_type=MESH)
    loads = [
        pltpu.make_async_copy(u_hbm, u_ref, load.at[0]),
        pltpu.make_async_copy(k_hbm, k_ref, load.at[1]),
        pltpu.make_async_copy(down_hbm, v_down, load.at[2]),
        pltpu.make_async_copy(stem_hbm, v_stem, load.at[3]),
        pltpu.make_async_copy(lift_hbm, lift_ref, load.at[4]),
        pltpu.make_async_copy(deep_hbm, deep_ref, load.at[5]),
        pltpu.make_async_copy(merge_hbm, v_merge, load.at[6]),
        pltpu.make_async_copy(proj_hbm, v_proj, load.at[7]),
    ]
    for copy in loads:
        copy.start()
    pl.semaphore_wait(barrier, 2)
    plan = (
        (u_hbm.at[pl.ds(depth - 2, 2)], ulo, after),
        (u_hbm.at[pl.ds(0, 2)], uhi, before),
        (k_hbm.at[pl.ds(depth - 2, 2)], klo, after),
        (k_hbm.at[pl.ds(0, 2)], khi, before),
    )
    copies = []
    for i, (src, dst, peer) in enumerate(plan):
        copy = pltpu.make_async_remote_copy(
            src_ref=src,
            dst_ref=dst,
            send_sem=send.at[i],
            recv_sem=recv.at[i],
            device_id=place(peer),
            device_id_type=MESH,
        )
        copy.start()
        copies.append(copy)

    rows, lanes = u_ref.shape[1:]
    row = lax.broadcasted_iota(jnp.int32, (rows, lanes), 0)
    lane = lax.broadcasted_iota(jnp.int32, (rows, lanes), 1)

    def step(up, uc, un, kp, kc, kn):
        flux = (kc + kn) * (un - uc) + (kc + kp) * (up - uc)
        for axis, place_, size in ((0, row, rows), (1, lane, lanes)):
            last = place_ == size - 1
            first = place_ == 0
            u_next = jnp.where(last, 0.0, pltpu.roll(uc, size - 1, axis))
            k_next = jnp.where(last, 0.0, pltpu.roll(kc, size - 1, axis))
            face = (kc + k_next) * (u_next - uc)
            back = jnp.where(first, kc * uc, pltpu.roll(face, 1, axis))
            flux = flux + (face - back)
        return uc + (0.5 * TIME_STEP) * flux

    for copy in loads:
        copy.wait()
    group = 7

    def interior(i, carry):
        for j in range(group):
            z = 1 + i * group + j
            h1[z + 1] = step(
                u_ref[z - 1], u_ref[z], u_ref[z + 1], k_ref[z - 1], k_ref[z], k_ref[z + 1]
            )
        return carry

    lax.fori_loop(0, (depth - 2) // group, interior, 0)

    def second(z):
        out_ref[z] = step(h1[z], h1[z + 1], h1[z + 2], k_ref[z - 1], k_ref[z], k_ref[z + 1])

    pack = 6

    def inner(i, carry):
        for j in range(pack):
            second(2 + i * pack + j)
        return carry

    lax.fori_loop(0, (depth - 4) // pack, inner, 0)
    unit = lax.broadcasted_iota(jnp.int32, (C2, C2), 0) == lax.broadcasted_iota(jnp.int32, (C2, C2), 1)
    eye = unit[0:C1, 0:C1]
    unit = unit.astype(BF16)
    stem_ref[...] = mm(unit[0:C1, 0:C1], v_stem[...], NT).astype(BF16)
    down_ref[...] = mm(unit, v_down[...], NT).astype(BF16)
    for j in range(9):
        down_back[:, j * C2 : (j + 1) * C2] = v_down[j * 3 * C1 : (j + 1) * 3 * C1, :]

    def turned(x):
        return x.astype(F32).T.astype(BF16)

    lift_t[...] = turned(lift_ref[...])
    deep_t[...] = turned(deep_ref[...])
    fine = v_merge[:, 0:C1]
    coarse = v_merge[:, C1 : C1 + C2]
    fine_ref[...] = fine
    fine_t[...] = turned(fine)
    coarse_ref[...] = coarse
    coarse_t[...] = turned(coarse)
    row64 = v_proj[...].astype(F32)
    proj_ref[...] = jnp.broadcast_to(row64, proj_ref.shape).astype(BF16)
    column = jnp.sum(jnp.where(eye, jnp.broadcast_to(row64, (C1, C1)), 0.0), axis=1, keepdims=True)
    proj_col[...] = jnp.broadcast_to(column, proj_col.shape)

    for copy in copies:
        copy.wait_recv()
    has_lo = (me > 0).astype(F32)
    has_hi = (me < total - 1).astype(F32)
    ul = [ulo[0] * has_lo, ulo[1] * has_lo]
    kl = [klo[0] * has_lo, klo[1] * has_lo]
    uh = [uhi[0] * has_hi, uhi[1] * has_hi]
    kh = [khi[0] * has_hi, khi[1] * has_hi]
    end = depth - 1
    h1[0] = has_lo * step(ul[0], ul[1], u_ref[0], kl[0], kl[1], k_ref[0])
    h1[1] = step(ul[1], u_ref[0], u_ref[1], kl[1], k_ref[0], k_ref[1])
    h1[depth] = step(u_ref[end - 1], u_ref[end], uh[0], k_ref[end - 1], k_ref[end], kh[0])
    h1[depth + 1] = has_hi * step(u_ref[end], uh[0], uh[1], k_ref[end], kh[0], kh[1])

    out_ref[0] = step(h1[0], h1[1], h1[2], kl[1], k_ref[0], k_ref[1])
    out_ref[end] = step(h1[end], h1[depth], h1[depth + 1], k_ref[end - 1], k_ref[end], kh[0])
    second(1)
    second(end - 1)
    pz = pz_ref[0]
    px = px_ref[0]
    for z in range(PZ):
        patch_ref[0, z] = h1[1 + pz + z, pl.ds(px, PX), :]
        patch_ref[1, z] = k_ref[pz + z, pl.ds(px, PX), :]
        patch_ref[2, z] = out_ref[pz + z, pl.ds(px, PX), :]
    for copy in copies:
        copy.wait_send()


def heat_steps(n_sec, n_dp, heat, cond, patch_z, patch_x, weights):
    layers = (2,) + heat.shape[1:]
    taps = weights[0].shape[0]
    return pl.pallas_call(
        functools.partial(heat_kernel, n_sec, n_dp),
        out_shape=(
            jax.ShapeDtypeStruct(heat.shape, F32),
            jax.ShapeDtypeStruct((3, PZ, PX, GY), F32),
            jax.ShapeDtypeStruct((C1, taps), BF16),
            jax.ShapeDtypeStruct((C1, C1), BF16),
            jax.ShapeDtypeStruct((C1, C1), BF16),
            jax.ShapeDtypeStruct((C2, 27 * C1), BF16),
            jax.ShapeDtypeStruct((3 * C1, 9 * C2), BF16),
            jax.ShapeDtypeStruct((C2, C2), BF16),
            jax.ShapeDtypeStruct((C2, C2), BF16),
            jax.ShapeDtypeStruct((C1, C1), BF16),
            jax.ShapeDtypeStruct((C1, C1), BF16),
            jax.ShapeDtypeStruct((C1, C2), BF16),
            jax.ShapeDtypeStruct((C2, C1), BF16),
            jax.ShapeDtypeStruct((16, C1), BF16),
            jax.ShapeDtypeStruct((C1, GY), F32),
        ),
        in_specs=[SMEM, SMEM] + [HBM] * 8,
        out_specs=(VMEM,) * 15,
        scratch_shapes=[
            pltpu.VMEM(weights[0].shape, BF16),
            pltpu.VMEM(weights[2].shape, BF16),
            pltpu.VMEM(weights[4].shape, BF16),
            pltpu.VMEM(weights[5].shape, BF16),
            pltpu.VMEM(heat.shape, F32),
            pltpu.VMEM(heat.shape, F32),
            pltpu.VMEM(layers, F32),
            pltpu.VMEM(layers, F32),
            pltpu.VMEM(layers, F32),
            pltpu.VMEM(layers, F32),
            pltpu.VMEM((heat.shape[0] + 2,) + heat.shape[1:], F32),
            pltpu.SemaphoreType.DMA((8,)),
            pltpu.SemaphoreType.DMA((4,)),
            pltpu.SemaphoreType.DMA((4,)),
        ],
        compiler_params=pltpu.CompilerParams(
            collective_id=0, has_side_effects=True, vmem_limit_bytes=16 * 2**20
        ),
        name="heat",
    )(patch_z, patch_x, *[pltpu.with_memory_space_constraint(x, pltpu.HBM) for x in (heat, cond, *weights)])


def silu_and_slope(z):
    s = 0.5 * jnp.tanh(0.5 * z) + 0.5
    value = z * s
    return value, s + value * (1.0 - s)


def block(x, b):
    return x[:, b * GY : (b + 1) * GY]


def train_kernel(
    scale,
    n_sec,
    n_hi,
    n_lo,
    slot_ref,
    patch_ref,
    w_stem,
    w_lift,
    w_lift_t,
    w_down,
    wback,
    w_deep,
    w_deep_t,
    w_fine,
    w_fine_t,
    w_coarse,
    w_coarse_t,
    w_proj,
    w_proj_col,
    pred_out,
    buf2,
    tall,
    cols,
    l1,
    l2,
    g1,
    g2,
    merged_ref,
    dz_ref,
    colsd,
    colsz,
    pack,
    pair,
    grads,
    packet,
    buf1,
    acc,
    pbuf,
    q_ref,
    qbuf,
    s1,
    r1,
    s1b,
    r1b,
    s2,
    r2,
    s3,
    r3,
    s4,
    r4,
):
    sec = lax.axis_index("section")
    dp = lax.axis_index("dp")
    hi = lax.div(dp, n_lo)
    lo = lax.rem(dp, n_lo)
    across = n_sec * n_hi
    mine = sec * n_hi + hi

    def in_line(d):
        peer = lax.rem(lo + d, n_lo)
        return peer, (sec, hi * n_lo + peer)

    def in_column(d):
        peer = lax.rem(mine + d, across)
        return peer, (lax.div(peer, n_hi), lax.rem(peer, n_hi) * n_lo + lo)

    def in_part(d):
        peer = lax.rem(hi + d, n_hi)
        return peer, (sec, peer * n_lo + lo)

    def send(src, dst, ssem, rsem, device):
        copy = pltpu.make_async_remote_copy(
            src_ref=src, dst_ref=dst, send_sem=ssem, recv_sem=rsem, device_id=device, device_id_type=MESH
        )
        copy.start()
        return copy

    barrier = pltpu.get_barrier_semaphore()
    for d in range(1, across):
        pl.semaphore_signal(barrier, inc=1, device_id=in_column(d)[1], device_id_type=MESH)
    for d in range(1, n_lo):
        pl.semaphore_signal(barrier, inc=1, device_id=in_line(d)[1], device_id_type=MESH)

    plane = PX * GY
    cells = PZ * plane
    small = cells // 4
    row8 = lax.broadcasted_iota(jnp.int32, (PX, GY), 0)
    lane8 = lax.broadcasted_iota(jnp.int32, (PX, GY), 1)
    lane64 = lax.broadcasted_iota(jnp.int32, (C1, GY), 1)

    tall[...] = jnp.zeros_like(tall)
    for channel in range(2):
        for dx in range(3):
            for dy in range(3):
                shifted = []
                for z in range(PZ):
                    v = rounded(patch_ref[channel, z])
                    if dx == 0:
                        v = jnp.where(row8 == 0, 0.0, pltpu.roll(v, 1, 0))
                    elif dx == 2:
                        v = jnp.where(row8 == PX - 1, 0.0, pltpu.roll(v, PX - 1, 0))
                    if dy == 0:
                        v = jnp.where(lane8 == 0, 0.0, pltpu.roll(v, 1, 1))
                    elif dy == 2:
                        v = jnp.where(lane8 == GY - 1, 0.0, pltpu.roll(v, GY - 1, 1))
                    shifted.append(v)
                for dz in range(3):
                    r = ((dz * 3 + dx) * 3 + dy) * 2 + channel
                    for z in range(PZ):
                        if 0 <= z + dz - 1 < PZ:
                            tall[pl.ds(z * PX * C1 + r, PX, stride=C1), :] = shifted[z + dz - 1]
    for b in range(PZ * PX):
        cols[:, b * GY : (b + 1) * GY] = tall[b * C1 : (b + 1) * C1, :].astype(BF16)

    taps = w_stem.shape[1]
    depth = 27 * C1
    stem = w_stem[...]
    lift = w_lift[...]
    pooled = []
    for zz in range(PZ // 2):
        rows = []
        for z in (2 * zz, 2 * zz + 1):
            here = slice(z * plane, (z + 1) * plane)
            value, slope = silu_and_slope(mm(stem, cols[0:taps, here]))
            g1[:, here] = slope
            one = value.astype(BF16)
            l1[:, here] = one
            value, slope = silu_and_slope(mm(lift, one))
            g2[:, here] = slope
            two = value.astype(BF16)
            l2[:, here] = two
            rows.append(two.astype(F32))
        both = rows[0] + rows[1]
        for xx in range(PX // 2):
            pooled.append(rounded((block(both, 2 * xx) + block(both, 2 * xx + 1)) * 0.25))

    hz, hx = PZ // 2, PX // 2
    shifted = []
    for dy in range(3):
        if dy == 0:
            part = [jnp.where(lane64 == 0, 0.0, pltpu.roll(v, 1, 1)) for v in pooled]
        elif dy == 1:
            part = pooled
        else:
            part = [jnp.where(lane64 == GY - 1, 0.0, pltpu.roll(v, GY - 1, 1)) for v in pooled]
        shifted.append([v.astype(BF16) for v in part])
    nothing = jnp.zeros((C1, GY), BF16)
    for dz in range(3):
        for dx in range(3):
            for dy in range(3):
                r = ((dz * 3 + dx) * 3 + dy) * C1
                for z in range(hz):
                    for x in range(hx):
                        sz, sx = z + dz - 1, x + dx - 1
                        inside = 0 <= sz < hz and 0 <= sx < hx
                        b = z * hx + x
                        colsd[r : r + C1, b * GY : (b + 1) * GY] = (
                            shifted[dy][sz * hx + sx] if inside else nothing
                        )
    colsd[depth : depth + C1, :] = jnp.zeros((C1, small), BF16)
    value, slope_down = silu_and_slope(mm(w_down[...], colsd[0:depth, :]))
    coarse = value.astype(BF16)
    value, slope_deep = silu_and_slope(mm(w_deep[...], coarse))
    deeper = value.astype(BF16)
    merge_fine = w_fine[...]
    lifted = mm(w_coarse[...], deeper)

    out_col = w_proj_col[...]
    out8 = w_proj[0:8, :]
    fine_t = w_fine_t[...]
    slim = []
    gathered = [None] * (hz * hx)
    forecast = []
    for z in range(PZ):
        here = slice(z * plane, (z + 1) * plane)
        two = l2[:, here]
        added = [block(lifted, (z // 2) * hx + x // 2) for x in range(PX)]
        value, slope = silu_and_slope(mm(merge_fine, two) + jnp.concatenate(added, axis=1))
        merged = value.astype(BF16)
        wide = mm(out8, merged)
        predicted = jnp.zeros((PX, GY), F32)
        for x in range(PX):
            predicted = jnp.where(row8 == x, block(wide, x), predicted)
        forecast.append(predicted)
        misfit = (predicted - rounded(patch_ref[2, z])) * scale
        d_wide = jnp.concatenate(
            [jnp.broadcast_to(misfit[x : x + 1, :], (8, GY)) for x in range(PX)], axis=1
        ).astype(BF16)
        merged_ref[:, here] = merged
        d_merged = jnp.concatenate([out_col * misfit[x : x + 1, :] for x in range(PX)], axis=1)
        dz = rounded(d_merged) * slope
        for x in range(PX):
            b = (z // 2) * hx + x // 2
            gathered[b] = block(dz, x) if gathered[b] is None else gathered[b] + block(dz, x)
        dz = dz.astype(BF16)
        dz_ref[:, here] = dz
        slim.append(d_wide)

    half = PZ * PX // 2
    packet[0:half, :] = jnp.concatenate(forecast[0 : PZ // 2], axis=0).astype(BF16)
    packet[half : 2 * half, :] = jnp.concatenate(forecast[PZ // 2 : PZ], axis=0).astype(BF16)
    packet[2 * half : 2 * half + 16, :] = jnp.full((16, GY), slot_ref[0].astype(F32)).astype(BF16)
    pl.semaphore_wait(barrier, n_lo - 1 + across - 1)
    packets = []
    for d in range(1, n_hi):
        peer, device = in_part(d)
        packets.append(send(packet, pbuf.at[d], s3.at[d - 1], r3.at[d - 1], device))
    pbuf[0] = packet[...]

    d_lifted = jnp.concatenate(gathered, axis=1).astype(BF16)
    d_deeper = mm(w_coarse_t[...], d_lifted)
    dz_deep = (rounded(d_deeper) * slope_deep).astype(BF16)
    d_coarse = mm(w_deep_t[...], dz_deep)
    dz_down = (rounded(d_coarse) * slope_down).astype(BF16)

    r_ = lax.broadcasted_iota(jnp.int32, (C2, C2), 0)
    c_ = lax.broadcasted_iota(jnp.int32, (C2, C2), 1)
    parted = jnp.where(r_ < C1, 2 * r_, 2 * r_ - (C2 - 1)) == c_
    dz_parted = mm(parted.astype(BF16), dz_down).astype(BF16)
    base = 27 + 32
    chunks = [mm(dz_parted, colsd[j * C2 : (j + 1) * C2, :], NT) for j in range(14)]
    low = lane64 < C1
    for j in range(13):
        pack[pl.ds(base + j, C1, stride=27), :] = chunks[j][0:C1]
        pack[pl.ds(base + 14 + j, C1, stride=27), :] = pltpu.roll(
            jnp.where(low, chunks[j + 1][C1:C2], chunks[j][C1:C2]), C1, 1
        )
    pack[pl.ds(base + 13, C1, stride=27), :] = jnp.where(
        low, chunks[13][0:C1], pltpu.roll(chunks[0][C1:C2], C1, 1)
    )

    per = grads.shape[2]
    first = -(-(27 + 32) // (per * n_lo))
    top = n_hi - (27 + 32 + 27 * C1) // (per * n_lo)
    tail = first + top

    def emit(hi_):
        for lo_ in range(n_lo):
            start = (hi_ * n_lo + lo_) * per
            grads[lo_, (hi_ + top) % n_hi] = pack[start : start + per, :].astype(BF16)

    for h in range(first, n_hi - top):
        emit(h)
    early = []
    for d in range(1, n_lo):
        peer, device = in_line(d)
        early.append(
            send(
                grads.at[peer, pl.ds(tail, n_hi - tail)],
                buf1.at[d - 1, pl.ds(tail, n_hi - tail)],
                s1.at[d - 1],
                r1.at[d - 1],
                device,
            )
        )

    d_coarse_merge = mm(d_lifted, deeper, NT)
    d_deep = mm(dz_deep, coarse, NT)
    d_fine = jnp.zeros((C1, GY), F32)
    d_out = jnp.zeros((8, GY), F32)
    for z in range(PZ):
        here = slice(z * plane, (z + 1) * plane)
        merged = merged_ref[:, here]
        d_out = d_out + mm(slim[z], jnp.concatenate([merged, merged], axis=0), NT)
        two = l2[:, here]
        d_fine = d_fine + mm(dz_ref[:, here], jnp.concatenate([two, two], axis=0), NT)
    low32 = lax.broadcasted_iota(jnp.int32, (32, GY), 1) < C1
    base = 27 + 32 + 27 * C1
    pack[base : base + C2, :] = d_deep
    base = base + C2
    pair[...] = d_fine
    fine_even_odd = [pair[pl.ds(i, 32, stride=2), :] for i in range(2)]
    pair[...] = d_coarse_merge
    coarse_even_odd = [pair[pl.ds(i, 32, stride=2), :] for i in range(2)]
    turn = pltpu.roll(coarse_even_odd[0], C1, 1)
    pack[pl.ds(base, 32, stride=3), :] = jnp.where(low32, fine_even_odd[0], turn)
    pack[pl.ds(base + 1, 32, stride=3), :] = jnp.where(low32, turn, fine_even_odd[1])
    pack[pl.ds(base + 2, 32, stride=3), :] = coarse_even_odd[1]
    base = base + 96
    pack[base : base + 1, :] = jnp.where(lane8[0:1] < C1, d_out[0:1, :], 0.0)
    pack[base + 1 : GROWS, :] = jnp.zeros((GROWS - base - 1, GY), F32)


    blank = jnp.zeros((C2, GY), BF16)
    for dz in range(3):
        for dx in range(3):
            j = dz * 3 + dx
            for z in range(hz):
                for x in range(hx):
                    sz, sx = z - (dz - 1), x - (dx - 1)
                    inside = 0 <= sz < hz and 0 <= sx < hx
                    b = z * hx + x
                    colsz[j * C2 : (j + 1) * C2, b * GY : (b + 1) * GY] = (
                        block(dz_down, sz * hx + sx) if inside else blank
                    )
    d_shifted = mm(wback[...], colsz[...])
    d_pooled = []
    for b in range(hz * hx):
        whole = block(d_shifted, b)
        total = whole[C1 : 2 * C1]
        total = total + jnp.where(lane64 == GY - 1, 0.0, pltpu.roll(whole[0:C1], GY - 1, 1))
        total = total + jnp.where(lane64 == 0, 0.0, pltpu.roll(whole[2 * C1 : 3 * C1], 1, 1))
        d_pooled.append(rounded(total) * 0.25)

    lift_t = w_lift_t[...]
    d_lift = jnp.zeros((C1, GY), F32)
    d_stem = jnp.zeros((C1, C1), F32)
    for z in range(PZ):
        here = slice(z * plane, (z + 1) * plane)
        spread = jnp.concatenate([d_pooled[(z // 2) * hx + x // 2] for x in range(PX)], axis=1)
        dz = ((rounded(mm(fine_t, dz_ref[:, here])) + spread) * g2[:, here]).astype(BF16)
        one = l1[:, here]
        d_lift = d_lift + mm(dz, jnp.concatenate([one, one], axis=0), NT)
        d_one = rounded(mm(lift_t, dz))
        dz = (d_one * g1[:, here]).astype(BF16)
        d_stem = d_stem + mm(dz, cols[:, here], NT)

    pair[:, 0:C1] = d_stem
    pair[:, C1:GY] = jnp.zeros((C1, GY - C1), F32)
    turned = pair[...]
    source = lax.broadcasted_iota(jnp.int32, (C1, GY), 0)
    for bit in range(6):
        moved = pltpu.roll(turned, (taps << bit) % GY, 1)
        turned = jnp.where((source >> bit) % 2 == 1, moved, turned)
    begin = source * taps
    wraps = lane64 < begin % GY
    stay = jnp.where(wraps, 0.0, turned).astype(BF16)
    over = jnp.where(wraps, turned, 0.0).astype(BF16)
    target_row = lax.broadcasted_iota(jnp.int32, (32, C1), 0)
    owner = lax.broadcasted_iota(jnp.int32, (32, C1), 1) * taps // GY
    stem_rows = mm((target_row == owner).astype(BF16), stay)
    stem_rows = stem_rows + mm((target_row == owner + 1).astype(BF16), over)
    pack[0:27, :] = stem_rows[0:27, :]

    low32 = lax.broadcasted_iota(jnp.int32, (32, GY), 1) < C1
    pair[...] = d_lift
    pack[27 : 27 + 32, :] = jnp.where(low32, pair[pl.ds(0, 32, stride=2), :], pair[pl.ds(1, 32, stride=2), :])


    for h in list(range(first)) + list(range(n_hi - top, n_hi)):
        emit(h)
    late = []
    for d in range(1, n_lo):
        peer, device = in_line(d)
        late.append(
            send(
                grads.at[peer, pl.ds(0, tail)],
                buf1.at[d - 1, pl.ds(0, tail)],
                s1b.at[d - 1],
                r1b.at[d - 1],
                device,
            )
        )

    for copy in packets:
        copy.wait_recv()
    rows = PZ * PX

    def route(q, carry):
        wanted = (hi * (2 * n_lo) + q).astype(F32)
        value = jnp.zeros((rows, GY), F32)
        for src in range(n_hi):
            named = pbuf[src, rows : rows + 16, :].astype(F32)
            named = jnp.concatenate([named] * (rows // 16), axis=0)
            value = value + jnp.where(named == wanted, pbuf[src, 0:rows, :].astype(F32), 0.0)
        q_ref[q] = value.astype(BF16)
        return carry

    lax.fori_loop(0, 2 * n_lo, route, 0)
    routed = []
    for d in range(1, n_lo):
        peer, device = in_line(d)
        routed.append(send(q_ref.at[pl.ds(2 * peer, 2)], qbuf.at[d - 1], s4.at[d - 1], r4.at[d - 1], device))

    for copy in early + late:
        copy.wait_recv()

    partials = []
    for e in range(1, n_hi + 1):
        h = lax.rem(hi + e, n_hi)
        at = lax.rem(h + top, n_hi)
        value = grads[lo, at].astype(F32)
        for d in range(n_lo - 1):
            value = value + buf1[d, at].astype(F32)
        acc[h] = value.astype(BF16)
        for q in range(n_sec):
            if e == n_hi and q == 0:
                buf2[mine] = acc[h]
                continue
            owner = lax.rem(sec + q, n_sec)
            partials.append(
                send(
                    acc.at[h],
                    buf2.at[mine],
                    s2.at[q * n_hi + e - 1],
                    r2.at[q * n_hi + e - 1],
                    (owner, h * n_lo + lo),
                )
            )

    for copy in routed:
        copy.wait_recv()
    for s in range(2):
        value = q_ref[2 * lo + s].astype(F32)
        for d in range(n_lo - 1):
            value = value + qbuf[d, s].astype(F32)
        pred_out[s] = value

    for copy in partials:
        copy.wait_recv()
    for copy in packets + early + late + routed + partials:
        copy.wait_send()


def train(scale, n_sec, n_hi, n_lo, slot, patch, weights):
    cells = PZ * PX * GY
    small = cells // 4
    per = GROWS // (n_lo * n_hi)
    across = n_sec * n_hi
    dma = pltpu.SemaphoreType.DMA
    return pl.pallas_call(
        functools.partial(train_kernel, scale, n_sec, n_hi, n_lo),
        out_shape=(
            jax.ShapeDtypeStruct((2, PZ * PX, GY), F32),
            jax.ShapeDtypeStruct((across, per, GY), BF16),
        ),
        in_specs=[SMEM] + [VMEM] * 14,
        out_specs=(VMEM, VMEM),
        scratch_shapes=[
            pltpu.VMEM((PZ * PX * C1, GY), F32),
            pltpu.VMEM((C1, cells), BF16),
            pltpu.VMEM((C1, cells), BF16),
            pltpu.VMEM((C1, cells), BF16),
            pltpu.VMEM((C1, cells), F32),
            pltpu.VMEM((C1, cells), F32),
            pltpu.VMEM((C1, cells), BF16),
            pltpu.VMEM((C1, cells), BF16),
            pltpu.VMEM((28 * C1, small), BF16),
            pltpu.VMEM((9 * C2, small), BF16),
            pltpu.VMEM((GROWS, GY), F32),
            pltpu.VMEM((C1, GY), F32),
            pltpu.VMEM((n_lo, n_hi, per, GY), BF16),
            pltpu.VMEM((PZ * PX + 16, GY), BF16),
            pltpu.VMEM((n_lo - 1, n_hi, per, GY), BF16),
            pltpu.VMEM((n_hi, per, GY), BF16),
            pltpu.VMEM((n_hi, PZ * PX + 16, GY), BF16),
            pltpu.VMEM((2 * n_lo, PZ * PX, GY), BF16),
            pltpu.VMEM((n_lo - 1, 2, PZ * PX, GY), BF16),
            dma((n_lo - 1,)),
            dma((n_lo - 1,)),
            dma((n_lo - 1,)),
            dma((n_lo - 1,)),
            dma((across,)),
            dma((across,)),
            dma((n_hi - 1,)),
            dma((n_hi - 1,)),
            dma((n_lo - 1,)),
            dma((n_lo - 1,)),
        ],
        compiler_params=pltpu.CompilerParams(
            collective_id=1, has_side_effects=True, vmem_limit_bytes=32 * 2**20
        ),
        name="train",
    )(slot, patch, *weights)


def finish_kernel(heat_in, pred_in, grad_in, heat_out, pred_out, grad_out, done):
    copy = pltpu.make_async_copy(heat_in, heat_out, done)
    copy.start()
    total = grad_in[0].astype(F32)
    for t in range(1, grad_in.shape[0]):
        total = total + grad_in[t].astype(F32)
    grad_out[...] = total
    for s in range(2):
        for z in range(PZ):
            pred_out[s, z] = pred_in[s, z * PX : (z + 1) * PX, :].astype(BF16)
    copy.wait()


def finish(heat, preds, partials):
    return pl.pallas_call(
        finish_kernel,
        out_shape=(
            jax.ShapeDtypeStruct(heat.shape, F32),
            jax.ShapeDtypeStruct((2, PZ, PX, GY), BF16),
            jax.ShapeDtypeStruct(partials.shape[1:], F32),
        ),
        in_specs=[pl.BlockSpec(memory_space=pl.ANY), VMEM, VMEM],
        out_specs=(HBM, VMEM, VMEM),
        scratch_shapes=[pltpu.SemaphoreType.DMA],
        compiler_params=pltpu.CompilerParams(vmem_limit_bytes=8 * 2**20),
        name="finish",
    )(heat, preds, partials)


def local(
    n_sec,
    n_dp,
    heat_start,
    conductivity,
    patch_z,
    patch_x,
    slot_table,
    w_stem,
    w_lift,
    w_down,
    w_deep,
    w_merge,
    w_out,
):
    n_lo = LINE
    n_hi = n_dp // n_lo
    weights = (w_stem.T, w_lift, w_down.T, w_deep, w_merge, w_out)
    heat_two, patch, *ready = heat_steps(
        n_sec, n_dp, heat_start, conductivity, patch_z, patch_x, weights
    )
    scale = 1.0 / (n_sec * n_dp * PZ * PX * GY)
    preds, partials = train(scale, n_sec, n_hi, n_lo, slot_table, patch, ready)
    return finish(heat_two, preds, partials)


def solution(mesh):
    n_sec, n_dp = mesh.shape["section"], mesh.shape["dp"]
    both = ("section", "dp")
    return jax.shard_map(
        functools.partial(local, n_sec, n_dp),
        mesh=mesh,
        in_specs=(P(both, None, None), P(both, None, None), P(both), P(both), P(both)) + (P(),) * 6,
        out_specs=(P(both, None, None), P(both, None, None, None), P("dp", None)),
        check_vma=False,
    )
```

```python
import functools

import jax
import jax.numpy as jnp
from jax import lax
from jax.experimental import pallas as pl
from jax.experimental.pallas import tpu as pltpu
from jax.sharding import PartitionSpec as P

MESH = pl.DeviceIdType.MESH
TIME_STEP = 0.15
GY = 128
PZ = 4
PX = 8
C1 = 64
C2 = 128
GROWS = 2048
LINE = 8
F32 = jnp.float32
BF16 = jnp.bfloat16
VMEM = pl.BlockSpec(memory_space=pltpu.VMEM)
SMEM = pl.BlockSpec(memory_space=pltpu.SMEM)
HBM = pl.BlockSpec(memory_space=pltpu.HBM)


def rounded(x):
    return x.astype(BF16).astype(F32)


NT = (((1,), (1,)), ((), ()))
NN = (((1,), (0,)), ((), ()))


def mm(a, b, dims=NN):
    return lax.dot_general(a, b, dims, preferred_element_type=F32)


def heat_kernel(
    n_sec,
    n_dp,
    pz_ref,
    px_ref,
    slot_ref,
    u_hbm,
    k_hbm,
    stem_hbm,
    lift_hbm,
    down_hbm,
    deep_hbm,
    merge_hbm,
    proj_hbm,
    out_ref,
    patch_ref,
    stem_ref,
    lift_ref,
    lift_t,
    down_ref,
    down_back,
    deep_ref,
    deep_t,
    fine_ref,
    fine_t,
    coarse_ref,
    coarse_t,
    proj_col,
    slot_tile,
    v_stem,
    v_down,
    v_merge,
    v_proj,
    u_ref,
    k_ref,
    ulo,
    klo,
    uhi,
    khi,
    h1,
    load,
    send,
    recv,
):
    total = n_sec * n_dp
    depth = u_ref.shape[0]
    me = lax.axis_index("section") * n_dp + lax.axis_index("dp")
    after = lax.rem(me + 1, total)
    before = lax.rem(me + total - 1, total)

    def place(i):
        return (lax.div(i, n_dp), lax.rem(i, n_dp))

    barrier = pltpu.get_barrier_semaphore()
    below, above = me > 0, me < total - 1

    @pl.when(below)
    def _():
        pl.semaphore_signal(barrier, inc=1, device_id=place(before), device_id_type=MESH)

    @pl.when(above)
    def _():
        pl.semaphore_signal(barrier, inc=1, device_id=place(after), device_id_type=MESH)

    loads = [
        pltpu.make_async_copy(u_hbm, u_ref, load.at[0]),
        pltpu.make_async_copy(k_hbm, k_ref, load.at[1]),
        pltpu.make_async_copy(down_hbm, v_down, load.at[2]),
        pltpu.make_async_copy(stem_hbm, v_stem, load.at[3]),
        pltpu.make_async_copy(lift_hbm, lift_ref, load.at[4]),
        pltpu.make_async_copy(deep_hbm, deep_ref, load.at[5]),
        pltpu.make_async_copy(merge_hbm, v_merge, load.at[6]),
        pltpu.make_async_copy(proj_hbm, v_proj, load.at[7]),
    ]
    for copy in loads:
        copy.start()
    inner_slab = jnp.logical_and(below, above)

    @pl.when(inner_slab)
    def _():
        pl.semaphore_wait(barrier, 2)

    @pl.when(jnp.logical_not(inner_slab))
    def _():
        pl.semaphore_wait(barrier, 1)

    plan = (
        (u_hbm.at[pl.ds(depth - 2, 2)], ulo, after),
        (k_hbm.at[pl.ds(depth - 2, 2)], klo, after),
        (u_hbm.at[pl.ds(0, 2)], uhi, before),
        (k_hbm.at[pl.ds(0, 2)], khi, before),
    )
    copies = [
        pltpu.make_async_remote_copy(
            src_ref=src,
            dst_ref=dst,
            send_sem=send.at[i],
            recv_sem=recv.at[i],
            device_id=place(peer),
            device_id_type=MESH,
        )
        for i, (src, dst, peer) in enumerate(plan)
    ]
    upward, downward = copies[0:2], copies[2:4]

    @pl.when(above)
    def _():
        for copy in upward:
            copy.start()

    @pl.when(below)
    def _():
        for copy in downward:
            copy.start()

    @pl.when(me == 0)
    def _():
        ulo[...] = jnp.zeros_like(ulo)
        klo[...] = jnp.zeros_like(klo)

    @pl.when(me == total - 1)
    def _():
        uhi[...] = jnp.zeros_like(uhi)
        khi[...] = jnp.zeros_like(khi)

    rows, lanes = u_ref.shape[1:]
    row = lax.broadcasted_iota(jnp.int32, (rows, lanes), 0)
    lane = lax.broadcasted_iota(jnp.int32, (rows, lanes), 1)

    def step(up, uc, un, kp, kc, kn):
        flux = (kc + kn) * (un - uc) + (kc + kp) * (up - uc)
        for axis, place_, size in ((0, row, rows), (1, lane, lanes)):
            last = place_ == size - 1
            first = place_ == 0
            u_next = jnp.where(last, 0.0, pltpu.roll(uc, size - 1, axis))
            k_next = jnp.where(last, 0.0, pltpu.roll(kc, size - 1, axis))
            face = (kc + k_next) * (u_next - uc)
            back = jnp.where(first, kc * uc, pltpu.roll(face, 1, axis))
            flux = flux + (face - back)
        return uc + (0.5 * TIME_STEP) * flux

    for copy in loads:
        copy.wait()
    group = 7

    def interior(i, carry):
        for j in range(group):
            z = 1 + i * group + j
            h1[z + 1] = step(
                u_ref[z - 1], u_ref[z], u_ref[z + 1], k_ref[z - 1], k_ref[z], k_ref[z + 1]
            )
        return carry

    lax.fori_loop(0, (depth - 2) // group, interior, 0)

    def second(z):
        out_ref[z] = step(h1[z], h1[z + 1], h1[z + 2], k_ref[z - 1], k_ref[z], k_ref[z + 1])

    pack = 6

    def inner(i, carry):
        for j in range(pack):
            second(2 + i * pack + j)
        return carry

    lax.fori_loop(0, (depth - 4) // pack, inner, 0)
    unit = lax.broadcasted_iota(jnp.int32, (C2, C2), 0) == lax.broadcasted_iota(jnp.int32, (C2, C2), 1)
    eye = unit[0:C1, 0:C1]
    unit = unit.astype(BF16)
    stem_ref[...] = mm(unit[0:C1, 0:C1], v_stem[...], NT).astype(BF16)
    for dy in range(3):
        starts = [(j * 3 + dy) * C1 for j in range(9)]
        part = jnp.concatenate([v_down[r : r + C1, :] for r in starts], axis=0)
        down_ref[dy * C2 : (dy + 1) * C2, :] = mm(unit, part, NT).astype(BF16)
    for j in range(9):
        down_back[:, j * C2 : (j + 1) * C2] = v_down[j * 3 * C1 : (j + 1) * 3 * C1, :]

    def turned(x):
        return x.astype(F32).T.astype(BF16)

    lift_t[...] = turned(lift_ref[...])
    slot_tile[...] = jnp.full((16, GY), slot_ref[0].astype(F32)).astype(BF16)
    deep_t[...] = turned(deep_ref[...])
    fine = v_merge[:, 0:C1]
    coarse = v_merge[:, C1 : C1 + C2]
    fine_ref[...] = fine
    fine_t[...] = turned(fine)
    coarse_ref[...] = coarse
    coarse_t[...] = turned(coarse)
    row64 = v_proj[...].astype(F32)
    column = jnp.sum(jnp.where(eye, jnp.broadcast_to(row64, (C1, C1)), 0.0), axis=1, keepdims=True)
    proj_col[...] = jnp.broadcast_to(column, proj_col.shape)

    @pl.when(below)
    def _():
        for copy in upward:
            copy.wait_recv()

    @pl.when(above)
    def _():
        for copy in downward:
            copy.wait_recv()

    has_lo = (me > 0).astype(F32)
    has_hi = (me < total - 1).astype(F32)
    ul, kl, uh, kh = ulo, klo, uhi, khi
    end = depth - 1
    h1[0] = has_lo * step(ul[0], ul[1], u_ref[0], kl[0], kl[1], k_ref[0])
    h1[1] = step(ul[1], u_ref[0], u_ref[1], kl[1], k_ref[0], k_ref[1])
    h1[depth] = step(u_ref[end - 1], u_ref[end], uh[0], k_ref[end - 1], k_ref[end], kh[0])
    h1[depth + 1] = has_hi * step(u_ref[end], uh[0], uh[1], k_ref[end], kh[0], kh[1])

    out_ref[0] = step(h1[0], h1[1], h1[2], kl[1], k_ref[0], k_ref[1])
    out_ref[end] = step(h1[end], h1[depth], h1[depth + 1], k_ref[end - 1], k_ref[end], kh[0])
    second(1)
    second(end - 1)
    pz = pz_ref[0]
    px = px_ref[0]
    for z in range(PZ):
        patch_ref[0, z] = h1[1 + pz + z, pl.ds(px, PX), :]
        patch_ref[1, z] = k_ref[pz + z, pl.ds(px, PX), :]
        patch_ref[2, z] = out_ref[pz + z, pl.ds(px, PX), :]

    @pl.when(above)
    def _():
        for copy in upward:
            copy.wait_send()

    @pl.when(below)
    def _():
        for copy in downward:
            copy.wait_send()


def heat_steps(n_sec, n_dp, heat, cond, patch_z, patch_x, slot, weights):
    layers = (2,) + heat.shape[1:]
    operands = (heat, cond, *weights)
    operands = [pltpu.with_memory_space_constraint(x, pltpu.HBM) for x in operands]
    taps = weights[0].shape[0]
    return pl.pallas_call(
        functools.partial(heat_kernel, n_sec, n_dp),
        out_shape=(
            jax.ShapeDtypeStruct(heat.shape, F32),
            jax.ShapeDtypeStruct((3, PZ, PX, GY), F32),
            jax.ShapeDtypeStruct((C1, taps), BF16),
            jax.ShapeDtypeStruct((C1, C1), BF16),
            jax.ShapeDtypeStruct((C1, C1), BF16),
            jax.ShapeDtypeStruct((3 * C2, 9 * C1), BF16),
            jax.ShapeDtypeStruct((3 * C1, 9 * C2), BF16),
            jax.ShapeDtypeStruct((C2, C2), BF16),
            jax.ShapeDtypeStruct((C2, C2), BF16),
            jax.ShapeDtypeStruct((C1, C1), BF16),
            jax.ShapeDtypeStruct((C1, C1), BF16),
            jax.ShapeDtypeStruct((C1, C2), BF16),
            jax.ShapeDtypeStruct((C2, C1), BF16),
            jax.ShapeDtypeStruct((C1, GY), F32),
            jax.ShapeDtypeStruct((16, GY), BF16),
        ),
        in_specs=[SMEM] * 3 + [HBM] * 8,
        out_specs=(VMEM,) * 15,
        scratch_shapes=[
            pltpu.VMEM(weights[0].shape, BF16),
            pltpu.VMEM(weights[2].shape, BF16),
            pltpu.VMEM(weights[4].shape, BF16),
            pltpu.VMEM(weights[5].shape, BF16),
            pltpu.VMEM(heat.shape, F32),
            pltpu.VMEM(heat.shape, F32),
            pltpu.VMEM(layers, F32),
            pltpu.VMEM(layers, F32),
            pltpu.VMEM(layers, F32),
            pltpu.VMEM(layers, F32),
            pltpu.VMEM((heat.shape[0] + 2,) + heat.shape[1:], F32),
            pltpu.SemaphoreType.DMA((8,)),
            pltpu.SemaphoreType.DMA((4,)),
            pltpu.SemaphoreType.DMA((4,)),
        ],
        compiler_params=pltpu.CompilerParams(
            collective_id=0, has_side_effects=True, vmem_limit_bytes=16 * 2**20
        ),
        name="heat",
    )(patch_z, patch_x, slot, *operands)


def silu_and_slope(z):
    s = 0.5 * jnp.tanh(0.5 * z) + 0.5
    value = z * s
    return value, s + value * (1.0 - s)


def block(x, b):
    return x[:, b * GY : (b + 1) * GY]


def train_kernel(
    scale,
    n_sec,
    n_hi,
    n_lo,
    slot_tile,
    patch_ref,
    w_stem,
    w_lift,
    w_lift_t,
    w_down,
    wback,
    w_deep,
    w_deep_t,
    w_fine,
    w_fine_t,
    w_coarse,
    w_coarse_t,
    w_proj_col,
    pred_out,
    buf2,
    tall,
    cols,
    l1,
    l2,
    g1,
    g2,
    dz_ref,
    dz2_ref,
    colsd,
    colsz,
    pack,
    pair,
    grads,
    packet,
    cbuf,
    half_ref,
    buf1,
    buf_late,
    acc,
    pbuf,
    q_ref,
    qbuf,
    s1,
    r1,
    sc,
    rc,
    s5,
    r5,
    s2,
    r2,
    s3,
    r3,
    s4,
    r4,
):
    sec = lax.axis_index("section")
    dp = lax.axis_index("dp")
    hi = lax.div(dp, n_lo)
    lo = lax.rem(dp, n_lo)
    across = n_sec * n_hi
    mine = sec * n_hi + hi
    n_y = n_lo // 2
    core = lax.rem(lo, 2)
    other = 1 - core
    y = lax.div(lo, 2)

    def in_line(d):
        peer = lax.rem(lo + d, n_lo)
        return peer, (sec, hi * n_lo + peer)

    def in_y(d):
        peer = lax.rem(y + d, n_y)
        return peer, (sec, hi * n_lo + 2 * peer + core)

    def in_column(d):
        peer = lax.rem(mine + d, across)
        return peer, (lax.div(peer, n_hi), lax.rem(peer, n_hi) * n_lo + lo)

    def in_part(d):
        peer = lax.rem(hi + d, n_hi)
        return peer, (sec, peer * n_lo + lo)

    def send(src, dst, ssem, rsem, device):
        copy = pltpu.make_async_remote_copy(
            src_ref=src, dst_ref=dst, send_sem=ssem, recv_sem=rsem, device_id=device, device_id_type=MESH
        )
        copy.start()
        return copy

    barrier = pltpu.get_barrier_semaphore()
    for d in range(1, across):
        pl.semaphore_signal(barrier, inc=1, device_id=in_column(d)[1], device_id_type=MESH)
    for d in range(1, n_lo):
        pl.semaphore_signal(barrier, inc=1, device_id=in_line(d)[1], device_id_type=MESH)

    plane = PX * GY
    cells = PZ * plane
    small = cells // 4
    row8 = lax.broadcasted_iota(jnp.int32, (PX, GY), 0)
    lane8 = lax.broadcasted_iota(jnp.int32, (PX, GY), 1)
    lane64 = lax.broadcasted_iota(jnp.int32, (C1, GY), 1)

    tall[...] = jnp.zeros_like(tall)
    for channel in range(2):
        for dx in range(3):
            for dy in range(3):
                shifted = []
                for z in range(PZ):
                    v = rounded(patch_ref[channel, z])
                    if dx == 0:
                        v = jnp.where(row8 == 0, 0.0, pltpu.roll(v, 1, 0))
                    elif dx == 2:
                        v = jnp.where(row8 == PX - 1, 0.0, pltpu.roll(v, PX - 1, 0))
                    if dy == 0:
                        v = jnp.where(lane8 == 0, 0.0, pltpu.roll(v, 1, 1))
                    elif dy == 2:
                        v = jnp.where(lane8 == GY - 1, 0.0, pltpu.roll(v, GY - 1, 1))
                    shifted.append(v)
                for dz in range(3):
                    r = ((dz * 3 + dx) * 3 + dy) * 2 + channel
                    for z in range(PZ):
                        if 0 <= z + dz - 1 < PZ:
                            tall[pl.ds(z * PX * C1 + r, PX, stride=C1), :] = shifted[z + dz - 1]
    for b in range(PZ * PX):
        cols[:, b * GY : (b + 1) * GY] = tall[b * C1 : (b + 1) * C1, :].astype(BF16)

    taps = w_stem.shape[1]
    stem = w_stem[...]
    lift = w_lift[...]
    pooled = []
    for zz in range(PZ // 2):
        rows = []
        for z in (2 * zz, 2 * zz + 1):
            here = slice(z * plane, (z + 1) * plane)
            value, slope = silu_and_slope(mm(stem, cols[0:taps, here]))
            g1[:, here] = slope
            one = value.astype(BF16)
            l1[:, here] = one
            value, slope = silu_and_slope(mm(lift, one))
            g2[:, here] = slope
            two = value.astype(BF16)
            l2[:, here] = two
            rows.append(two.astype(F32))
        both = rows[0] + rows[1]
        for xx in range(PX // 2):
            pooled.append(rounded((block(both, 2 * xx) + block(both, 2 * xx + 1)) * 0.25))

    hz, hx = PZ // 2, PX // 2
    nothing = jnp.zeros((C1, GY), BF16)
    pooled = [v.astype(BF16) for v in pooled]
    for dz in range(3):
        for dx in range(3):
            r = (dz * 3 + dx) * C1
            for z in range(hz):
                for x in range(hx):
                    sz, sx = z + dz - 1, x + dx - 1
                    inside = 0 <= sz < hz and 0 <= sx < hx
                    b = z * hx + x
                    colsd[r : r + C1, b * GY : (b + 1) * GY] = pooled[sz * hx + sx] if inside else nothing
    depth = 9 * C1
    colsd[depth : depth + C1, :] = jnp.zeros((C1, small), BF16)
    products = mm(w_down[...], colsd[0:depth, :])
    lane128 = lax.broadcasted_iota(jnp.int32, (C2, GY), 1)

    def later(v):
        return jnp.where(lane128 == 0, 0.0, pltpu.roll(v, 1, 1))

    def sooner(v):
        return jnp.where(lane128 == GY - 1, 0.0, pltpu.roll(v, GY - 1, 1))

    summed = []
    for b in range(hz * hx):
        v = block(products, b)
        summed.append(later(v[0:C2]) + v[C2 : 2 * C2] + sooner(v[2 * C2 : 3 * C2]))
    value, slope_down = silu_and_slope(jnp.concatenate(summed, axis=1))
    coarse = value.astype(BF16)
    value, slope_deep = silu_and_slope(mm(w_deep[...], coarse))
    deeper = value.astype(BF16)
    merge_fine = w_fine[...]
    lifted = mm(w_coarse[...], deeper)

    out_col = w_proj_col[...]
    fine_t = w_fine_t[...]
    d_out = jnp.zeros((C1, GY), F32)
    gathered = [None] * (hz * hx)
    forecast = []
    for z in range(PZ):
        here = slice(z * plane, (z + 1) * plane)
        two = l2[:, here]
        added = [block(lifted, (z // 2) * hx + x // 2) for x in range(PX)]
        value, slope = silu_and_slope(mm(merge_fine, two) + jnp.concatenate(added, axis=1))
        merged = value.astype(BF16)
        held = merged.astype(F32)
        predicted = jnp.zeros((PX, GY), F32)
        for x in range(PX):
            summed = jnp.sum(block(held, x) * out_col, axis=0, keepdims=True)
            predicted = jnp.where(row8 == x, summed, predicted)
        forecast.append(predicted)
        misfit = (predicted - rounded(patch_ref[2, z])) * scale
        for x in range(PX):
            d_out = d_out + block(held, x) * misfit[x : x + 1, :]
        d_merged = jnp.concatenate([out_col * misfit[x : x + 1, :] for x in range(PX)], axis=1)
        dz = rounded(d_merged) * slope
        for x in range(PX):
            b = (z // 2) * hx + x // 2
            gathered[b] = block(dz, x) if gathered[b] is None else gathered[b] + block(dz, x)
        dz = dz.astype(BF16)
        dz_ref[:, here] = dz

    half = PZ * PX // 2
    packet[0:half, :] = jnp.concatenate(forecast[0 : PZ // 2], axis=0).astype(BF16)
    packet[half : 2 * half, :] = jnp.concatenate(forecast[PZ // 2 : PZ], axis=0).astype(BF16)
    packet[2 * half : 2 * half + 16, :] = slot_tile[...]
    pl.semaphore_wait(barrier, n_lo - 1 + across - 1)
    packets = []
    for d in range(1, n_hi):
        peer, device = in_part(d)
        packets.append(send(packet, pbuf.at[d], s3.at[d - 1], r3.at[d - 1], device))
    pbuf[0] = packet[...]

    d_lifted = jnp.concatenate(gathered, axis=1).astype(BF16)
    d_deeper = mm(w_coarse_t[...], d_lifted)
    dz_deep = (rounded(d_deeper) * slope_deep).astype(BF16)
    d_coarse = mm(w_deep_t[...], dz_deep)
    dz_down = (rounded(d_coarse) * slope_down).astype(BF16)

    r_ = lax.broadcasted_iota(jnp.int32, (C2, C2), 0)
    c_ = lax.broadcasted_iota(jnp.int32, (C2, C2), 1)
    parted = jnp.where(r_ < C1, 2 * r_, 2 * r_ - (C2 - 1)) == c_
    dz_parted = mm(parted.astype(BF16), dz_down)
    blocks = [block(dz_parted, b) for b in range(hz * hx)]
    dz_shifts = jnp.concatenate(
        [
            jnp.concatenate([f(v) for v in blocks], axis=1).astype(BF16)
            for f in (sooner, lambda v: v, later)
        ],
        axis=0,
    )
    d_down = mm(dz_shifts, colsd[...], NT)
    low = lane64 < C1
    turned_chunks = {}

    def piece(h, lanes_low):
        odd, h = divmod(h, 27)
        zx, dy = divmod(h, 3)
        q, high = divmod(zx, 2)
        r = dy * C2 + odd * C1
        chunk = d_down[r : r + C1, q * GY : (q + 1) * GY]
        if bool(high) != lanes_low:
            return chunk
        if (r, q) not in turned_chunks:
            turned_chunks[r, q] = pltpu.roll(chunk, C1, 1)
        return turned_chunks[r, q]

    base = 27 + 32
    for j in range(27):
        pack[pl.ds(base + j, C1, stride=27), :] = jnp.where(
            low, piece(2 * j, True), piece(2 * j + 1, False)
        )

    per = grads.shape[3]
    first = -(-(27 + 32) // (per * n_lo))
    top = n_hi - (27 + 32 + 27 * C1) // (per * n_lo)
    tail = first + top

    def emit(hi_):
        for lo_ in range(n_lo):
            start = (hi_ * n_lo + lo_) * per
            grads[lo_ % 2, lo_ // 2, (hi_ + top) % n_hi] = pack[start : start + per, :].astype(BF16)

    for h in range(first, n_hi - top):
        emit(h)

    def swap(begin, count, i):
        return send(
            grads.at[other, :, pl.ds(begin, count)],
            cbuf.at[:, pl.ds(begin, count)],
            sc.at[i],
            rc.at[i],
            (sec, hi * n_lo + 2 * y + other),
        )

    def chip_sum(begin, count, copy, i):
        copy.wait_recv()
        part = slice(begin, begin + count)
        for y_ in range(n_y):
            total = grads[core, y_, part].astype(F32) + cbuf[y_, part].astype(F32)
            half_ref[y_, part] = total.astype(BF16)
        copies = []
        for d in range(1, n_y):
            peer, device = in_y(d)
            copies.append(
                send(
                    half_ref.at[peer, pl.ds(begin, count)],
                    buf1.at[d - 1, pl.ds(begin, count)],
                    s1.at[i, d - 1],
                    r1.at[i, d - 1],
                    device,
                )
            )
        return copies

    swap_down = swap(tail, n_hi - tail, 0)

    def twice(x):
        pair[:, 0:C1] = x
        pair[:, C1:GY] = jnp.zeros((C1, GY - C1), F32)
        once = pair[...]
        return once + pltpu.roll(once, C1, 1)

    d_coarse_merge = mm(d_lifted, deeper, NT)
    d_deep = mm(dz_deep, coarse, NT)
    d_fine = twice(mm(dz_ref[...], l2[...], NT))
    low32 = lax.broadcasted_iota(jnp.int32, (32, GY), 1) < C1
    base = 27 + 32 + 27 * C1
    pack[base : base + C2, :] = d_deep
    base = base + C2
    pair[...] = d_fine
    fine_even_odd = [pair[pl.ds(i, 32, stride=2), :] for i in range(2)]
    pair[...] = d_coarse_merge
    coarse_even_odd = [pair[pl.ds(i, 32, stride=2), :] for i in range(2)]
    turn = pltpu.roll(coarse_even_odd[0], C1, 1)
    pack[pl.ds(base, 32, stride=3), :] = jnp.where(low32, fine_even_odd[0], turn)
    pack[pl.ds(base + 1, 32, stride=3), :] = jnp.where(low32, turn, fine_even_odd[1])
    pack[pl.ds(base + 2, 32, stride=3), :] = coarse_even_odd[1]
    base = base + 96
    column = jnp.sum(d_out, axis=1, keepdims=True)
    across_ = lane64 == lax.broadcasted_iota(jnp.int32, (C1, GY), 0)
    pack[base : base + 1, :] = jnp.sum(
        jnp.where(across_, jnp.broadcast_to(column, (C1, GY)), 0.0), axis=0, keepdims=True
    )
    pack[base + 1 : GROWS, :] = jnp.zeros((GROWS - base - 1, GY), F32)


    for h in range(n_hi - top, n_hi):
        emit(h)
    swap_join = swap(0, top, 1)

    blank = jnp.zeros((C2, GY), BF16)
    for dz in range(3):
        for dx in range(3):
            j = dz * 3 + dx
            for z in range(hz):
                for x in range(hx):
                    sz, sx = z - (dz - 1), x - (dx - 1)
                    inside = 0 <= sz < hz and 0 <= sx < hx
                    b = z * hx + x
                    colsz[j * C2 : (j + 1) * C2, b * GY : (b + 1) * GY] = (
                        block(dz_down, sz * hx + sx) if inside else blank
                    )
    early = chip_sum(tail, n_hi - tail, swap_down, 0)
    d_shifted = mm(wback[...], colsz[...])
    d_pooled = []
    for b in range(hz * hx):
        whole = block(d_shifted, b)
        total = whole[C1 : 2 * C1]
        total = total + jnp.where(lane64 == GY - 1, 0.0, pltpu.roll(whole[0:C1], GY - 1, 1))
        total = total + jnp.where(lane64 == 0, 0.0, pltpu.roll(whole[2 * C1 : 3 * C1], 1, 1))
        d_pooled.append(rounded(total) * 0.25)

    early += chip_sum(0, top, swap_join, 1)
    lift_t = w_lift_t[...]
    d_stem = jnp.zeros((C1, C1), F32)
    for z in range(PZ):
        here = slice(z * plane, (z + 1) * plane)
        spread = jnp.concatenate([d_pooled[(z // 2) * hx + x // 2] for x in range(PX)], axis=1)
        dz = ((rounded(mm(fine_t, dz_ref[:, here])) + spread) * g2[:, here]).astype(BF16)
        dz2_ref[:, here] = dz
        d_one = rounded(mm(lift_t, dz))
        dz = (d_one * g1[:, here]).astype(BF16)
        d_stem = d_stem + mm(dz, cols[:, here], NT)

    d_lift = twice(mm(dz2_ref[...], l1[...], NT))

    pair[:, 0:C1] = d_stem
    pair[:, C1:GY] = jnp.zeros((C1, GY - C1), F32)
    turned = pair[...]
    source = lax.broadcasted_iota(jnp.int32, (C1, GY), 0)
    for bit in range(6):
        moved = pltpu.roll(turned, (taps << bit) % GY, 1)
        turned = jnp.where((source >> bit) % 2 == 1, moved, turned)
    begin = source * taps
    wraps = lane64 < begin % GY
    stay = jnp.where(wraps, 0.0, turned).astype(BF16)
    over = jnp.where(wraps, turned, 0.0).astype(BF16)
    target_row = lax.broadcasted_iota(jnp.int32, (32, C1), 0)
    owner = lax.broadcasted_iota(jnp.int32, (32, C1), 1) * taps // GY
    stem_rows = mm((target_row == owner).astype(BF16), stay)
    stem_rows = stem_rows + mm((target_row == owner + 1).astype(BF16), over)
    pack[0:27, :] = stem_rows[0:27, :]

    low32 = lax.broadcasted_iota(jnp.int32, (32, GY), 1) < C1
    pair[...] = d_lift
    pack[27 : 27 + 32, :] = jnp.where(low32, pair[pl.ds(0, 32, stride=2), :], pair[pl.ds(1, 32, stride=2), :])


    for h in range(first):
        emit(h)
    late = []
    for d in range(1, n_lo):
        peer, device = in_line(d)
        late.append(
            send(
                grads.at[lax.rem(peer, 2), lax.div(peer, 2), pl.ds(top, first)],
                buf_late.at[d - 1],
                s5.at[d - 1],
                r5.at[d - 1],
                device,
            )
        )

    for copy in packets:
        copy.wait_recv()
    rows = PZ * PX

    def route(q, carry):
        wanted = (hi * (2 * n_lo) + q).astype(F32)
        value = jnp.zeros((rows, GY), F32)
        for src in range(n_hi):
            named = pbuf[src, rows : rows + 16, :].astype(F32)
            named = jnp.concatenate([named] * (rows // 16), axis=0)
            value = value + jnp.where(named == wanted, pbuf[src, 0:rows, :].astype(F32), 0.0)
        q_ref[q] = value.astype(BF16)
        return carry

    lax.fori_loop(0, 2 * n_lo, route, 0)
    routed = []
    for d in range(1, n_lo):
        peer, device = in_line(d)
        routed.append(send(q_ref.at[pl.ds(2 * peer, 2)], qbuf.at[d - 1], s4.at[d - 1], r4.at[d - 1], device))

    for copy in early:
        copy.wait_recv()
    for h in range(first, n_hi):
        at = (h + top) % n_hi
        value = half_ref[y, at].astype(F32)
        for d in range(n_y - 1):
            value = value + buf1[d, at].astype(F32)
        acc[h] = value.astype(BF16)
    for copy in late:
        copy.wait_recv()
    for h in range(first):
        value = grads[core, y, h + top].astype(F32)
        for d in range(n_lo - 1):
            value = value + buf_late[d, h].astype(F32)
        acc[h] = value.astype(BF16)
    partials = []
    ring = 8
    far_first = sorted(range(1, n_hi + 1), key=lambda e: (e == n_hi, -min(e % ring, ring - e % ring)))
    for e in far_first:
        h = lax.rem(hi + e, n_hi)
        for q in range(n_sec):
            if e == n_hi and q == 0:
                buf2[mine] = acc[h]
                continue
            owner = lax.rem(sec + q, n_sec)
            partials.append(
                send(
                    acc.at[h],
                    buf2.at[mine],
                    s2.at[q * n_hi + e - 1],
                    r2.at[q * n_hi + e - 1],
                    (owner, h * n_lo + lo),
                )
            )

    for copy in routed:
        copy.wait_recv()
    for s in range(2):
        value = q_ref[2 * lo + s].astype(F32)
        for d in range(n_lo - 1):
            value = value + qbuf[d, s].astype(F32)
        pred_out[s] = value

    for copy in partials:
        copy.wait_recv()
    for copy in [swap_down, swap_join] + packets + early + late + routed + partials:
        copy.wait_send()


def train(scale, n_sec, n_hi, n_lo, slot, patch, weights):
    cells = PZ * PX * GY
    small = cells // 4
    per = GROWS // (n_lo * n_hi)
    across = n_sec * n_hi
    n_y = n_lo // 2
    first = -(-(27 + 32) // (per * n_lo))
    dma = pltpu.SemaphoreType.DMA
    return pl.pallas_call(
        functools.partial(train_kernel, scale, n_sec, n_hi, n_lo),
        out_shape=(
            jax.ShapeDtypeStruct((2, PZ * PX, GY), F32),
            jax.ShapeDtypeStruct((across, per, GY), BF16),
        ),
        in_specs=[VMEM] * 14,
        out_specs=(VMEM, VMEM),
        scratch_shapes=[
            pltpu.VMEM((PZ * PX * C1, GY), F32),
            pltpu.VMEM((C1, cells), BF16),
            pltpu.VMEM((C1, cells), BF16),
            pltpu.VMEM((C1, cells), BF16),
            pltpu.VMEM((C1, cells), F32),
            pltpu.VMEM((C1, cells), F32),
            pltpu.VMEM((C1, cells), BF16),
            pltpu.VMEM((C1, cells), BF16),
            pltpu.VMEM((10 * C1, small), BF16),
            pltpu.VMEM((9 * C2, small), BF16),
            pltpu.VMEM((GROWS, GY), F32),
            pltpu.VMEM((C1, GY), F32),
            pltpu.VMEM((2, n_y, n_hi, per, GY), BF16),
            pltpu.VMEM((PZ * PX + 16, GY), BF16),
            pltpu.VMEM((n_y, n_hi, per, GY), BF16),
            pltpu.VMEM((n_y, n_hi, per, GY), BF16),
            pltpu.VMEM((n_y - 1, n_hi, per, GY), BF16),
            pltpu.VMEM((n_lo - 1, first, per, GY), BF16),
            pltpu.VMEM((n_hi, per, GY), BF16),
            pltpu.VMEM((n_hi, PZ * PX + 16, GY), BF16),
            pltpu.VMEM((2 * n_lo, PZ * PX, GY), BF16),
            pltpu.VMEM((n_lo - 1, 2, PZ * PX, GY), BF16),
            dma((2, n_y - 1)),
            dma((2, n_y - 1)),
            dma((2,)),
            dma((2,)),
            dma((n_lo - 1,)),
            dma((n_lo - 1,)),
            dma((across,)),
            dma((across,)),
            dma((n_hi - 1,)),
            dma((n_hi - 1,)),
            dma((n_lo - 1,)),
            dma((n_lo - 1,)),
        ],
        compiler_params=pltpu.CompilerParams(
            collective_id=1, has_side_effects=True, vmem_limit_bytes=32 * 2**20
        ),
        name="train",
    )(slot, patch, *weights)


def finish_kernel(heat_in, pred_in, grad_in, heat_out, pred_out, grad_out, done):
    copy = pltpu.make_async_copy(heat_in, heat_out, done)
    copy.start()
    total = grad_in[0].astype(F32)
    for t in range(1, grad_in.shape[0]):
        total = total + grad_in[t].astype(F32)
    grad_out[...] = total
    for s in range(2):
        for z in range(PZ):
            pred_out[s, z] = pred_in[s, z * PX : (z + 1) * PX, :].astype(BF16)
    copy.wait()


def finish(heat, preds, partials):
    return pl.pallas_call(
        finish_kernel,
        out_shape=(
            jax.ShapeDtypeStruct(heat.shape, F32),
            jax.ShapeDtypeStruct((2, PZ, PX, GY), BF16),
            jax.ShapeDtypeStruct(partials.shape[1:], F32),
        ),
        in_specs=[pl.BlockSpec(memory_space=pl.ANY), VMEM, VMEM],
        out_specs=(HBM, VMEM, VMEM),
        scratch_shapes=[pltpu.SemaphoreType.DMA],
        compiler_params=pltpu.CompilerParams(vmem_limit_bytes=8 * 2**20),
        name="finish",
    )(heat, preds, partials)


def local(
    n_sec,
    n_dp,
    heat_start,
    conductivity,
    patch_z,
    patch_x,
    slot_table,
    w_stem,
    w_lift,
    w_down,
    w_deep,
    w_merge,
    w_out,
):
    n_lo = LINE
    n_hi = n_dp // n_lo
    weights = (w_stem.T, w_lift, w_down.T, w_deep, w_merge, w_out)
    heat_two, patch, *ready, slot = heat_steps(
        n_sec, n_dp, heat_start, conductivity, patch_z, patch_x, slot_table, weights
    )
    scale = 1.0 / (n_sec * n_dp * PZ * PX * GY)
    preds, partials = train(scale, n_sec, n_hi, n_lo, slot, patch, ready)
    return finish(heat_two, preds, partials)


def solution(mesh):
    n_sec, n_dp = mesh.shape["section"], mesh.shape["dp"]
    both = ("section", "dp")
    return jax.shard_map(
        functools.partial(local, n_sec, n_dp),
        mesh=mesh,
        in_specs=(P(both, None, None), P(both, None, None), P(both), P(both), P(both)) + (P(),) * 6,
        out_specs=(P(both, None, None), P(both, None, None, None), P("dp", None)),
        check_vma=False,
    )
```

```python
import functools

import jax
import jax.numpy as jnp
from jax import lax
from jax.experimental import pallas as pl
from jax.experimental.pallas import tpu as pltpu
from jax.sharding import PartitionSpec as P

MESH = pl.DeviceIdType.MESH
TIME_STEP = 0.15
GY = 128
PZ = 4
PX = 8
C1 = 64
C2 = 128
GROWS = 2048
LINE = 8
F32 = jnp.float32
BF16 = jnp.bfloat16
VMEM = pl.BlockSpec(memory_space=pltpu.VMEM)
SMEM = pl.BlockSpec(memory_space=pltpu.SMEM)
HBM = pl.BlockSpec(memory_space=pltpu.HBM)


def rounded(x):
    return x.astype(BF16).astype(F32)


NT = (((1,), (1,)), ((), ()))
NN = (((1,), (0,)), ((), ()))


def mm(a, b, dims=NN):
    return lax.dot_general(a, b, dims, preferred_element_type=F32)


def heat_kernel(
    n_sec,
    n_dp,
    pz_ref,
    px_ref,
    slot_ref,
    u_hbm,
    k_hbm,
    stem_hbm,
    lift_hbm,
    down_hbm,
    deep_hbm,
    merge_hbm,
    proj_hbm,
    out_ref,
    patch_ref,
    stem_ref,
    lift_ref,
    lift_t,
    down_ref,
    down_back,
    deep_ref,
    deep_t,
    fine_ref,
    fine_t,
    coarse_ref,
    coarse_t,
    proj_col,
    slot_tile,
    v_stem,
    v_down,
    v_merge,
    v_proj,
    u_ref,
    k_ref,
    ulo,
    klo,
    uhi,
    khi,
    h1,
    load,
    send,
    recv,
):
    total = n_sec * n_dp
    depth = u_ref.shape[0]
    me = lax.axis_index("section") * n_dp + lax.axis_index("dp")
    after = lax.rem(me + 1, total)
    before = lax.rem(me + total - 1, total)

    def place(i):
        return (lax.div(i, n_dp), lax.rem(i, n_dp))

    barrier = pltpu.get_barrier_semaphore()
    below, above = me > 0, me < total - 1

    @pl.when(below)
    def _():
        pl.semaphore_signal(barrier, inc=1, device_id=place(before), device_id_type=MESH)

    @pl.when(above)
    def _():
        pl.semaphore_signal(barrier, inc=1, device_id=place(after), device_id_type=MESH)

    loads = [
        pltpu.make_async_copy(u_hbm, u_ref, load.at[0]),
        pltpu.make_async_copy(k_hbm, k_ref, load.at[1]),
        pltpu.make_async_copy(down_hbm, v_down, load.at[2]),
        pltpu.make_async_copy(stem_hbm, v_stem, load.at[3]),
        pltpu.make_async_copy(lift_hbm, lift_ref, load.at[4]),
        pltpu.make_async_copy(deep_hbm, deep_ref, load.at[5]),
        pltpu.make_async_copy(merge_hbm, v_merge, load.at[6]),
        pltpu.make_async_copy(proj_hbm, v_proj, load.at[7]),
    ]
    for copy in loads:
        copy.start()
    inner_slab = jnp.logical_and(below, above)

    @pl.when(inner_slab)
    def _():
        pl.semaphore_wait(barrier, 2)

    @pl.when(jnp.logical_not(inner_slab))
    def _():
        pl.semaphore_wait(barrier, 1)

    plan = (
        (u_hbm.at[pl.ds(depth - 2, 2)], ulo, after),
        (k_hbm.at[pl.ds(depth - 2, 2)], klo, after),
        (u_hbm.at[pl.ds(0, 2)], uhi, before),
        (k_hbm.at[pl.ds(0, 2)], khi, before),
    )
    copies = [
        pltpu.make_async_remote_copy(
            src_ref=src,
            dst_ref=dst,
            send_sem=send.at[i],
            recv_sem=recv.at[i],
            device_id=place(peer),
            device_id_type=MESH,
        )
        for i, (src, dst, peer) in enumerate(plan)
    ]
    upward, downward = copies[0:2], copies[2:4]

    @pl.when(above)
    def _():
        for copy in upward:
            copy.start()

    @pl.when(below)
    def _():
        for copy in downward:
            copy.start()

    @pl.when(me == 0)
    def _():
        ulo[...] = jnp.zeros_like(ulo)
        klo[...] = jnp.zeros_like(klo)

    @pl.when(me == total - 1)
    def _():
        uhi[...] = jnp.zeros_like(uhi)
        khi[...] = jnp.zeros_like(khi)

    rows, lanes = u_ref.shape[1:]
    row = lax.broadcasted_iota(jnp.int32, (rows, lanes), 0)
    lane = lax.broadcasted_iota(jnp.int32, (rows, lanes), 1)

    def step(up, uc, un, kp, kc, kn):
        flux = (kc + kn) * (un - uc) + (kc + kp) * (up - uc)
        for axis, place_, size in ((0, row, rows), (1, lane, lanes)):
            last = place_ == size - 1
            first = place_ == 0
            u_next = jnp.where(last, 0.0, pltpu.roll(uc, size - 1, axis))
            k_next = jnp.where(last, 0.0, pltpu.roll(kc, size - 1, axis))
            face = (kc + k_next) * (u_next - uc)
            back = jnp.where(first, kc * uc, pltpu.roll(face, 1, axis))
            flux = flux + (face - back)
        return uc + (0.5 * TIME_STEP) * flux

    for copy in loads:
        copy.wait()
    group = 7

    def interior(i, carry):
        for j in range(group):
            z = 1 + i * group + j
            h1[z + 1] = step(
                u_ref[z - 1], u_ref[z], u_ref[z + 1], k_ref[z - 1], k_ref[z], k_ref[z + 1]
            )
        return carry

    lax.fori_loop(0, (depth - 2) // group, interior, 0)

    def second(z):
        out_ref[z] = step(h1[z], h1[z + 1], h1[z + 2], k_ref[z - 1], k_ref[z], k_ref[z + 1])

    pack = 6

    def inner(i, carry):
        for j in range(pack):
            second(2 + i * pack + j)
        return carry

    lax.fori_loop(0, (depth - 4) // pack, inner, 0)
    unit = lax.broadcasted_iota(jnp.int32, (C2, C2), 0) == lax.broadcasted_iota(jnp.int32, (C2, C2), 1)
    eye = unit[0:C1, 0:C1]
    unit = unit.astype(BF16)
    stem_ref[...] = mm(unit[0:C1, 0:C1], v_stem[...], NT).astype(BF16)
    for dy in range(3):
        starts = [(j * 3 + dy) * C1 for j in range(9)]
        part = jnp.concatenate([v_down[r : r + C1, :] for r in starts], axis=0)
        down_ref[dy * C2 : (dy + 1) * C2, :] = mm(unit, part, NT).astype(BF16)
    for j in range(9):
        down_back[:, j * C2 : (j + 1) * C2] = v_down[j * 3 * C1 : (j + 1) * 3 * C1, :]

    def turned(x):
        return x.astype(F32).T.astype(BF16)

    lift_t[...] = turned(lift_ref[...])
    slot_tile[...] = jnp.full((16, GY), slot_ref[0].astype(F32)).astype(BF16)
    deep_t[...] = turned(deep_ref[...])
    fine = v_merge[:, 0:C1]
    coarse = v_merge[:, C1 : C1 + C2]
    fine_ref[...] = fine
    fine_t[...] = turned(fine)
    coarse_ref[...] = coarse
    coarse_t[...] = turned(coarse)
    row64 = v_proj[...].astype(F32)
    column = jnp.sum(jnp.where(eye, jnp.broadcast_to(row64, (C1, C1)), 0.0), axis=1, keepdims=True)
    proj_col[...] = jnp.broadcast_to(column, proj_col.shape)

    @pl.when(below)
    def _():
        for copy in upward:
            copy.wait_recv()

    @pl.when(above)
    def _():
        for copy in downward:
            copy.wait_recv()

    has_lo = (me > 0).astype(F32)
    has_hi = (me < total - 1).astype(F32)
    ul, kl, uh, kh = ulo, klo, uhi, khi
    end = depth - 1
    h1[0] = has_lo * step(ul[0], ul[1], u_ref[0], kl[0], kl[1], k_ref[0])
    h1[1] = step(ul[1], u_ref[0], u_ref[1], kl[1], k_ref[0], k_ref[1])
    h1[depth] = step(u_ref[end - 1], u_ref[end], uh[0], k_ref[end - 1], k_ref[end], kh[0])
    h1[depth + 1] = has_hi * step(u_ref[end], uh[0], uh[1], k_ref[end], kh[0], kh[1])

    out_ref[0] = step(h1[0], h1[1], h1[2], kl[1], k_ref[0], k_ref[1])
    out_ref[end] = step(h1[end], h1[depth], h1[depth + 1], k_ref[end - 1], k_ref[end], kh[0])
    second(1)
    second(end - 1)
    pz = pz_ref[0]
    px = px_ref[0]
    for z in range(PZ):
        patch_ref[0, z] = h1[1 + pz + z, pl.ds(px, PX), :]
        patch_ref[1, z] = k_ref[pz + z, pl.ds(px, PX), :]
        patch_ref[2, z] = out_ref[pz + z, pl.ds(px, PX), :]

    @pl.when(above)
    def _():
        for copy in upward:
            copy.wait_send()

    @pl.when(below)
    def _():
        for copy in downward:
            copy.wait_send()


def heat_steps(n_sec, n_dp, heat, cond, patch_z, patch_x, slot, weights):
    layers = (2,) + heat.shape[1:]
    operands = (heat, cond, *weights)
    operands = [pltpu.with_memory_space_constraint(x, pltpu.HBM) for x in operands]
    taps = weights[0].shape[0]
    return pl.pallas_call(
        functools.partial(heat_kernel, n_sec, n_dp),
        out_shape=(
            jax.ShapeDtypeStruct(heat.shape, F32),
            jax.ShapeDtypeStruct((3, PZ, PX, GY), F32),
            jax.ShapeDtypeStruct((C1, taps), BF16),
            jax.ShapeDtypeStruct((C1, C1), BF16),
            jax.ShapeDtypeStruct((C1, C1), BF16),
            jax.ShapeDtypeStruct((3 * C2, 9 * C1), BF16),
            jax.ShapeDtypeStruct((3 * C1, 9 * C2), BF16),
            jax.ShapeDtypeStruct((C2, C2), BF16),
            jax.ShapeDtypeStruct((C2, C2), BF16),
            jax.ShapeDtypeStruct((C1, C1), BF16),
            jax.ShapeDtypeStruct((C1, C1), BF16),
            jax.ShapeDtypeStruct((C1, C2), BF16),
            jax.ShapeDtypeStruct((C2, C1), BF16),
            jax.ShapeDtypeStruct((C1, GY), F32),
            jax.ShapeDtypeStruct((16, GY), BF16),
        ),
        in_specs=[SMEM] * 3 + [HBM] * 8,
        out_specs=(VMEM,) * 15,
        scratch_shapes=[
            pltpu.VMEM(weights[0].shape, BF16),
            pltpu.VMEM(weights[2].shape, BF16),
            pltpu.VMEM(weights[4].shape, BF16),
            pltpu.VMEM(weights[5].shape, BF16),
            pltpu.VMEM(heat.shape, F32),
            pltpu.VMEM(heat.shape, F32),
            pltpu.VMEM(layers, F32),
            pltpu.VMEM(layers, F32),
            pltpu.VMEM(layers, F32),
            pltpu.VMEM(layers, F32),
            pltpu.VMEM((heat.shape[0] + 2,) + heat.shape[1:], F32),
            pltpu.SemaphoreType.DMA((8,)),
            pltpu.SemaphoreType.DMA((4,)),
            pltpu.SemaphoreType.DMA((4,)),
        ],
        compiler_params=pltpu.CompilerParams(
            collective_id=0, has_side_effects=True, vmem_limit_bytes=16 * 2**20
        ),
        name="heat",
    )(patch_z, patch_x, slot, *operands)


def silu_and_slope(z):
    s = 0.5 * jnp.tanh(0.5 * z) + 0.5
    value = z * s
    return value, s + value * (1.0 - s)


def block(x, b):
    return x[:, b * GY : (b + 1) * GY]


def train_kernel(
    scale,
    n_sec,
    n_hi,
    n_lo,
    slot_tile,
    patch_ref,
    w_stem,
    w_lift,
    w_lift_t,
    w_down,
    wback,
    w_deep,
    w_deep_t,
    w_fine,
    w_fine_t,
    w_coarse,
    w_coarse_t,
    w_proj_col,
    pred_out,
    buf2,
    tall,
    cols,
    l1,
    l2,
    g1,
    g2,
    dz_ref,
    dz2_ref,
    colsd,
    colsz,
    pack,
    pair,
    grads,
    packet,
    cbuf,
    half_ref,
    buf1,
    buf_late,
    acc,
    pbuf,
    q_ref,
    qbuf,
    s1,
    r1,
    sc,
    rc,
    s5,
    r5,
    s2,
    r2,
    s3,
    r3,
    s4,
    r4,
):
    sec = lax.axis_index("section")
    dp = lax.axis_index("dp")
    hi = lax.div(dp, n_lo)
    lo = lax.rem(dp, n_lo)
    across = n_sec * n_hi
    mine = sec * n_hi + hi
    n_y = n_lo // 2
    core = lax.rem(lo, 2)
    other = 1 - core
    y = lax.div(lo, 2)

    def in_line(d):
        peer = lax.rem(lo + d, n_lo)
        return peer, (sec, hi * n_lo + peer)

    def in_y(d):
        peer = lax.rem(y + d, n_y)
        return peer, (sec, hi * n_lo + 2 * peer + core)

    def in_column(d):
        peer = lax.rem(mine + d, across)
        return peer, (lax.div(peer, n_hi), lax.rem(peer, n_hi) * n_lo + lo)

    def in_part(d):
        peer = lax.rem(hi + d, n_hi)
        return peer, (sec, peer * n_lo + lo)

    def send(src, dst, ssem, rsem, device):
        copy = pltpu.make_async_remote_copy(
            src_ref=src, dst_ref=dst, send_sem=ssem, recv_sem=rsem, device_id=device, device_id_type=MESH
        )
        copy.start()
        return copy

    barrier = pltpu.get_barrier_semaphore()
    for d in range(1, across):
        pl.semaphore_signal(barrier, inc=1, device_id=in_column(d)[1], device_id_type=MESH)
    for d in range(1, n_lo):
        pl.semaphore_signal(barrier, inc=1, device_id=in_line(d)[1], device_id_type=MESH)

    plane = PX * GY
    cells = PZ * plane
    small = cells // 4
    row8 = lax.broadcasted_iota(jnp.int32, (PX, GY), 0)
    lane8 = lax.broadcasted_iota(jnp.int32, (PX, GY), 1)
    lane64 = lax.broadcasted_iota(jnp.int32, (C1, GY), 1)

    tall[...] = jnp.zeros_like(tall)
    for channel in range(2):
        for dx in range(3):
            for dy in range(3):
                shifted = []
                for z in range(PZ):
                    v = rounded(patch_ref[channel, z])
                    if dx == 0:
                        v = jnp.where(row8 == 0, 0.0, pltpu.roll(v, 1, 0))
                    elif dx == 2:
                        v = jnp.where(row8 == PX - 1, 0.0, pltpu.roll(v, PX - 1, 0))
                    if dy == 0:
                        v = jnp.where(lane8 == 0, 0.0, pltpu.roll(v, 1, 1))
                    elif dy == 2:
                        v = jnp.where(lane8 == GY - 1, 0.0, pltpu.roll(v, GY - 1, 1))
                    shifted.append(v)
                for dz in range(3):
                    r = ((dz * 3 + dx) * 3 + dy) * 2 + channel
                    for z in range(PZ):
                        if 0 <= z + dz - 1 < PZ:
                            tall[pl.ds(z * PX * C1 + r, PX, stride=C1), :] = shifted[z + dz - 1]
    for b in range(PZ * PX):
        cols[:, b * GY : (b + 1) * GY] = tall[b * C1 : (b + 1) * C1, :].astype(BF16)

    taps = w_stem.shape[1]
    stem = w_stem[...]
    lift = w_lift[...]
    pooled = []
    for zz in range(PZ // 2):
        rows = []
        for z in (2 * zz, 2 * zz + 1):
            here = slice(z * plane, (z + 1) * plane)
            value, slope = silu_and_slope(mm(stem, cols[0:taps, here]))
            g1[:, here] = slope
            one = value.astype(BF16)
            l1[:, here] = one
            value, slope = silu_and_slope(mm(lift, one))
            g2[:, here] = slope
            two = value.astype(BF16)
            l2[:, here] = two
            rows.append(two.astype(F32))
        both = rows[0] + rows[1]
        for xx in range(PX // 2):
            pooled.append(rounded((block(both, 2 * xx) + block(both, 2 * xx + 1)) * 0.25))

    hz, hx = PZ // 2, PX // 2
    nothing = jnp.zeros((C1, GY), BF16)
    pooled = [v.astype(BF16) for v in pooled]
    for dz in range(3):
        for dx in range(3):
            r = (dz * 3 + dx) * C1
            for z in range(hz):
                for x in range(hx):
                    sz, sx = z + dz - 1, x + dx - 1
                    inside = 0 <= sz < hz and 0 <= sx < hx
                    b = z * hx + x
                    colsd[r : r + C1, b * GY : (b + 1) * GY] = pooled[sz * hx + sx] if inside else nothing
    depth = 9 * C1
    colsd[depth : depth + C1, :] = jnp.zeros((C1, small), BF16)
    products = mm(w_down[...], colsd[0:depth, :])
    lane128 = lax.broadcasted_iota(jnp.int32, (C2, GY), 1)

    def later(v):
        return jnp.where(lane128 == 0, 0.0, pltpu.roll(v, 1, 1))

    def sooner(v):
        return jnp.where(lane128 == GY - 1, 0.0, pltpu.roll(v, GY - 1, 1))

    summed = []
    for b in range(hz * hx):
        v = block(products, b)
        summed.append(later(v[0:C2]) + v[C2 : 2 * C2] + sooner(v[2 * C2 : 3 * C2]))
    value, slope_down = silu_and_slope(jnp.concatenate(summed, axis=1))
    coarse = value.astype(BF16)
    value, slope_deep = silu_and_slope(mm(w_deep[...], coarse))
    deeper = value.astype(BF16)
    merge_fine = w_fine[...]
    lifted = mm(w_coarse[...], deeper)

    out_col = w_proj_col[...]
    fine_t = w_fine_t[...]
    d_out = jnp.zeros((C1, GY), F32)
    gathered = [None] * (hz * hx)
    forecast = []
    for z in range(PZ):
        here = slice(z * plane, (z + 1) * plane)
        two = l2[:, here]
        added = [block(lifted, (z // 2) * hx + x // 2) for x in range(PX)]
        value, slope = silu_and_slope(mm(merge_fine, two) + jnp.concatenate(added, axis=1))
        merged = value.astype(BF16)
        held = merged.astype(F32)
        predicted = jnp.zeros((PX, GY), F32)
        for x in range(PX):
            summed = jnp.sum(block(held, x) * out_col, axis=0, keepdims=True)
            predicted = jnp.where(row8 == x, summed, predicted)
        forecast.append(predicted)
        misfit = (predicted - rounded(patch_ref[2, z])) * scale
        for x in range(PX):
            d_out = d_out + block(held, x) * misfit[x : x + 1, :]
        d_merged = jnp.concatenate([out_col * misfit[x : x + 1, :] for x in range(PX)], axis=1)
        dz = rounded(d_merged) * slope
        for x in range(PX):
            b = (z // 2) * hx + x // 2
            gathered[b] = block(dz, x) if gathered[b] is None else gathered[b] + block(dz, x)
        dz = dz.astype(BF16)
        dz_ref[:, here] = dz

    half = PZ * PX // 2
    packet[0:half, :] = jnp.concatenate(forecast[0 : PZ // 2], axis=0).astype(BF16)
    packet[half : 2 * half, :] = jnp.concatenate(forecast[PZ // 2 : PZ], axis=0).astype(BF16)
    packet[2 * half : 2 * half + 16, :] = slot_tile[...]
    pl.semaphore_wait(barrier, n_lo - 1 + across - 1)
    packets = []
    for d in range(1, n_hi):
        peer, device = in_part(d)
        packets.append(send(packet, pbuf.at[d], s3.at[d - 1], r3.at[d - 1], device))
    pbuf[0] = packet[...]

    d_lifted = jnp.concatenate(gathered, axis=1).astype(BF16)
    d_deeper = mm(w_coarse_t[...], d_lifted)
    dz_deep = (rounded(d_deeper) * slope_deep).astype(BF16)
    d_coarse = mm(w_deep_t[...], dz_deep)
    dz_down = (rounded(d_coarse) * slope_down).astype(BF16)

    r_ = lax.broadcasted_iota(jnp.int32, (C2, C2), 0)
    c_ = lax.broadcasted_iota(jnp.int32, (C2, C2), 1)
    parted = jnp.where(r_ < C1, 2 * r_, 2 * r_ - (C2 - 1)) == c_
    dz_parted = mm(parted.astype(BF16), dz_down)
    blocks = [block(dz_parted, b) for b in range(hz * hx)]
    dz_shifts = jnp.concatenate(
        [
            jnp.concatenate([f(v) for v in blocks], axis=1).astype(BF16)
            for f in (sooner, lambda v: v, later)
        ],
        axis=0,
    )
    d_down = mm(dz_shifts, colsd[...], NT)
    low = lane64 < C1
    turned_chunks = {}

    def piece(h, lanes_low):
        odd, h = divmod(h, 27)
        zx, dy = divmod(h, 3)
        q, high = divmod(zx, 2)
        r = dy * C2 + odd * C1
        chunk = d_down[r : r + C1, q * GY : (q + 1) * GY]
        if bool(high) != lanes_low:
            return chunk
        if (r, q) not in turned_chunks:
            turned_chunks[r, q] = pltpu.roll(chunk, C1, 1)
        return turned_chunks[r, q]

    base = 27 + 32
    for j in range(27):
        pack[pl.ds(base + j, C1, stride=27), :] = jnp.where(
            low, piece(2 * j, True), piece(2 * j + 1, False)
        )

    per = grads.shape[3]
    first = -(-(27 + 32) // (per * n_lo))
    top = n_hi - (27 + 32 + 27 * C1) // (per * n_lo)
    tail = first + top

    def emit(hi_):
        for lo_ in range(n_lo):
            start = (hi_ * n_lo + lo_) * per
            grads[lo_ % 2, lo_ // 2, (hi_ + top) % n_hi] = pack[start : start + per, :].astype(BF16)

    for h in range(first, n_hi - top):
        emit(h)

    def swap(begin, count, i):
        return send(
            grads.at[other, :, pl.ds(begin, count)],
            cbuf.at[:, pl.ds(begin, count)],
            sc.at[i],
            rc.at[i],
            (sec, hi * n_lo + 2 * y + other),
        )

    def chip_sum(begin, count, copy, i):
        copy.wait_recv()
        part = slice(begin, begin + count)
        for y_ in range(n_y):
            total = grads[core, y_, part].astype(F32) + cbuf[y_, part].astype(F32)
            half_ref[y_, part] = total.astype(BF16)
        copies = []
        for d in range(1, n_y):
            peer, device = in_y(d)
            copies.append(
                send(
                    half_ref.at[peer, pl.ds(begin, count)],
                    buf1.at[d - 1, pl.ds(begin, count)],
                    s1.at[i, d - 1],
                    r1.at[i, d - 1],
                    device,
                )
            )
        return copies

    swap_down = swap(tail, n_hi - tail, 0)

    def twice(x):
        pair[:, 0:C1] = x
        pair[:, C1:GY] = jnp.zeros((C1, GY - C1), F32)
        once = pair[...]
        return once + pltpu.roll(once, C1, 1)

    d_coarse_merge = mm(d_lifted, deeper, NT)
    d_deep = mm(dz_deep, coarse, NT)
    d_fine = twice(mm(dz_ref[...], l2[...], NT))
    low32 = lax.broadcasted_iota(jnp.int32, (32, GY), 1) < C1
    base = 27 + 32 + 27 * C1
    pack[base : base + C2, :] = d_deep
    base = base + C2
    pair[...] = d_fine
    fine_even_odd = [pair[pl.ds(i, 32, stride=2), :] for i in range(2)]
    pair[...] = d_coarse_merge
    coarse_even_odd = [pair[pl.ds(i, 32, stride=2), :] for i in range(2)]
    turn = pltpu.roll(coarse_even_odd[0], C1, 1)
    pack[pl.ds(base, 32, stride=3), :] = jnp.where(low32, fine_even_odd[0], turn)
    pack[pl.ds(base + 1, 32, stride=3), :] = jnp.where(low32, turn, fine_even_odd[1])
    pack[pl.ds(base + 2, 32, stride=3), :] = coarse_even_odd[1]
    base = base + 96
    column = jnp.sum(d_out, axis=1, keepdims=True)
    across_ = lane64 == lax.broadcasted_iota(jnp.int32, (C1, GY), 0)
    pack[base : base + 1, :] = jnp.sum(
        jnp.where(across_, jnp.broadcast_to(column, (C1, GY)), 0.0), axis=0, keepdims=True
    )
    pack[base + 1 : GROWS, :] = jnp.zeros((GROWS - base - 1, GY), F32)


    for h in range(n_hi - top, n_hi):
        emit(h)
    swap_join = swap(0, top, 1)

    blank = jnp.zeros((C2, GY), BF16)
    for dz in range(3):
        for dx in range(3):
            j = dz * 3 + dx
            for z in range(hz):
                for x in range(hx):
                    sz, sx = z - (dz - 1), x - (dx - 1)
                    inside = 0 <= sz < hz and 0 <= sx < hx
                    b = z * hx + x
                    colsz[j * C2 : (j + 1) * C2, b * GY : (b + 1) * GY] = (
                        block(dz_down, sz * hx + sx) if inside else blank
                    )
    early = chip_sum(tail, n_hi - tail, swap_down, 0)
    d_shifted = mm(wback[...], colsz[...])
    d_pooled = []
    for b in range(hz * hx):
        whole = block(d_shifted, b)
        total = whole[C1 : 2 * C1]
        total = total + jnp.where(lane64 == GY - 1, 0.0, pltpu.roll(whole[0:C1], GY - 1, 1))
        total = total + jnp.where(lane64 == 0, 0.0, pltpu.roll(whole[2 * C1 : 3 * C1], 1, 1))
        d_pooled.append(rounded(total) * 0.25)

    early += chip_sum(0, top, swap_join, 1)
    lift_t = w_lift_t[...]
    d_stem = jnp.zeros((C1, C1), F32)
    for z in range(PZ):
        here = slice(z * plane, (z + 1) * plane)
        spread = jnp.concatenate([d_pooled[(z // 2) * hx + x // 2] for x in range(PX)], axis=1)
        dz = ((rounded(mm(fine_t, dz_ref[:, here])) + spread) * g2[:, here]).astype(BF16)
        dz2_ref[:, here] = dz
        d_one = rounded(mm(lift_t, dz))
        dz = (d_one * g1[:, here]).astype(BF16)
        d_stem = d_stem + mm(dz, cols[:, here], NT)

    d_lift = twice(mm(dz2_ref[...], l1[...], NT))

    pair[:, 0:C1] = d_stem
    pair[:, C1:GY] = jnp.zeros((C1, GY - C1), F32)
    turned = pair[...]
    source = lax.broadcasted_iota(jnp.int32, (C1, GY), 0)
    for bit in range(6):
        moved = pltpu.roll(turned, (taps << bit) % GY, 1)
        turned = jnp.where((source >> bit) % 2 == 1, moved, turned)
    begin = source * taps
    wraps = lane64 < begin % GY
    stay = jnp.where(wraps, 0.0, turned).astype(BF16)
    over = jnp.where(wraps, turned, 0.0).astype(BF16)
    target_row = lax.broadcasted_iota(jnp.int32, (32, C1), 0)
    owner = lax.broadcasted_iota(jnp.int32, (32, C1), 1) * taps // GY
    stem_rows = mm((target_row == owner).astype(BF16), stay)
    stem_rows = stem_rows + mm((target_row == owner + 1).astype(BF16), over)
    pack[0:27, :] = stem_rows[0:27, :]

    low32 = lax.broadcasted_iota(jnp.int32, (32, GY), 1) < C1
    pair[...] = d_lift
    pack[27 : 27 + 32, :] = jnp.where(low32, pair[pl.ds(0, 32, stride=2), :], pair[pl.ds(1, 32, stride=2), :])


    for h in range(first):
        emit(h)
    late = []
    for d in range(1, n_lo):
        peer, device = in_line(d)
        late.append(
            send(
                grads.at[lax.rem(peer, 2), lax.div(peer, 2), pl.ds(top, first)],
                buf_late.at[d - 1],
                s5.at[d - 1],
                r5.at[d - 1],
                device,
            )
        )

    for copy in early:
        copy.wait_recv()
    for h in range(first, n_hi):
        at = (h + top) % n_hi
        value = half_ref[y, at].astype(F32)
        for d in range(n_y - 1):
            value = value + buf1[d, at].astype(F32)
        acc[h] = value.astype(BF16)
    for copy in late:
        copy.wait_recv()
    for h in range(first):
        value = grads[core, y, h + top].astype(F32)
        for d in range(n_lo - 1):
            value = value + buf_late[d, h].astype(F32)
        acc[h] = value.astype(BF16)
    partials = []
    ring = 8
    far_first = sorted(range(1, n_hi + 1), key=lambda e: (e == n_hi, -min(e % ring, ring - e % ring)))
    for e in far_first:
        h = lax.rem(hi + e, n_hi)
        for q in range(n_sec):
            if e == n_hi and q == 0:
                buf2[mine] = acc[h]
                continue
            owner = lax.rem(sec + q, n_sec)
            partials.append(
                send(
                    acc.at[h],
                    buf2.at[mine],
                    s2.at[q * n_hi + e - 1],
                    r2.at[q * n_hi + e - 1],
                    (owner, h * n_lo + lo),
                )
            )

    for copy in packets:
        copy.wait_recv()
    rows = PZ * PX

    def route(q, carry):
        wanted = (hi * (2 * n_lo) + q).astype(F32)
        value = jnp.zeros((rows, GY), F32)
        for src in range(n_hi):
            named = pbuf[src, rows : rows + 16, :].astype(F32)
            named = jnp.concatenate([named] * (rows // 16), axis=0)
            value = value + jnp.where(named == wanted, pbuf[src, 0:rows, :].astype(F32), 0.0)
        q_ref[q] = value.astype(BF16)
        return carry

    lax.fori_loop(0, 2 * n_lo, route, 0)
    routed = []
    for d in range(1, n_lo):
        peer, device = in_line(d)
        routed.append(send(q_ref.at[pl.ds(2 * peer, 2)], qbuf.at[d - 1], s4.at[d - 1], r4.at[d - 1], device))

    for copy in routed:
        copy.wait_recv()
    for s in range(2):
        value = q_ref[2 * lo + s].astype(F32)
        for d in range(n_lo - 1):
            value = value + qbuf[d, s].astype(F32)
        pred_out[s] = value

    for copy in partials:
        copy.wait_recv()
    for copy in [swap_down, swap_join] + packets + early + late + routed + partials:
        copy.wait_send()


def train(scale, n_sec, n_hi, n_lo, slot, patch, weights):
    cells = PZ * PX * GY
    small = cells // 4
    per = GROWS // (n_lo * n_hi)
    across = n_sec * n_hi
    n_y = n_lo // 2
    first = -(-(27 + 32) // (per * n_lo))
    dma = pltpu.SemaphoreType.DMA
    return pl.pallas_call(
        functools.partial(train_kernel, scale, n_sec, n_hi, n_lo),
        out_shape=(
            jax.ShapeDtypeStruct((2, PZ * PX, GY), F32),
            jax.ShapeDtypeStruct((across, per, GY), BF16),
        ),
        in_specs=[VMEM] * 14,
        out_specs=(VMEM, VMEM),
        scratch_shapes=[
            pltpu.VMEM((PZ * PX * C1, GY), F32),
            pltpu.VMEM((C1, cells), BF16),
            pltpu.VMEM((C1, cells), BF16),
            pltpu.VMEM((C1, cells), BF16),
            pltpu.VMEM((C1, cells), F32),
            pltpu.VMEM((C1, cells), F32),
            pltpu.VMEM((C1, cells), BF16),
            pltpu.VMEM((C1, cells), BF16),
            pltpu.VMEM((10 * C1, small), BF16),
            pltpu.VMEM((9 * C2, small), BF16),
            pltpu.VMEM((GROWS, GY), F32),
            pltpu.VMEM((C1, GY), F32),
            pltpu.VMEM((2, n_y, n_hi, per, GY), BF16),
            pltpu.VMEM((PZ * PX + 16, GY), BF16),
            pltpu.VMEM((n_y, n_hi, per, GY), BF16),
            pltpu.VMEM((n_y, n_hi, per, GY), BF16),
            pltpu.VMEM((n_y - 1, n_hi, per, GY), BF16),
            pltpu.VMEM((n_lo - 1, first, per, GY), BF16),
            pltpu.VMEM((n_hi, per, GY), BF16),
            pltpu.VMEM((n_hi, PZ * PX + 16, GY), BF16),
            pltpu.VMEM((2 * n_lo, PZ * PX, GY), BF16),
            pltpu.VMEM((n_lo - 1, 2, PZ * PX, GY), BF16),
            dma((2, n_y - 1)),
            dma((2, n_y - 1)),
            dma((2,)),
            dma((2,)),
            dma((n_lo - 1,)),
            dma((n_lo - 1,)),
            dma((across,)),
            dma((across,)),
            dma((n_hi - 1,)),
            dma((n_hi - 1,)),
            dma((n_lo - 1,)),
            dma((n_lo - 1,)),
        ],
        compiler_params=pltpu.CompilerParams(
            collective_id=1, has_side_effects=True, vmem_limit_bytes=32 * 2**20
        ),
        name="train",
    )(slot, patch, *weights)


def finish_kernel(heat_in, pred_in, grad_in, heat_out, pred_out, grad_out, done):
    copy = pltpu.make_async_copy(heat_in, heat_out, done)
    copy.start()
    total = grad_in[0].astype(F32)
    for t in range(1, grad_in.shape[0]):
        total = total + grad_in[t].astype(F32)
    grad_out[...] = total
    for s in range(2):
        for z in range(PZ):
            pred_out[s, z] = pred_in[s, z * PX : (z + 1) * PX, :].astype(BF16)
    copy.wait()


def finish(heat, preds, partials):
    return pl.pallas_call(
        finish_kernel,
        out_shape=(
            jax.ShapeDtypeStruct(heat.shape, F32),
            jax.ShapeDtypeStruct((2, PZ, PX, GY), BF16),
            jax.ShapeDtypeStruct(partials.shape[1:], F32),
        ),
        in_specs=[pl.BlockSpec(memory_space=pl.ANY), VMEM, VMEM],
        out_specs=(HBM, VMEM, VMEM),
        scratch_shapes=[pltpu.SemaphoreType.DMA],
        compiler_params=pltpu.CompilerParams(vmem_limit_bytes=8 * 2**20),
        name="finish",
    )(heat, preds, partials)


def local(
    n_sec,
    n_dp,
    heat_start,
    conductivity,
    patch_z,
    patch_x,
    slot_table,
    w_stem,
    w_lift,
    w_down,
    w_deep,
    w_merge,
    w_out,
):
    n_lo = LINE
    n_hi = n_dp // n_lo
    weights = (w_stem.T, w_lift, w_down.T, w_deep, w_merge, w_out)
    heat_two, patch, *ready, slot = heat_steps(
        n_sec, n_dp, heat_start, conductivity, patch_z, patch_x, slot_table, weights
    )
    scale = 1.0 / (n_sec * n_dp * PZ * PX * GY)
    preds, partials = train(scale, n_sec, n_hi, n_lo, slot, patch, ready)
    return finish(heat_two, preds, partials)


def solution(mesh):
    n_sec, n_dp = mesh.shape["section"], mesh.shape["dp"]
    both = ("section", "dp")
    return jax.shard_map(
        functools.partial(local, n_sec, n_dp),
        mesh=mesh,
        in_specs=(P(both, None, None), P(both, None, None), P(both), P(both), P(both)) + (P(),) * 6,
        out_specs=(P(both, None, None), P(both, None, None, None), P("dp", None)),
        check_vma=False,
    )
```

```python
import functools

import jax
import jax.numpy as jnp
from jax import lax
from jax.experimental import pallas as pl
from jax.experimental.pallas import tpu as pltpu
from jax.sharding import PartitionSpec as P

MESH = pl.DeviceIdType.MESH
TIME_STEP = 0.15
GY = 128
PZ = 4
PX = 8
C1 = 64
C2 = 128
GROWS = 2048
LINE = 8
F32 = jnp.float32
BF16 = jnp.bfloat16
VMEM = pl.BlockSpec(memory_space=pltpu.VMEM)
SMEM = pl.BlockSpec(memory_space=pltpu.SMEM)
HBM = pl.BlockSpec(memory_space=pltpu.HBM)


def rounded(x):
    return x.astype(BF16).astype(F32)


NT = (((1,), (1,)), ((), ()))
NN = (((1,), (0,)), ((), ()))


def mm(a, b, dims=NN):
    return lax.dot_general(a, b, dims, preferred_element_type=F32)


def heat_kernel(
    n_sec,
    n_dp,
    pz_ref,
    px_ref,
    slot_ref,
    u_hbm,
    k_hbm,
    stem_hbm,
    lift_hbm,
    down_hbm,
    deep_hbm,
    merge_hbm,
    proj_hbm,
    out_ref,
    patch_ref,
    stem_ref,
    lift_ref,
    lift_t,
    down_ref,
    down_back,
    deep_ref,
    deep_t,
    fine_ref,
    fine_t,
    coarse_ref,
    coarse_t,
    proj_col,
    slot_tile,
    v_stem,
    v_down,
    v_merge,
    v_proj,
    u_ref,
    k_ref,
    ulo,
    klo,
    uhi,
    khi,
    h1,
    load,
    send,
    recv,
):
    total = n_sec * n_dp
    depth = u_ref.shape[0]
    me = lax.axis_index("section") * n_dp + lax.axis_index("dp")
    after = lax.rem(me + 1, total)
    before = lax.rem(me + total - 1, total)

    def place(i):
        return (lax.div(i, n_dp), lax.rem(i, n_dp))

    barrier = pltpu.get_barrier_semaphore()
    below, above = me > 0, me < total - 1

    @pl.when(below)
    def _():
        pl.semaphore_signal(barrier, inc=1, device_id=place(before), device_id_type=MESH)

    @pl.when(above)
    def _():
        pl.semaphore_signal(barrier, inc=1, device_id=place(after), device_id_type=MESH)

    loads = [
        pltpu.make_async_copy(u_hbm, u_ref, load.at[0]),
        pltpu.make_async_copy(k_hbm, k_ref, load.at[1]),
        pltpu.make_async_copy(down_hbm, v_down, load.at[2]),
        pltpu.make_async_copy(stem_hbm, v_stem, load.at[3]),
        pltpu.make_async_copy(lift_hbm, lift_ref, load.at[4]),
        pltpu.make_async_copy(deep_hbm, deep_ref, load.at[5]),
        pltpu.make_async_copy(merge_hbm, v_merge, load.at[6]),
        pltpu.make_async_copy(proj_hbm, v_proj, load.at[7]),
    ]
    for copy in loads:
        copy.start()
    inner_slab = jnp.logical_and(below, above)

    @pl.when(inner_slab)
    def _():
        pl.semaphore_wait(barrier, 2)

    @pl.when(jnp.logical_not(inner_slab))
    def _():
        pl.semaphore_wait(barrier, 1)

    plan = (
        (u_hbm.at[pl.ds(depth - 2, 2)], ulo, after),
        (k_hbm.at[pl.ds(depth - 2, 2)], klo, after),
        (u_hbm.at[pl.ds(0, 2)], uhi, before),
        (k_hbm.at[pl.ds(0, 2)], khi, before),
    )
    copies = [
        pltpu.make_async_remote_copy(
            src_ref=src,
            dst_ref=dst,
            send_sem=send.at[i],
            recv_sem=recv.at[i],
            device_id=place(peer),
            device_id_type=MESH,
        )
        for i, (src, dst, peer) in enumerate(plan)
    ]
    upward, downward = copies[0:2], copies[2:4]

    @pl.when(above)
    def _():
        for copy in upward:
            copy.start()

    @pl.when(below)
    def _():
        for copy in downward:
            copy.start()

    @pl.when(me == 0)
    def _():
        ulo[...] = jnp.zeros_like(ulo)
        klo[...] = jnp.zeros_like(klo)

    @pl.when(me == total - 1)
    def _():
        uhi[...] = jnp.zeros_like(uhi)
        khi[...] = jnp.zeros_like(khi)

    rows, lanes = u_ref.shape[1:]
    row = lax.broadcasted_iota(jnp.int32, (rows, lanes), 0)
    lane = lax.broadcasted_iota(jnp.int32, (rows, lanes), 1)

    def step(up, uc, un, kp, kc, kn):
        flux = (kc + kn) * (un - uc) + (kc + kp) * (up - uc)
        for axis, place_, size in ((0, row, rows), (1, lane, lanes)):
            last = place_ == size - 1
            first = place_ == 0
            u_next = jnp.where(last, 0.0, pltpu.roll(uc, size - 1, axis))
            k_next = jnp.where(last, 0.0, pltpu.roll(kc, size - 1, axis))
            face = (kc + k_next) * (u_next - uc)
            back = jnp.where(first, kc * uc, pltpu.roll(face, 1, axis))
            flux = flux + (face - back)
        return uc + (0.5 * TIME_STEP) * flux

    for copy in loads:
        copy.wait()
    group = 7

    def interior(i, carry):
        for j in range(group):
            z = 1 + i * group + j
            h1[z + 1] = step(
                u_ref[z - 1], u_ref[z], u_ref[z + 1], k_ref[z - 1], k_ref[z], k_ref[z + 1]
            )
        return carry

    lax.fori_loop(0, (depth - 2) // group, interior, 0)

    def second(z):
        out_ref[z] = step(h1[z], h1[z + 1], h1[z + 2], k_ref[z - 1], k_ref[z], k_ref[z + 1])

    pack = 6

    def inner(i, carry):
        for j in range(pack):
            second(2 + i * pack + j)
        return carry

    lax.fori_loop(0, (depth - 4) // pack, inner, 0)
    unit = lax.broadcasted_iota(jnp.int32, (C2, C2), 0) == lax.broadcasted_iota(jnp.int32, (C2, C2), 1)
    eye = unit[0:C1, 0:C1]
    unit = unit.astype(BF16)
    stem_ref[...] = mm(unit[0:C1, 0:C1], v_stem[...], NT).astype(BF16)
    for dy in range(3):
        starts = [(j * 3 + dy) * C1 for j in range(9)]
        part = jnp.concatenate([v_down[r : r + C1, :] for r in starts], axis=0)
        down_ref[dy * C2 : (dy + 1) * C2, :] = mm(unit, part, NT).astype(BF16)
    for j in range(9):
        down_back[:, j * C2 : (j + 1) * C2] = v_down[j * 3 * C1 : (j + 1) * 3 * C1, :]

    def turned(x):
        return x.astype(F32).T.astype(BF16)

    lift_t[...] = turned(lift_ref[...])
    slot_tile[...] = jnp.full((16, GY), slot_ref[0].astype(F32)).astype(BF16)
    deep_t[...] = turned(deep_ref[...])
    fine = v_merge[:, 0:C1]
    coarse = v_merge[:, C1 : C1 + C2]
    fine_ref[...] = fine
    fine_t[...] = turned(fine)
    coarse_ref[...] = coarse
    coarse_t[...] = turned(coarse)
    row64 = v_proj[...].astype(F32)
    column = jnp.sum(jnp.where(eye, jnp.broadcast_to(row64, (C1, C1)), 0.0), axis=1, keepdims=True)
    proj_col[...] = jnp.broadcast_to(column, proj_col.shape)

    @pl.when(below)
    def _():
        for copy in upward:
            copy.wait_recv()

    @pl.when(above)
    def _():
        for copy in downward:
            copy.wait_recv()

    has_lo = (me > 0).astype(F32)
    has_hi = (me < total - 1).astype(F32)
    ul, kl, uh, kh = ulo, klo, uhi, khi
    end = depth - 1
    h1[0] = has_lo * step(ul[0], ul[1], u_ref[0], kl[0], kl[1], k_ref[0])
    h1[1] = step(ul[1], u_ref[0], u_ref[1], kl[1], k_ref[0], k_ref[1])
    h1[depth] = step(u_ref[end - 1], u_ref[end], uh[0], k_ref[end - 1], k_ref[end], kh[0])
    h1[depth + 1] = has_hi * step(u_ref[end], uh[0], uh[1], k_ref[end], kh[0], kh[1])

    out_ref[0] = step(h1[0], h1[1], h1[2], kl[1], k_ref[0], k_ref[1])
    out_ref[end] = step(h1[end], h1[depth], h1[depth + 1], k_ref[end - 1], k_ref[end], kh[0])
    second(1)
    second(end - 1)
    pz = pz_ref[0]
    px = px_ref[0]
    for z in range(PZ):
        patch_ref[0, z] = h1[1 + pz + z, pl.ds(px, PX), :]
        patch_ref[1, z] = k_ref[pz + z, pl.ds(px, PX), :]
        patch_ref[2, z] = out_ref[pz + z, pl.ds(px, PX), :]

    @pl.when(above)
    def _():
        for copy in upward:
            copy.wait_send()

    @pl.when(below)
    def _():
        for copy in downward:
            copy.wait_send()


def heat_steps(n_sec, n_dp, heat, cond, patch_z, patch_x, slot, weights):
    layers = (2,) + heat.shape[1:]
    operands = (heat, cond, *weights)
    operands = [pltpu.with_memory_space_constraint(x, pltpu.HBM) for x in operands]
    taps = weights[0].shape[0]
    return pl.pallas_call(
        functools.partial(heat_kernel, n_sec, n_dp),
        out_shape=(
            jax.ShapeDtypeStruct(heat.shape, F32),
            jax.ShapeDtypeStruct((3, PZ, PX, GY), F32),
            jax.ShapeDtypeStruct((C1, taps), BF16),
            jax.ShapeDtypeStruct((C1, C1), BF16),
            jax.ShapeDtypeStruct((C1, C1), BF16),
            jax.ShapeDtypeStruct((3 * C2, 9 * C1), BF16),
            jax.ShapeDtypeStruct((3 * C1, 9 * C2), BF16),
            jax.ShapeDtypeStruct((C2, C2), BF16),
            jax.ShapeDtypeStruct((C2, C2), BF16),
            jax.ShapeDtypeStruct((C1, C1), BF16),
            jax.ShapeDtypeStruct((C1, C1), BF16),
            jax.ShapeDtypeStruct((C1, C2), BF16),
            jax.ShapeDtypeStruct((C2, C1), BF16),
            jax.ShapeDtypeStruct((C1, GY), F32),
            jax.ShapeDtypeStruct((16, GY), BF16),
        ),
        in_specs=[SMEM] * 3 + [HBM] * 8,
        out_specs=(VMEM,) * 15,
        scratch_shapes=[
            pltpu.VMEM(weights[0].shape, BF16),
            pltpu.VMEM(weights[2].shape, BF16),
            pltpu.VMEM(weights[4].shape, BF16),
            pltpu.VMEM(weights[5].shape, BF16),
            pltpu.VMEM(heat.shape, F32),
            pltpu.VMEM(heat.shape, F32),
            pltpu.VMEM(layers, F32),
            pltpu.VMEM(layers, F32),
            pltpu.VMEM(layers, F32),
            pltpu.VMEM(layers, F32),
            pltpu.VMEM((heat.shape[0] + 2,) + heat.shape[1:], F32),
            pltpu.SemaphoreType.DMA((8,)),
            pltpu.SemaphoreType.DMA((4,)),
            pltpu.SemaphoreType.DMA((4,)),
        ],
        compiler_params=pltpu.CompilerParams(
            collective_id=0, has_side_effects=True, vmem_limit_bytes=16 * 2**20
        ),
        name="heat",
    )(patch_z, patch_x, slot, *operands)


def silu_and_slope(z):
    s = 0.5 * jnp.tanh(0.5 * z) + 0.5
    value = z * s
    return value, s + value * (1.0 - s)


def block(x, b):
    return x[:, b * GY : (b + 1) * GY]


def train_kernel(
    scale,
    n_sec,
    n_hi,
    n_lo,
    slot_tile,
    patch_ref,
    w_stem,
    w_lift,
    w_lift_t,
    w_down,
    wback,
    w_deep,
    w_deep_t,
    w_fine,
    w_fine_t,
    w_coarse,
    w_coarse_t,
    w_proj_col,
    pred_out,
    buf2,
    tall,
    cols,
    l1,
    l2,
    g1,
    g2,
    dz_ref,
    dz2_ref,
    colsd,
    colsz,
    pack,
    pair,
    grads,
    packet,
    cbuf,
    half_ref,
    buf1,
    buf_late,
    acc,
    pbuf,
    q_ref,
    qbuf,
    s1,
    r1,
    sc,
    rc,
    s5,
    r5,
    s2,
    r2,
    s3,
    r3,
    s4,
    r4,
):
    sec = lax.axis_index("section")
    dp = lax.axis_index("dp")
    hi = lax.div(dp, n_lo)
    lo = lax.rem(dp, n_lo)
    across = n_sec * n_hi
    mine = sec * n_hi + hi
    n_y = n_lo // 2
    core = lax.rem(lo, 2)
    other = 1 - core
    y = lax.div(lo, 2)

    def in_line(d):
        peer = lax.rem(lo + d, n_lo)
        return peer, (sec, hi * n_lo + peer)

    def in_y(d):
        peer = lax.rem(y + d, n_y)
        return peer, (sec, hi * n_lo + 2 * peer + core)

    def in_column(d):
        peer = lax.rem(mine + d, across)
        return peer, (lax.div(peer, n_hi), lax.rem(peer, n_hi) * n_lo + lo)

    def in_part(d):
        peer = lax.rem(hi + d, n_hi)
        return peer, (sec, peer * n_lo + lo)

    def send(src, dst, ssem, rsem, device):
        copy = pltpu.make_async_remote_copy(
            src_ref=src, dst_ref=dst, send_sem=ssem, recv_sem=rsem, device_id=device, device_id_type=MESH
        )
        copy.start()
        return copy

    def group(like, ssem, rsem, device):
        return pltpu.make_async_remote_copy(
            src_ref=like, dst_ref=like, send_sem=ssem, recv_sem=rsem, device_id=device, device_id_type=MESH
        )

    barrier = pltpu.get_barrier_semaphore()
    for d in range(1, across):
        pl.semaphore_signal(barrier, inc=1, device_id=in_column(d)[1], device_id_type=MESH)
    for d in range(1, n_lo):
        pl.semaphore_signal(barrier, inc=1, device_id=in_line(d)[1], device_id_type=MESH)

    plane = PX * GY
    cells = PZ * plane
    small = cells // 4
    row8 = lax.broadcasted_iota(jnp.int32, (PX, GY), 0)
    lane8 = lax.broadcasted_iota(jnp.int32, (PX, GY), 1)
    lane64 = lax.broadcasted_iota(jnp.int32, (C1, GY), 1)

    tall[...] = jnp.zeros_like(tall)
    for channel in range(2):
        for dx in range(3):
            for dy in range(3):
                shifted = []
                for z in range(PZ):
                    v = rounded(patch_ref[channel, z])
                    if dx == 0:
                        v = jnp.where(row8 == 0, 0.0, pltpu.roll(v, 1, 0))
                    elif dx == 2:
                        v = jnp.where(row8 == PX - 1, 0.0, pltpu.roll(v, PX - 1, 0))
                    if dy == 0:
                        v = jnp.where(lane8 == 0, 0.0, pltpu.roll(v, 1, 1))
                    elif dy == 2:
                        v = jnp.where(lane8 == GY - 1, 0.0, pltpu.roll(v, GY - 1, 1))
                    shifted.append(v)
                for dz in range(3):
                    r = ((dz * 3 + dx) * 3 + dy) * 2 + channel
                    for z in range(PZ):
                        if 0 <= z + dz - 1 < PZ:
                            tall[pl.ds(z * PX * C1 + r, PX, stride=C1), :] = shifted[z + dz - 1]
    for b in range(PZ * PX):
        cols[:, b * GY : (b + 1) * GY] = tall[b * C1 : (b + 1) * C1, :].astype(BF16)

    taps = w_stem.shape[1]
    stem = w_stem[...]
    lift = w_lift[...]
    pooled = []
    for zz in range(PZ // 2):
        rows = []
        for z in (2 * zz, 2 * zz + 1):
            here = slice(z * plane, (z + 1) * plane)
            value, slope = silu_and_slope(mm(stem, cols[0:taps, here]))
            g1[:, here] = slope
            one = value.astype(BF16)
            l1[:, here] = one
            value, slope = silu_and_slope(mm(lift, one))
            g2[:, here] = slope
            two = value.astype(BF16)
            l2[:, here] = two
            rows.append(two.astype(F32))
        both = rows[0] + rows[1]
        for xx in range(PX // 2):
            pooled.append(rounded((block(both, 2 * xx) + block(both, 2 * xx + 1)) * 0.25))

    hz, hx = PZ // 2, PX // 2
    nothing = jnp.zeros((C1, GY), BF16)
    pooled = [v.astype(BF16) for v in pooled]
    for dz in range(3):
        for dx in range(3):
            r = (dz * 3 + dx) * C1
            for z in range(hz):
                for x in range(hx):
                    sz, sx = z + dz - 1, x + dx - 1
                    inside = 0 <= sz < hz and 0 <= sx < hx
                    b = z * hx + x
                    colsd[r : r + C1, b * GY : (b + 1) * GY] = pooled[sz * hx + sx] if inside else nothing
    depth = 9 * C1
    colsd[depth : depth + C1, :] = jnp.zeros((C1, small), BF16)
    products = mm(w_down[...], colsd[0:depth, :])
    lane128 = lax.broadcasted_iota(jnp.int32, (C2, GY), 1)

    def later(v):
        return jnp.where(lane128 == 0, 0.0, pltpu.roll(v, 1, 1))

    def sooner(v):
        return jnp.where(lane128 == GY - 1, 0.0, pltpu.roll(v, GY - 1, 1))

    summed = []
    for b in range(hz * hx):
        v = block(products, b)
        summed.append(later(v[0:C2]) + v[C2 : 2 * C2] + sooner(v[2 * C2 : 3 * C2]))
    value, slope_down = silu_and_slope(jnp.concatenate(summed, axis=1))
    coarse = value.astype(BF16)
    value, slope_deep = silu_and_slope(mm(w_deep[...], coarse))
    deeper = value.astype(BF16)
    merge_fine = w_fine[...]
    lifted = mm(w_coarse[...], deeper)

    out_col = w_proj_col[...]
    fine_t = w_fine_t[...]
    d_out = jnp.zeros((C1, GY), F32)
    gathered = [None] * (hz * hx)
    forecast = []
    for z in range(PZ):
        here = slice(z * plane, (z + 1) * plane)
        two = l2[:, here]
        added = [block(lifted, (z // 2) * hx + x // 2) for x in range(PX)]
        value, slope = silu_and_slope(mm(merge_fine, two) + jnp.concatenate(added, axis=1))
        merged = value.astype(BF16)
        held = merged.astype(F32)
        predicted = jnp.zeros((PX, GY), F32)
        for x in range(PX):
            summed = jnp.sum(block(held, x) * out_col, axis=0, keepdims=True)
            predicted = jnp.where(row8 == x, summed, predicted)
        forecast.append(predicted)
        misfit = (predicted - rounded(patch_ref[2, z])) * scale
        for x in range(PX):
            d_out = d_out + block(held, x) * misfit[x : x + 1, :]
        d_merged = jnp.concatenate([out_col * misfit[x : x + 1, :] for x in range(PX)], axis=1)
        dz = rounded(d_merged) * slope
        for x in range(PX):
            b = (z // 2) * hx + x // 2
            gathered[b] = block(dz, x) if gathered[b] is None else gathered[b] + block(dz, x)
        dz = dz.astype(BF16)
        dz_ref[:, here] = dz

    half = PZ * PX // 2
    packet[0:half, :] = jnp.concatenate(forecast[0 : PZ // 2], axis=0).astype(BF16)
    packet[half : 2 * half, :] = jnp.concatenate(forecast[PZ // 2 : PZ], axis=0).astype(BF16)
    packet[2 * half : 2 * half + 16, :] = slot_tile[...]
    pl.semaphore_wait(barrier, n_lo - 1 + across - 1)
    for d in range(1, n_hi):
        peer, device = in_part(d)
        send(packet, pbuf.at[d], s3, r3, device)
    packets = group(pbuf.at[pl.ds(1, n_hi - 1)], s3, r3, device)
    pbuf[0] = packet[...]

    d_lifted = jnp.concatenate(gathered, axis=1).astype(BF16)
    d_deeper = mm(w_coarse_t[...], d_lifted)
    dz_deep = (rounded(d_deeper) * slope_deep).astype(BF16)
    d_coarse = mm(w_deep_t[...], dz_deep)
    dz_down = (rounded(d_coarse) * slope_down).astype(BF16)

    r_ = lax.broadcasted_iota(jnp.int32, (C2, C2), 0)
    c_ = lax.broadcasted_iota(jnp.int32, (C2, C2), 1)
    parted = jnp.where(r_ < C1, 2 * r_, 2 * r_ - (C2 - 1)) == c_
    dz_parted = mm(parted.astype(BF16), dz_down)
    blocks = [block(dz_parted, b) for b in range(hz * hx)]
    dz_shifts = jnp.concatenate(
        [
            jnp.concatenate([f(v) for v in blocks], axis=1).astype(BF16)
            for f in (sooner, lambda v: v, later)
        ],
        axis=0,
    )
    d_down = mm(dz_shifts, colsd[...], NT)
    low = lane64 < C1
    turned_chunks = {}

    def piece(h, lanes_low):
        odd, h = divmod(h, 27)
        zx, dy = divmod(h, 3)
        q, high = divmod(zx, 2)
        r = dy * C2 + odd * C1
        chunk = d_down[r : r + C1, q * GY : (q + 1) * GY]
        if bool(high) != lanes_low:
            return chunk
        if (r, q) not in turned_chunks:
            turned_chunks[r, q] = pltpu.roll(chunk, C1, 1)
        return turned_chunks[r, q]

    base = 27 + 32
    for j in range(27):
        pack[pl.ds(base + j, C1, stride=27), :] = jnp.where(
            low, piece(2 * j, True), piece(2 * j + 1, False)
        )

    per = grads.shape[3]
    first = -(-(27 + 32) // (per * n_lo))
    top = n_hi - (27 + 32 + 27 * C1) // (per * n_lo)
    tail = first + top

    def emit(hi_):
        for lo_ in range(n_lo):
            start = (hi_ * n_lo + lo_) * per
            grads[lo_ % 2, lo_ // 2, (hi_ + top) % n_hi] = pack[start : start + per, :].astype(BF16)

    for h in range(first, n_hi - top):
        emit(h)

    def swap(begin, count, i):
        return send(
            grads.at[other, :, pl.ds(begin, count)],
            cbuf.at[:, pl.ds(begin, count)],
            sc.at[i],
            rc.at[i],
            (sec, hi * n_lo + 2 * y + other),
        )

    def chip_sum(begin, count, copy, i):
        copy.wait_recv()
        part = slice(begin, begin + count)
        for y_ in range(n_y):
            total = grads[core, y_, part].astype(F32) + cbuf[y_, part].astype(F32)
            half_ref[y_, part] = total.astype(BF16)
        for d in range(1, n_y):
            peer, device = in_y(d)
            send(
                half_ref.at[peer, pl.ds(begin, count)],
                buf1.at[d - 1, pl.ds(begin, count)],
                s1.at[i],
                r1.at[i],
                device,
            )
        return group(buf1.at[:, pl.ds(begin, count)], s1.at[i], r1.at[i], device)

    swap_down = swap(tail, n_hi - tail, 0)

    def twice(x):
        pair[:, 0:C1] = x
        pair[:, C1:GY] = jnp.zeros((C1, GY - C1), F32)
        once = pair[...]
        return once + pltpu.roll(once, C1, 1)

    d_coarse_merge = mm(d_lifted, deeper, NT)
    d_deep = mm(dz_deep, coarse, NT)
    d_fine = twice(mm(dz_ref[...], l2[...], NT))
    low32 = lax.broadcasted_iota(jnp.int32, (32, GY), 1) < C1
    base = 27 + 32 + 27 * C1
    pack[base : base + C2, :] = d_deep
    base = base + C2
    pair[...] = d_fine
    fine_even_odd = [pair[pl.ds(i, 32, stride=2), :] for i in range(2)]
    pair[...] = d_coarse_merge
    coarse_even_odd = [pair[pl.ds(i, 32, stride=2), :] for i in range(2)]
    turn = pltpu.roll(coarse_even_odd[0], C1, 1)
    pack[pl.ds(base, 32, stride=3), :] = jnp.where(low32, fine_even_odd[0], turn)
    pack[pl.ds(base + 1, 32, stride=3), :] = jnp.where(low32, turn, fine_even_odd[1])
    pack[pl.ds(base + 2, 32, stride=3), :] = coarse_even_odd[1]
    base = base + 96
    column = jnp.sum(d_out, axis=1, keepdims=True)
    across_ = lane64 == lax.broadcasted_iota(jnp.int32, (C1, GY), 0)
    pack[base : base + 1, :] = jnp.sum(
        jnp.where(across_, jnp.broadcast_to(column, (C1, GY)), 0.0), axis=0, keepdims=True
    )
    pack[base + 1 : GROWS, :] = jnp.zeros((GROWS - base - 1, GY), F32)


    for h in range(n_hi - top, n_hi):
        emit(h)
    swap_join = swap(0, top, 1)

    blank = jnp.zeros((C2, GY), BF16)
    for dz in range(3):
        for dx in range(3):
            j = dz * 3 + dx
            for z in range(hz):
                for x in range(hx):
                    sz, sx = z - (dz - 1), x - (dx - 1)
                    inside = 0 <= sz < hz and 0 <= sx < hx
                    b = z * hx + x
                    colsz[j * C2 : (j + 1) * C2, b * GY : (b + 1) * GY] = (
                        block(dz_down, sz * hx + sx) if inside else blank
                    )
    early_down = chip_sum(tail, n_hi - tail, swap_down, 0)
    d_shifted = mm(wback[...], colsz[...])
    d_pooled = []
    for b in range(hz * hx):
        whole = block(d_shifted, b)
        total = whole[C1 : 2 * C1]
        total = total + jnp.where(lane64 == GY - 1, 0.0, pltpu.roll(whole[0:C1], GY - 1, 1))
        total = total + jnp.where(lane64 == 0, 0.0, pltpu.roll(whole[2 * C1 : 3 * C1], 1, 1))
        d_pooled.append(rounded(total) * 0.25)

    early_join = chip_sum(0, top, swap_join, 1)
    lift_t = w_lift_t[...]
    d_stem = jnp.zeros((C1, C1), F32)
    for z in range(PZ):
        here = slice(z * plane, (z + 1) * plane)
        spread = jnp.concatenate([d_pooled[(z // 2) * hx + x // 2] for x in range(PX)], axis=1)
        dz = ((rounded(mm(fine_t, dz_ref[:, here])) + spread) * g2[:, here]).astype(BF16)
        dz2_ref[:, here] = dz
        d_one = rounded(mm(lift_t, dz))
        dz = (d_one * g1[:, here]).astype(BF16)
        d_stem = d_stem + mm(dz, cols[:, here], NT)

    d_lift = twice(mm(dz2_ref[...], l1[...], NT))

    pair[:, 0:C1] = d_stem
    pair[:, C1:GY] = jnp.zeros((C1, GY - C1), F32)
    turned = pair[...]
    source = lax.broadcasted_iota(jnp.int32, (C1, GY), 0)
    for bit in range(6):
        moved = pltpu.roll(turned, (taps << bit) % GY, 1)
        turned = jnp.where((source >> bit) % 2 == 1, moved, turned)
    begin = source * taps
    wraps = lane64 < begin % GY
    stay = jnp.where(wraps, 0.0, turned).astype(BF16)
    over = jnp.where(wraps, turned, 0.0).astype(BF16)
    target_row = lax.broadcasted_iota(jnp.int32, (32, C1), 0)
    owner = lax.broadcasted_iota(jnp.int32, (32, C1), 1) * taps // GY
    stem_rows = mm((target_row == owner).astype(BF16), stay)
    stem_rows = stem_rows + mm((target_row == owner + 1).astype(BF16), over)
    pack[0:27, :] = stem_rows[0:27, :]

    low32 = lax.broadcasted_iota(jnp.int32, (32, GY), 1) < C1
    pair[...] = d_lift
    pack[27 : 27 + 32, :] = jnp.where(low32, pair[pl.ds(0, 32, stride=2), :], pair[pl.ds(1, 32, stride=2), :])


    for h in range(first):
        emit(h)
    for d in range(1, n_lo):
        peer, device = in_line(d)
        send(
            grads.at[lax.rem(peer, 2), lax.div(peer, 2), pl.ds(top, first)],
            buf_late.at[d - 1],
            s5,
            r5,
            device,
        )
    late = group(buf_late, s5, r5, device)

    for copy in (early_down, early_join):
        copy.wait_recv()
    for h in range(first, n_hi):
        at = (h + top) % n_hi
        value = half_ref[y, at].astype(F32)
        for d in range(n_y - 1):
            value = value + buf1[d, at].astype(F32)
        acc[h] = value.astype(BF16)
    late.wait_recv()
    for h in range(first):
        value = grads[core, y, h + top].astype(F32)
        for d in range(n_lo - 1):
            value = value + buf_late[d, h].astype(F32)
        acc[h] = value.astype(BF16)
    ring = 8
    far_first = sorted(range(1, n_hi + 1), key=lambda e: (e == n_hi, -min(e % ring, ring - e % ring)))
    for e in far_first:
        h = lax.rem(hi + e, n_hi)
        for q in range(n_sec):
            if e == n_hi and q == 0:
                buf2[mine] = acc[h]
                continue
            owner = lax.rem(sec + q, n_sec)
            device = (owner, h * n_lo + lo)
            send(acc.at[h], buf2.at[mine], s2, r2, device)
    partials = group(buf2.at[pl.ds(0, across - 1)], s2, r2, device)

    packets.wait_recv()
    rows = PZ * PX

    def route(q, carry):
        wanted = (hi * (2 * n_lo) + q).astype(F32)
        value = jnp.zeros((rows, GY), F32)
        for src in range(n_hi):
            named = pbuf[src, rows : rows + 16, :].astype(F32)
            named = jnp.concatenate([named] * (rows // 16), axis=0)
            value = value + jnp.where(named == wanted, pbuf[src, 0:rows, :].astype(F32), 0.0)
        q_ref[q] = value.astype(BF16)
        return carry

    lax.fori_loop(0, 2 * n_lo, route, 0)
    for d in range(1, n_lo):
        peer, device = in_line(d)
        send(q_ref.at[pl.ds(2 * peer, 2)], qbuf.at[d - 1], s4, r4, device)
    routed = group(qbuf, s4, r4, device)

    routed.wait_recv()
    for s in range(2):
        value = q_ref[2 * lo + s].astype(F32)
        for d in range(n_lo - 1):
            value = value + qbuf[d, s].astype(F32)
        pred_out[s] = value

    partials.wait_recv()
    for copy in (swap_down, swap_join, packets, early_down, early_join, late, routed, partials):
        copy.wait_send()


def train(scale, n_sec, n_hi, n_lo, slot, patch, weights):
    cells = PZ * PX * GY
    small = cells // 4
    per = GROWS // (n_lo * n_hi)
    across = n_sec * n_hi
    n_y = n_lo // 2
    first = -(-(27 + 32) // (per * n_lo))
    dma = pltpu.SemaphoreType.DMA
    return pl.pallas_call(
        functools.partial(train_kernel, scale, n_sec, n_hi, n_lo),
        out_shape=(
            jax.ShapeDtypeStruct((2, PZ * PX, GY), F32),
            jax.ShapeDtypeStruct((across, per, GY), BF16),
        ),
        in_specs=[VMEM] * 14,
        out_specs=(VMEM, VMEM),
        scratch_shapes=[
            pltpu.VMEM((PZ * PX * C1, GY), F32),
            pltpu.VMEM((C1, cells), BF16),
            pltpu.VMEM((C1, cells), BF16),
            pltpu.VMEM((C1, cells), BF16),
            pltpu.VMEM((C1, cells), F32),
            pltpu.VMEM((C1, cells), F32),
            pltpu.VMEM((C1, cells), BF16),
            pltpu.VMEM((C1, cells), BF16),
            pltpu.VMEM((10 * C1, small), BF16),
            pltpu.VMEM((9 * C2, small), BF16),
            pltpu.VMEM((GROWS, GY), F32),
            pltpu.VMEM((C1, GY), F32),
            pltpu.VMEM((2, n_y, n_hi, per, GY), BF16),
            pltpu.VMEM((PZ * PX + 16, GY), BF16),
            pltpu.VMEM((n_y, n_hi, per, GY), BF16),
            pltpu.VMEM((n_y, n_hi, per, GY), BF16),
            pltpu.VMEM((n_y - 1, n_hi, per, GY), BF16),
            pltpu.VMEM((n_lo - 1, first, per, GY), BF16),
            pltpu.VMEM((n_hi, per, GY), BF16),
            pltpu.VMEM((n_hi, PZ * PX + 16, GY), BF16),
            pltpu.VMEM((2 * n_lo, PZ * PX, GY), BF16),
            pltpu.VMEM((n_lo - 1, 2, PZ * PX, GY), BF16),
            dma((2,)),
            dma((2,)),
            dma((2,)),
            dma((2,)),
            dma,
            dma,
            dma,
            dma,
            dma,
            dma,
            dma,
            dma,
        ],
        compiler_params=pltpu.CompilerParams(
            collective_id=1, has_side_effects=True, vmem_limit_bytes=32 * 2**20
        ),
        name="train",
    )(slot, patch, *weights)


def finish_kernel(heat_in, pred_in, grad_in, heat_out, pred_out, grad_out, done):
    copy = pltpu.make_async_copy(heat_in, heat_out, done)
    copy.start()
    total = grad_in[0].astype(F32)
    for t in range(1, grad_in.shape[0]):
        total = total + grad_in[t].astype(F32)
    grad_out[...] = total
    for s in range(2):
        for z in range(PZ):
            pred_out[s, z] = pred_in[s, z * PX : (z + 1) * PX, :].astype(BF16)
    copy.wait()


def finish(heat, preds, partials):
    return pl.pallas_call(
        finish_kernel,
        out_shape=(
            jax.ShapeDtypeStruct(heat.shape, F32),
            jax.ShapeDtypeStruct((2, PZ, PX, GY), BF16),
            jax.ShapeDtypeStruct(partials.shape[1:], F32),
        ),
        in_specs=[pl.BlockSpec(memory_space=pl.ANY), VMEM, VMEM],
        out_specs=(HBM, VMEM, VMEM),
        scratch_shapes=[pltpu.SemaphoreType.DMA],
        compiler_params=pltpu.CompilerParams(vmem_limit_bytes=8 * 2**20),
        name="finish",
    )(heat, preds, partials)


def local(
    n_sec,
    n_dp,
    heat_start,
    conductivity,
    patch_z,
    patch_x,
    slot_table,
    w_stem,
    w_lift,
    w_down,
    w_deep,
    w_merge,
    w_out,
):
    n_lo = LINE
    n_hi = n_dp // n_lo
    weights = (w_stem.T, w_lift, w_down.T, w_deep, w_merge, w_out)
    heat_two, patch, *ready, slot = heat_steps(
        n_sec, n_dp, heat_start, conductivity, patch_z, patch_x, slot_table, weights
    )
    scale = 1.0 / (n_sec * n_dp * PZ * PX * GY)
    preds, partials = train(scale, n_sec, n_hi, n_lo, slot, patch, ready)
    return finish(heat_two, preds, partials)


def solution(mesh):
    n_sec, n_dp = mesh.shape["section"], mesh.shape["dp"]
    both = ("section", "dp")
    return jax.shard_map(
        functools.partial(local, n_sec, n_dp),
        mesh=mesh,
        in_specs=(P(both, None, None), P(both, None, None), P(both), P(both), P(both)) + (P(),) * 6,
        out_specs=(P(both, None, None), P(both, None, None, None), P("dp", None)),
        check_vma=False,
    )
```

```python
import functools

import jax
import jax.numpy as jnp
from jax import lax
from jax.experimental import pallas as pl
from jax.experimental.pallas import tpu as pltpu
from jax.sharding import PartitionSpec as P

MESH = pl.DeviceIdType.MESH
TIME_STEP = 0.15
GY = 128
PZ = 4
PX = 8
C1 = 64
C2 = 128
GROWS = 2048
LINE = 8
F32 = jnp.float32
BF16 = jnp.bfloat16
VMEM = pl.BlockSpec(memory_space=pltpu.VMEM)
SMEM = pl.BlockSpec(memory_space=pltpu.SMEM)
HBM = pl.BlockSpec(memory_space=pltpu.HBM)


def rounded(x):
    return x.astype(BF16).astype(F32)


NT = (((1,), (1,)), ((), ()))
NN = (((1,), (0,)), ((), ()))


def mm(a, b, dims=NN):
    return lax.dot_general(a, b, dims, preferred_element_type=F32)


def heat_part(
    enter,
    ready,
    n_sec,
    n_dp,
    pz_ref,
    px_ref,
    slot_ref,
    u_hbm,
    k_hbm,
    stem_hbm,
    lift_hbm,
    down_hbm,
    deep_hbm,
    merge_hbm,
    proj_hbm,
    out_ref,
    patch_ref,
    stem_ref,
    lift_ref,
    lift_t,
    down_ref,
    down_back,
    deep_ref,
    deep_t,
    fine_ref,
    fine_t,
    coarse_ref,
    coarse_t,
    proj_col,
    slot_tile,
    v_stem,
    v_down,
    v_merge,
    v_proj,
    u_ref,
    k_ref,
    ulo,
    klo,
    uhi,
    khi,
    h1,
    load,
    send,
    recv,
):
    total = n_sec * n_dp
    depth = u_ref.shape[0]
    me = lax.axis_index("section") * n_dp + lax.axis_index("dp")
    after = lax.rem(me + 1, total)
    before = lax.rem(me + total - 1, total)

    def place(i):
        return (lax.div(i, n_dp), lax.rem(i, n_dp))

    below, above = me > 0, me < total - 1
    enter()
    loads = [
        pltpu.make_async_copy(u_hbm, u_ref, load.at[0]),
        pltpu.make_async_copy(k_hbm, k_ref, load.at[1]),
        pltpu.make_async_copy(down_hbm, v_down, load.at[2]),
        pltpu.make_async_copy(stem_hbm, v_stem, load.at[3]),
        pltpu.make_async_copy(lift_hbm, lift_ref, load.at[4]),
        pltpu.make_async_copy(deep_hbm, deep_ref, load.at[5]),
        pltpu.make_async_copy(merge_hbm, v_merge, load.at[6]),
        pltpu.make_async_copy(proj_hbm, v_proj, load.at[7]),
    ]
    for copy in loads:
        copy.start()
    ready()
    plan = (
        (u_hbm.at[pl.ds(depth - 2, 2)], ulo, after),
        (k_hbm.at[pl.ds(depth - 2, 2)], klo, after),
        (u_hbm.at[pl.ds(0, 2)], uhi, before),
        (k_hbm.at[pl.ds(0, 2)], khi, before),
    )
    copies = [
        pltpu.make_async_remote_copy(
            src_ref=src,
            dst_ref=dst,
            send_sem=send.at[i],
            recv_sem=recv.at[i],
            device_id=place(peer),
            device_id_type=MESH,
        )
        for i, (src, dst, peer) in enumerate(plan)
    ]
    upward, downward = copies[0:2], copies[2:4]

    @pl.when(above)
    def _():
        for copy in upward:
            copy.start()

    @pl.when(below)
    def _():
        for copy in downward:
            copy.start()

    @pl.when(me == 0)
    def _():
        ulo[...] = jnp.zeros_like(ulo)
        klo[...] = jnp.zeros_like(klo)

    @pl.when(me == total - 1)
    def _():
        uhi[...] = jnp.zeros_like(uhi)
        khi[...] = jnp.zeros_like(khi)

    rows, lanes = u_ref.shape[1:]
    row = lax.broadcasted_iota(jnp.int32, (rows, lanes), 0)
    lane = lax.broadcasted_iota(jnp.int32, (rows, lanes), 1)

    def step(up, uc, un, kp, kc, kn):
        flux = (kc + kn) * (un - uc) + (kc + kp) * (up - uc)
        for axis, place_, size in ((0, row, rows), (1, lane, lanes)):
            last = place_ == size - 1
            first = place_ == 0
            u_next = jnp.where(last, 0.0, pltpu.roll(uc, size - 1, axis))
            k_next = jnp.where(last, 0.0, pltpu.roll(kc, size - 1, axis))
            face = (kc + k_next) * (u_next - uc)
            back = jnp.where(first, kc * uc, pltpu.roll(face, 1, axis))
            flux = flux + (face - back)
        return uc + (0.5 * TIME_STEP) * flux

    for copy in loads:
        copy.wait()
    group = 7

    def interior(i, carry):
        for j in range(group):
            z = 1 + i * group + j
            h1[z + 1] = step(
                u_ref[z - 1], u_ref[z], u_ref[z + 1], k_ref[z - 1], k_ref[z], k_ref[z + 1]
            )
        return carry

    lax.fori_loop(0, (depth - 2) // group, interior, 0)

    def second(z):
        out_ref[z] = step(h1[z], h1[z + 1], h1[z + 2], k_ref[z - 1], k_ref[z], k_ref[z + 1])

    pack = 6

    def inner(i, carry):
        for j in range(pack):
            second(2 + i * pack + j)
        return carry

    lax.fori_loop(0, (depth - 4) // pack, inner, 0)
    unit = lax.broadcasted_iota(jnp.int32, (C2, C2), 0) == lax.broadcasted_iota(jnp.int32, (C2, C2), 1)
    eye = unit[0:C1, 0:C1]
    unit = unit.astype(BF16)
    stem_ref[...] = mm(unit[0:C1, 0:C1], v_stem[...], NT).astype(BF16)
    for dy in range(3):
        starts = [(j * 3 + dy) * C1 for j in range(9)]
        part = jnp.concatenate([v_down[r : r + C1, :] for r in starts], axis=0)
        down_ref[dy * C2 : (dy + 1) * C2, :] = mm(unit, part, NT).astype(BF16)
    for j in range(9):
        down_back[:, j * C2 : (j + 1) * C2] = v_down[j * 3 * C1 : (j + 1) * 3 * C1, :]

    def turned(x):
        return x.astype(F32).T.astype(BF16)

    lift_t[...] = turned(lift_ref[...])
    slot_tile[...] = jnp.full((16, GY), slot_ref[0].astype(F32)).astype(BF16)
    deep_t[...] = turned(deep_ref[...])
    fine = v_merge[:, 0:C1]
    coarse = v_merge[:, C1 : C1 + C2]
    fine_ref[...] = fine
    fine_t[...] = turned(fine)
    coarse_ref[...] = coarse
    coarse_t[...] = turned(coarse)
    row64 = v_proj[...].astype(F32)
    column = jnp.sum(jnp.where(eye, jnp.broadcast_to(row64, (C1, C1)), 0.0), axis=1, keepdims=True)
    proj_col[...] = jnp.broadcast_to(column, proj_col.shape)

    @pl.when(below)
    def _():
        for copy in upward:
            copy.wait_recv()

    @pl.when(above)
    def _():
        for copy in downward:
            copy.wait_recv()

    has_lo = (me > 0).astype(F32)
    has_hi = (me < total - 1).astype(F32)
    ul, kl, uh, kh = ulo, klo, uhi, khi
    end = depth - 1
    h1[0] = has_lo * step(ul[0], ul[1], u_ref[0], kl[0], kl[1], k_ref[0])
    h1[1] = step(ul[1], u_ref[0], u_ref[1], kl[1], k_ref[0], k_ref[1])
    h1[depth] = step(u_ref[end - 1], u_ref[end], uh[0], k_ref[end - 1], k_ref[end], kh[0])
    h1[depth + 1] = has_hi * step(u_ref[end], uh[0], uh[1], k_ref[end], kh[0], kh[1])

    out_ref[0] = step(h1[0], h1[1], h1[2], kl[1], k_ref[0], k_ref[1])
    out_ref[end] = step(h1[end], h1[depth], h1[depth + 1], k_ref[end - 1], k_ref[end], kh[0])
    second(1)
    second(end - 1)
    pz = pz_ref[0]
    px = px_ref[0]
    for z in range(PZ):
        patch_ref[0, z] = h1[1 + pz + z, pl.ds(px, PX), :]
        patch_ref[1, z] = k_ref[pz + z, pl.ds(px, PX), :]
        patch_ref[2, z] = out_ref[pz + z, pl.ds(px, PX), :]

    @pl.when(above)
    def _():
        for copy in upward:
            copy.wait_send()

    @pl.when(below)
    def _():
        for copy in downward:
            copy.wait_send()


def silu_and_slope(z):
    s = 0.5 * jnp.tanh(0.5 * z) + 0.5
    value = z * s
    return value, s + value * (1.0 - s)


def block(x, b):
    return x[:, b * GY : (b + 1) * GY]


def train_part(
    scale,
    n_sec,
    n_hi,
    n_lo,
    slot_tile,
    patch_ref,
    w_stem,
    w_lift,
    w_lift_t,
    w_down,
    wback,
    w_deep,
    w_deep_t,
    w_fine,
    w_fine_t,
    w_coarse,
    w_coarse_t,
    w_proj_col,
    pred_out,
    buf2,
    tall,
    cols,
    l1,
    l2,
    g1,
    g2,
    dz_ref,
    dz2_ref,
    colsd,
    colsz,
    pack,
    pair,
    grads,
    packet,
    cbuf,
    half_ref,
    buf1,
    buf_late,
    acc,
    pbuf,
    q_ref,
    qbuf,
    s1,
    r1,
    sc,
    rc,
    s5,
    r5,
    s2,
    r2,
    s3,
    r3,
    s4,
    r4,
):
    sec = lax.axis_index("section")
    dp = lax.axis_index("dp")
    hi = lax.div(dp, n_lo)
    lo = lax.rem(dp, n_lo)
    across = n_sec * n_hi
    mine = sec * n_hi + hi
    n_y = n_lo // 2
    core = lax.rem(lo, 2)
    other = 1 - core
    y = lax.div(lo, 2)

    def in_line(d):
        peer = lax.rem(lo + d, n_lo)
        return peer, (sec, hi * n_lo + peer)

    def in_y(d):
        peer = lax.rem(y + d, n_y)
        return peer, (sec, hi * n_lo + 2 * peer + core)

    def in_column(d):
        peer = lax.rem(mine + d, across)
        return peer, (lax.div(peer, n_hi), lax.rem(peer, n_hi) * n_lo + lo)

    def in_part(d):
        peer = lax.rem(hi + d, n_hi)
        return peer, (sec, peer * n_lo + lo)

    def send(src, dst, ssem, rsem, device):
        copy = pltpu.make_async_remote_copy(
            src_ref=src, dst_ref=dst, send_sem=ssem, recv_sem=rsem, device_id=device, device_id_type=MESH
        )
        copy.start()
        return copy

    def group(like, ssem, rsem, device):
        return pltpu.make_async_remote_copy(
            src_ref=like, dst_ref=like, send_sem=ssem, recv_sem=rsem, device_id=device, device_id_type=MESH
        )

    plane = PX * GY
    cells = PZ * plane
    small = cells // 4
    row8 = lax.broadcasted_iota(jnp.int32, (PX, GY), 0)
    lane8 = lax.broadcasted_iota(jnp.int32, (PX, GY), 1)
    lane64 = lax.broadcasted_iota(jnp.int32, (C1, GY), 1)

    tall[...] = jnp.zeros_like(tall)
    for channel in range(2):
        for dx in range(3):
            for dy in range(3):
                shifted = []
                for z in range(PZ):
                    v = rounded(patch_ref[channel, z])
                    if dx == 0:
                        v = jnp.where(row8 == 0, 0.0, pltpu.roll(v, 1, 0))
                    elif dx == 2:
                        v = jnp.where(row8 == PX - 1, 0.0, pltpu.roll(v, PX - 1, 0))
                    if dy == 0:
                        v = jnp.where(lane8 == 0, 0.0, pltpu.roll(v, 1, 1))
                    elif dy == 2:
                        v = jnp.where(lane8 == GY - 1, 0.0, pltpu.roll(v, GY - 1, 1))
                    shifted.append(v)
                for dz in range(3):
                    r = ((dz * 3 + dx) * 3 + dy) * 2 + channel
                    for z in range(PZ):
                        if 0 <= z + dz - 1 < PZ:
                            tall[pl.ds(z * PX * C1 + r, PX, stride=C1), :] = shifted[z + dz - 1]
    for b in range(PZ * PX):
        cols[:, b * GY : (b + 1) * GY] = tall[b * C1 : (b + 1) * C1, :].astype(BF16)

    taps = w_stem.shape[1]
    stem = w_stem[...]
    lift = w_lift[...]
    pooled = []
    for zz in range(PZ // 2):
        rows = []
        for z in (2 * zz, 2 * zz + 1):
            here = slice(z * plane, (z + 1) * plane)
            value, slope = silu_and_slope(mm(stem, cols[0:taps, here]))
            g1[:, here] = slope
            one = value.astype(BF16)
            l1[:, here] = one
            value, slope = silu_and_slope(mm(lift, one))
            g2[:, here] = slope
            two = value.astype(BF16)
            l2[:, here] = two
            rows.append(two.astype(F32))
        both = rows[0] + rows[1]
        for xx in range(PX // 2):
            pooled.append(rounded((block(both, 2 * xx) + block(both, 2 * xx + 1)) * 0.25))

    hz, hx = PZ // 2, PX // 2
    nothing = jnp.zeros((C1, GY), BF16)
    pooled = [v.astype(BF16) for v in pooled]
    for dz in range(3):
        for dx in range(3):
            r = (dz * 3 + dx) * C1
            for z in range(hz):
                for x in range(hx):
                    sz, sx = z + dz - 1, x + dx - 1
                    inside = 0 <= sz < hz and 0 <= sx < hx
                    b = z * hx + x
                    colsd[r : r + C1, b * GY : (b + 1) * GY] = pooled[sz * hx + sx] if inside else nothing
    depth = 9 * C1
    colsd[depth : depth + C1, :] = jnp.zeros((C1, small), BF16)
    products = mm(w_down[...], colsd[0:depth, :])
    lane128 = lax.broadcasted_iota(jnp.int32, (C2, GY), 1)

    def later(v):
        return jnp.where(lane128 == 0, 0.0, pltpu.roll(v, 1, 1))

    def sooner(v):
        return jnp.where(lane128 == GY - 1, 0.0, pltpu.roll(v, GY - 1, 1))

    summed = []
    for b in range(hz * hx):
        v = block(products, b)
        summed.append(later(v[0:C2]) + v[C2 : 2 * C2] + sooner(v[2 * C2 : 3 * C2]))
    value, slope_down = silu_and_slope(jnp.concatenate(summed, axis=1))
    coarse = value.astype(BF16)
    value, slope_deep = silu_and_slope(mm(w_deep[...], coarse))
    deeper = value.astype(BF16)
    merge_fine = w_fine[...]
    lifted = mm(w_coarse[...], deeper)

    out_col = w_proj_col[...]
    fine_t = w_fine_t[...]
    d_out = jnp.zeros((C1, GY), F32)
    gathered = [None] * (hz * hx)
    forecast = []
    for z in range(PZ):
        here = slice(z * plane, (z + 1) * plane)
        two = l2[:, here]
        added = [block(lifted, (z // 2) * hx + x // 2) for x in range(PX)]
        value, slope = silu_and_slope(mm(merge_fine, two) + jnp.concatenate(added, axis=1))
        merged = value.astype(BF16)
        held = merged.astype(F32)
        predicted = jnp.zeros((PX, GY), F32)
        for x in range(PX):
            summed = jnp.sum(block(held, x) * out_col, axis=0, keepdims=True)
            predicted = jnp.where(row8 == x, summed, predicted)
        forecast.append(predicted)
        misfit = (predicted - rounded(patch_ref[2, z])) * scale
        for x in range(PX):
            d_out = d_out + block(held, x) * misfit[x : x + 1, :]
        d_merged = jnp.concatenate([out_col * misfit[x : x + 1, :] for x in range(PX)], axis=1)
        dz = rounded(d_merged) * slope
        for x in range(PX):
            b = (z // 2) * hx + x // 2
            gathered[b] = block(dz, x) if gathered[b] is None else gathered[b] + block(dz, x)
        dz = dz.astype(BF16)
        dz_ref[:, here] = dz

    half = PZ * PX // 2
    packet[0:half, :] = jnp.concatenate(forecast[0 : PZ // 2], axis=0).astype(BF16)
    packet[half : 2 * half, :] = jnp.concatenate(forecast[PZ // 2 : PZ], axis=0).astype(BF16)
    packet[2 * half : 2 * half + 16, :] = slot_tile[...]
    for d in range(1, n_hi):
        peer, device = in_part(d)
        send(packet, pbuf.at[d], s3, r3, device)
    packets = group(pbuf.at[pl.ds(1, n_hi - 1)], s3, r3, device)
    pbuf[0] = packet[...]

    d_lifted = jnp.concatenate(gathered, axis=1).astype(BF16)
    d_deeper = mm(w_coarse_t[...], d_lifted)
    dz_deep = (rounded(d_deeper) * slope_deep).astype(BF16)
    d_coarse = mm(w_deep_t[...], dz_deep)
    dz_down = (rounded(d_coarse) * slope_down).astype(BF16)

    r_ = lax.broadcasted_iota(jnp.int32, (C2, C2), 0)
    c_ = lax.broadcasted_iota(jnp.int32, (C2, C2), 1)
    parted = jnp.where(r_ < C1, 2 * r_, 2 * r_ - (C2 - 1)) == c_
    dz_parted = mm(parted.astype(BF16), dz_down)
    blocks = [block(dz_parted, b) for b in range(hz * hx)]
    dz_shifts = jnp.concatenate(
        [
            jnp.concatenate([f(v) for v in blocks], axis=1).astype(BF16)
            for f in (sooner, lambda v: v, later)
        ],
        axis=0,
    )
    d_down = mm(dz_shifts, colsd[...], NT)
    low = lane64 < C1
    turned_chunks = {}

    def piece(h, lanes_low):
        odd, h = divmod(h, 27)
        zx, dy = divmod(h, 3)
        q, high = divmod(zx, 2)
        r = dy * C2 + odd * C1
        chunk = d_down[r : r + C1, q * GY : (q + 1) * GY]
        if bool(high) != lanes_low:
            return chunk
        if (r, q) not in turned_chunks:
            turned_chunks[r, q] = pltpu.roll(chunk, C1, 1)
        return turned_chunks[r, q]

    base = 27 + 32
    for j in range(27):
        pack[pl.ds(base + j, C1, stride=27), :] = jnp.where(
            low, piece(2 * j, True), piece(2 * j + 1, False)
        )

    per = grads.shape[3]
    first = -(-(27 + 32) // (per * n_lo))
    top = n_hi - (27 + 32 + 27 * C1) // (per * n_lo)
    tail = first + top

    def emit(hi_):
        for lo_ in range(n_lo):
            start = (hi_ * n_lo + lo_) * per
            grads[lo_ % 2, lo_ // 2, (hi_ + top) % n_hi] = pack[start : start + per, :].astype(BF16)

    for h in range(first, n_hi - top):
        emit(h)

    def swap(begin, count, i):
        return send(
            grads.at[other, :, pl.ds(begin, count)],
            cbuf.at[:, pl.ds(begin, count)],
            sc.at[i],
            rc.at[i],
            (sec, hi * n_lo + 2 * y + other),
        )

    def chip_sum(begin, count, copy, i):
        copy.wait_recv()
        part = slice(begin, begin + count)
        for y_ in range(n_y):
            total = grads[core, y_, part].astype(F32) + cbuf[y_, part].astype(F32)
            half_ref[y_, part] = total.astype(BF16)
        for d in range(1, n_y):
            peer, device = in_y(d)
            send(
                half_ref.at[peer, pl.ds(begin, count)],
                buf1.at[d - 1, pl.ds(begin, count)],
                s1.at[i],
                r1.at[i],
                device,
            )
        return group(buf1.at[:, pl.ds(begin, count)], s1.at[i], r1.at[i], device)

    swap_down = swap(tail, n_hi - tail, 0)

    def twice(x):
        pair[:, 0:C1] = x
        pair[:, C1:GY] = jnp.zeros((C1, GY - C1), F32)
        once = pair[...]
        return once + pltpu.roll(once, C1, 1)

    d_coarse_merge = mm(d_lifted, deeper, NT)
    d_deep = mm(dz_deep, coarse, NT)
    d_fine = twice(mm(dz_ref[...], l2[...], NT))
    low32 = lax.broadcasted_iota(jnp.int32, (32, GY), 1) < C1
    base = 27 + 32 + 27 * C1
    pack[base : base + C2, :] = d_deep
    base = base + C2
    pair[...] = d_fine
    fine_even_odd = [pair[pl.ds(i, 32, stride=2), :] for i in range(2)]
    pair[...] = d_coarse_merge
    coarse_even_odd = [pair[pl.ds(i, 32, stride=2), :] for i in range(2)]
    turn = pltpu.roll(coarse_even_odd[0], C1, 1)
    pack[pl.ds(base, 32, stride=3), :] = jnp.where(low32, fine_even_odd[0], turn)
    pack[pl.ds(base + 1, 32, stride=3), :] = jnp.where(low32, turn, fine_even_odd[1])
    pack[pl.ds(base + 2, 32, stride=3), :] = coarse_even_odd[1]
    base = base + 96
    column = jnp.sum(d_out, axis=1, keepdims=True)
    across_ = lane64 == lax.broadcasted_iota(jnp.int32, (C1, GY), 0)
    pack[base : base + 1, :] = jnp.sum(
        jnp.where(across_, jnp.broadcast_to(column, (C1, GY)), 0.0), axis=0, keepdims=True
    )
    pack[base + 1 : GROWS, :] = jnp.zeros((GROWS - base - 1, GY), F32)


    for h in range(n_hi - top, n_hi):
        emit(h)
    swap_join = swap(0, top, 1)

    blank = jnp.zeros((C2, GY), BF16)
    for dz in range(3):
        for dx in range(3):
            j = dz * 3 + dx
            for z in range(hz):
                for x in range(hx):
                    sz, sx = z - (dz - 1), x - (dx - 1)
                    inside = 0 <= sz < hz and 0 <= sx < hx
                    b = z * hx + x
                    colsz[j * C2 : (j + 1) * C2, b * GY : (b + 1) * GY] = (
                        block(dz_down, sz * hx + sx) if inside else blank
                    )
    early_down = chip_sum(tail, n_hi - tail, swap_down, 0)
    d_shifted = mm(wback[...], colsz[...])
    d_pooled = []
    for b in range(hz * hx):
        whole = block(d_shifted, b)
        total = whole[C1 : 2 * C1]
        total = total + jnp.where(lane64 == GY - 1, 0.0, pltpu.roll(whole[0:C1], GY - 1, 1))
        total = total + jnp.where(lane64 == 0, 0.0, pltpu.roll(whole[2 * C1 : 3 * C1], 1, 1))
        d_pooled.append(rounded(total) * 0.25)

    early_join = chip_sum(0, top, swap_join, 1)
    lift_t = w_lift_t[...]
    d_stem = jnp.zeros((C1, C1), F32)
    for z in range(PZ):
        here = slice(z * plane, (z + 1) * plane)
        spread = jnp.concatenate([d_pooled[(z // 2) * hx + x // 2] for x in range(PX)], axis=1)
        dz = ((rounded(mm(fine_t, dz_ref[:, here])) + spread) * g2[:, here]).astype(BF16)
        dz2_ref[:, here] = dz
        d_one = rounded(mm(lift_t, dz))
        dz = (d_one * g1[:, here]).astype(BF16)
        d_stem = d_stem + mm(dz, cols[:, here], NT)

    d_lift = twice(mm(dz2_ref[...], l1[...], NT))

    pair[:, 0:C1] = d_stem
    pair[:, C1:GY] = jnp.zeros((C1, GY - C1), F32)
    turned = pair[...]
    source = lax.broadcasted_iota(jnp.int32, (C1, GY), 0)
    for bit in range(6):
        moved = pltpu.roll(turned, (taps << bit) % GY, 1)
        turned = jnp.where((source >> bit) % 2 == 1, moved, turned)
    begin = source * taps
    wraps = lane64 < begin % GY
    stay = jnp.where(wraps, 0.0, turned).astype(BF16)
    over = jnp.where(wraps, turned, 0.0).astype(BF16)
    target_row = lax.broadcasted_iota(jnp.int32, (32, C1), 0)
    owner = lax.broadcasted_iota(jnp.int32, (32, C1), 1) * taps // GY
    stem_rows = mm((target_row == owner).astype(BF16), stay)
    stem_rows = stem_rows + mm((target_row == owner + 1).astype(BF16), over)
    pack[0:27, :] = stem_rows[0:27, :]

    low32 = lax.broadcasted_iota(jnp.int32, (32, GY), 1) < C1
    pair[...] = d_lift
    pack[27 : 27 + 32, :] = jnp.where(low32, pair[pl.ds(0, 32, stride=2), :], pair[pl.ds(1, 32, stride=2), :])


    for h in range(first):
        emit(h)
    for d in range(1, n_lo):
        peer, device = in_line(d)
        send(
            grads.at[lax.rem(peer, 2), lax.div(peer, 2), pl.ds(top, first)],
            buf_late.at[d - 1],
            s5,
            r5,
            device,
        )
    late = group(buf_late, s5, r5, device)

    for copy in (early_down, early_join):
        copy.wait_recv()
    for h in range(first, n_hi):
        at = (h + top) % n_hi
        value = half_ref[y, at].astype(F32)
        for d in range(n_y - 1):
            value = value + buf1[d, at].astype(F32)
        acc[h] = value.astype(BF16)
    late.wait_recv()
    for h in range(first):
        value = grads[core, y, h + top].astype(F32)
        for d in range(n_lo - 1):
            value = value + buf_late[d, h].astype(F32)
        acc[h] = value.astype(BF16)
    ring = 8
    far_first = sorted(range(1, n_hi + 1), key=lambda e: (e == n_hi, -min(e % ring, ring - e % ring)))
    for e in far_first:
        h = lax.rem(hi + e, n_hi)
        for q in range(n_sec):
            if e == n_hi and q == 0:
                buf2[mine] = acc[h]
                continue
            owner = lax.rem(sec + q, n_sec)
            device = (owner, h * n_lo + lo)
            send(acc.at[h], buf2.at[mine], s2, r2, device)
    partials = group(buf2.at[pl.ds(0, across - 1)], s2, r2, device)

    packets.wait_recv()
    rows = PZ * PX

    def route(q, carry):
        wanted = (hi * (2 * n_lo) + q).astype(F32)
        value = jnp.zeros((rows, GY), F32)
        for src in range(n_hi):
            named = pbuf[src, rows : rows + 16, :].astype(F32)
            named = jnp.concatenate([named] * (rows // 16), axis=0)
            value = value + jnp.where(named == wanted, pbuf[src, 0:rows, :].astype(F32), 0.0)
        q_ref[q] = value.astype(BF16)
        return carry

    lax.fori_loop(0, 2 * n_lo, route, 0)
    for d in range(1, n_lo):
        peer, device = in_line(d)
        send(q_ref.at[pl.ds(2 * peer, 2)], qbuf.at[d - 1], s4, r4, device)
    routed = group(qbuf, s4, r4, device)

    routed.wait_recv()
    for s in range(2):
        value = q_ref[2 * lo + s].astype(F32)
        for d in range(n_lo - 1):
            value = value + qbuf[d, s].astype(F32)
        pred_out[s] = value

    partials.wait_recv()
    for copy in (swap_down, swap_join, packets, early_down, early_join, late, routed, partials):
        copy.wait_send()


def whole_kernel(n_sec, n_hi, n_lo, scale, *refs):
    ins, refs = refs[:11], refs[11:]
    (heat_out, pred_out, buf2), refs = refs[:3], refs[3:]
    made, refs = refs[:14], refs[14:]
    heat_scratch, train_scratch = refs[:14], refs[14:]
    sec = lax.axis_index("section")
    dp = lax.axis_index("dp")
    hi = lax.div(dp, n_lo)
    lo = lax.rem(dp, n_lo)
    across = n_sec * n_hi
    mine = sec * n_hi + hi
    n_dp = n_hi * n_lo
    total = n_sec * n_dp
    me = sec * n_dp + dp
    barrier = pltpu.get_barrier_semaphore()
    at_start = jnp.logical_and(lo == 0, me > 0)
    at_end = jnp.logical_and(lo == n_lo - 1, me < total - 1)
    outside = jnp.logical_or(at_start, at_end)

    def signal(section, index):
        pl.semaphore_signal(barrier, inc=1, device_id=(section, index), device_id_type=MESH)

    def enter():
        @pl.when(at_start)
        def _():
            signal(lax.div(me - 1, n_dp), lax.rem(me - 1, n_dp))

        @pl.when(at_end)
        def _():
            signal(lax.div(me + 1, n_dp), lax.rem(me + 1, n_dp))

        for d in range(1, n_lo):
            signal(sec, hi * n_lo + lax.rem(lo + d, n_lo))
        for d in range(1, across):
            peer = lax.rem(mine + d, across)
            signal(lax.div(peer, n_hi), lax.rem(peer, n_hi) * n_lo + lo)

    def ready():
        peers = n_lo - 1 + across - 1

        @pl.when(outside)
        def _():
            pl.semaphore_wait(barrier, peers + 1)

        @pl.when(jnp.logical_not(outside))
        def _():
            pl.semaphore_wait(barrier, peers)

    heat_part(enter, ready, n_sec, n_dp, *ins, heat_out, *made, *heat_scratch)
    patch, *weights, slot_tile = made
    train_part(scale, n_sec, n_hi, n_lo, slot_tile, patch, *weights, pred_out, buf2, *train_scratch)


def whole(scale, n_sec, n_hi, n_lo, heat, cond, patch_z, patch_x, slot, weights):
    layers = (2,) + heat.shape[1:]
    taps = weights[0].shape[0]
    cells = PZ * PX * GY
    small = cells // 4
    per = GROWS // (n_lo * n_hi)
    across = n_sec * n_hi
    n_y = n_lo // 2
    first = -(-(27 + 32) // (per * n_lo))
    dma = pltpu.SemaphoreType.DMA
    operands = (heat, cond, *weights)
    operands = [pltpu.with_memory_space_constraint(x, pltpu.HBM) for x in operands]
    return pl.pallas_call(
        functools.partial(whole_kernel, n_sec, n_hi, n_lo, scale),
        out_shape=(
            jax.ShapeDtypeStruct(heat.shape, F32),
            jax.ShapeDtypeStruct((2, PZ * PX, GY), F32),
            jax.ShapeDtypeStruct((across, per, GY), BF16),
        ),
        in_specs=[SMEM] * 3 + [HBM] * 8,
        out_specs=(VMEM,) * 3,
        scratch_shapes=[
            pltpu.VMEM((3, PZ, PX, GY), F32),
            pltpu.VMEM((C1, taps), BF16),
            pltpu.VMEM((C1, C1), BF16),
            pltpu.VMEM((C1, C1), BF16),
            pltpu.VMEM((3 * C2, 9 * C1), BF16),
            pltpu.VMEM((3 * C1, 9 * C2), BF16),
            pltpu.VMEM((C2, C2), BF16),
            pltpu.VMEM((C2, C2), BF16),
            pltpu.VMEM((C1, C1), BF16),
            pltpu.VMEM((C1, C1), BF16),
            pltpu.VMEM((C1, C2), BF16),
            pltpu.VMEM((C2, C1), BF16),
            pltpu.VMEM((C1, GY), F32),
            pltpu.VMEM((16, GY), BF16),
            pltpu.VMEM(weights[0].shape, BF16),
            pltpu.VMEM(weights[2].shape, BF16),
            pltpu.VMEM(weights[4].shape, BF16),
            pltpu.VMEM(weights[5].shape, BF16),
            pltpu.VMEM(heat.shape, F32),
            pltpu.VMEM(heat.shape, F32),
            pltpu.VMEM(layers, F32),
            pltpu.VMEM(layers, F32),
            pltpu.VMEM(layers, F32),
            pltpu.VMEM(layers, F32),
            pltpu.VMEM((heat.shape[0] + 2,) + heat.shape[1:], F32),
            dma((8,)),
            dma((4,)),
            dma((4,)),
            pltpu.VMEM((PZ * PX * C1, GY), F32),
            pltpu.VMEM((C1, cells), BF16),
            pltpu.VMEM((C1, cells), BF16),
            pltpu.VMEM((C1, cells), BF16),
            pltpu.VMEM((C1, cells), F32),
            pltpu.VMEM((C1, cells), F32),
            pltpu.VMEM((C1, cells), BF16),
            pltpu.VMEM((C1, cells), BF16),
            pltpu.VMEM((10 * C1, small), BF16),
            pltpu.VMEM((9 * C2, small), BF16),
            pltpu.VMEM((GROWS, GY), F32),
            pltpu.VMEM((C1, GY), F32),
            pltpu.VMEM((2, n_y, n_hi, per, GY), BF16),
            pltpu.VMEM((PZ * PX + 16, GY), BF16),
            pltpu.VMEM((n_y, n_hi, per, GY), BF16),
            pltpu.VMEM((n_y, n_hi, per, GY), BF16),
            pltpu.VMEM((n_y - 1, n_hi, per, GY), BF16),
            pltpu.VMEM((n_lo - 1, first, per, GY), BF16),
            pltpu.VMEM((n_hi, per, GY), BF16),
            pltpu.VMEM((n_hi, PZ * PX + 16, GY), BF16),
            pltpu.VMEM((2 * n_lo, PZ * PX, GY), BF16),
            pltpu.VMEM((n_lo - 1, 2, PZ * PX, GY), BF16),
            dma((2,)),
            dma((2,)),
            dma((2,)),
            dma((2,)),
            dma,
            dma,
            dma,
            dma,
            dma,
            dma,
            dma,
            dma,
        ],
        compiler_params=pltpu.CompilerParams(
            collective_id=0, has_side_effects=True, vmem_limit_bytes=48 * 2**20
        ),
        name="whole",
    )(patch_z, patch_x, slot, *operands)


def finish_kernel(heat_in, pred_in, grad_in, heat_out, pred_out, grad_out, done):
    copy = pltpu.make_async_copy(heat_in, heat_out, done)
    copy.start()
    total = grad_in[0].astype(F32)
    for t in range(1, grad_in.shape[0]):
        total = total + grad_in[t].astype(F32)
    grad_out[...] = total
    for s in range(2):
        for z in range(PZ):
            pred_out[s, z] = pred_in[s, z * PX : (z + 1) * PX, :].astype(BF16)
    copy.wait()


def finish(heat, preds, partials):
    return pl.pallas_call(
        finish_kernel,
        out_shape=(
            jax.ShapeDtypeStruct(heat.shape, F32),
            jax.ShapeDtypeStruct((2, PZ, PX, GY), BF16),
            jax.ShapeDtypeStruct(partials.shape[1:], F32),
        ),
        in_specs=[pl.BlockSpec(memory_space=pl.ANY), VMEM, VMEM],
        out_specs=(HBM, VMEM, VMEM),
        scratch_shapes=[pltpu.SemaphoreType.DMA],
        compiler_params=pltpu.CompilerParams(vmem_limit_bytes=8 * 2**20),
        name="finish",
    )(heat, preds, partials)


def local(
    n_sec,
    n_dp,
    heat_start,
    conductivity,
    patch_z,
    patch_x,
    slot_table,
    w_stem,
    w_lift,
    w_down,
    w_deep,
    w_merge,
    w_out,
):
    n_lo = LINE
    n_hi = n_dp // n_lo
    weights = (w_stem.T, w_lift, w_down.T, w_deep, w_merge, w_out)
    scale = 1.0 / (n_sec * n_dp * PZ * PX * GY)
    heat_two, preds, partials = whole(
        scale, n_sec, n_hi, n_lo, heat_start, conductivity, patch_z, patch_x, slot_table, weights
    )
    return finish(heat_two, preds, partials)


def solution(mesh):
    n_sec, n_dp = mesh.shape["section"], mesh.shape["dp"]
    both = ("section", "dp")
    return jax.shard_map(
        functools.partial(local, n_sec, n_dp),
        mesh=mesh,
        in_specs=(P(both, None, None), P(both, None, None), P(both), P(both), P(both)) + (P(),) * 6,
        out_specs=(P(both, None, None), P(both, None, None, None), P("dp", None)),
        check_vma=False,
    )
```

```python
import functools

import jax
import jax.numpy as jnp
from jax import lax
from jax.experimental import pallas as pl
from jax.experimental.pallas import tpu as pltpu
from jax.sharding import PartitionSpec as P

MESH = pl.DeviceIdType.MESH
TIME_STEP = 0.15
GY = 128
PZ = 4
PX = 8
C1 = 64
C2 = 128
GROWS = 2048
LINE = 8
F32 = jnp.float32
BF16 = jnp.bfloat16
VMEM = pl.BlockSpec(memory_space=pltpu.VMEM)
SMEM = pl.BlockSpec(memory_space=pltpu.SMEM)
HBM = pl.BlockSpec(memory_space=pltpu.HBM)


def rounded(x):
    return x.astype(BF16).astype(F32)


NT = (((1,), (1,)), ((), ()))
NN = (((1,), (0,)), ((), ()))


def mm(a, b, dims=NN):
    return lax.dot_general(a, b, dims, preferred_element_type=F32)


def heat_part(
    enter,
    ready,
    n_sec,
    n_dp,
    pz_ref,
    px_ref,
    slot_ref,
    u_hbm,
    k_hbm,
    stem_hbm,
    lift_hbm,
    down_hbm,
    deep_hbm,
    merge_hbm,
    proj_hbm,
    out_ref,
    patch_ref,
    stem_ref,
    lift_ref,
    lift_t,
    down_ref,
    down_back,
    deep_ref,
    deep_t,
    fine_ref,
    fine_t,
    coarse_ref,
    coarse_t,
    proj_col,
    slot_tile,
    v_stem,
    v_down,
    v_merge,
    v_proj,
    u_ref,
    k_ref,
    ulo,
    klo,
    uhi,
    khi,
    h1,
    load,
    send,
    recv,
):
    total = n_sec * n_dp
    depth = u_ref.shape[0]
    me = lax.axis_index("section") * n_dp + lax.axis_index("dp")
    after = lax.rem(me + 1, total)
    before = lax.rem(me + total - 1, total)

    def place(i):
        return (lax.div(i, n_dp), lax.rem(i, n_dp))

    below, above = me > 0, me < total - 1
    enter()
    loads = [
        pltpu.make_async_copy(u_hbm, u_ref, load.at[0]),
        pltpu.make_async_copy(k_hbm, k_ref, load.at[1]),
        pltpu.make_async_copy(down_hbm, v_down, load.at[2]),
        pltpu.make_async_copy(stem_hbm, v_stem, load.at[3]),
        pltpu.make_async_copy(lift_hbm, lift_ref, load.at[4]),
        pltpu.make_async_copy(deep_hbm, deep_ref, load.at[5]),
        pltpu.make_async_copy(merge_hbm, v_merge, load.at[6]),
        pltpu.make_async_copy(proj_hbm, v_proj, load.at[7]),
    ]
    for copy in loads:
        copy.start()
    ready()
    plan = (
        (u_hbm.at[pl.ds(depth - 2, 2)], ulo, after),
        (k_hbm.at[pl.ds(depth - 2, 2)], klo, after),
        (u_hbm.at[pl.ds(0, 2)], uhi, before),
        (k_hbm.at[pl.ds(0, 2)], khi, before),
    )
    copies = [
        pltpu.make_async_remote_copy(
            src_ref=src,
            dst_ref=dst,
            send_sem=send.at[i],
            recv_sem=recv.at[i],
            device_id=place(peer),
            device_id_type=MESH,
        )
        for i, (src, dst, peer) in enumerate(plan)
    ]
    upward, downward = copies[0:2], copies[2:4]

    @pl.when(above)
    def _():
        for copy in upward:
            copy.start()

    @pl.when(below)
    def _():
        for copy in downward:
            copy.start()

    @pl.when(me == 0)
    def _():
        ulo[...] = jnp.zeros_like(ulo)
        klo[...] = jnp.zeros_like(klo)

    @pl.when(me == total - 1)
    def _():
        uhi[...] = jnp.zeros_like(uhi)
        khi[...] = jnp.zeros_like(khi)

    rows, lanes = u_ref.shape[1:]
    row = lax.broadcasted_iota(jnp.int32, (rows, lanes), 0)
    lane = lax.broadcasted_iota(jnp.int32, (rows, lanes), 1)

    def step(up, uc, un, kp, kc, kn):
        flux = (kc + kn) * (un - uc) + (kc + kp) * (up - uc)
        for axis, place_, size in ((0, row, rows), (1, lane, lanes)):
            last = place_ == size - 1
            first = place_ == 0
            u_next = jnp.where(last, 0.0, pltpu.roll(uc, size - 1, axis))
            k_next = jnp.where(last, 0.0, pltpu.roll(kc, size - 1, axis))
            face = (kc + k_next) * (u_next - uc)
            back = jnp.where(first, kc * uc, pltpu.roll(face, 1, axis))
            flux = flux + (face - back)
        return uc + (0.5 * TIME_STEP) * flux

    for copy in loads:
        copy.wait()
    group = 7

    def interior(i, carry):
        for j in range(group):
            z = 1 + i * group + j
            h1[z + 1] = step(
                u_ref[z - 1], u_ref[z], u_ref[z + 1], k_ref[z - 1], k_ref[z], k_ref[z + 1]
            )
        return carry

    lax.fori_loop(0, (depth - 2) // group, interior, 0)

    def second(z):
        out_ref[z] = step(h1[z], h1[z + 1], h1[z + 2], k_ref[z - 1], k_ref[z], k_ref[z + 1])

    pack = 6

    def inner(i, carry):
        for j in range(pack):
            second(2 + i * pack + j)
        return carry

    lax.fori_loop(0, (depth - 4) // pack, inner, 0)
    unit = lax.broadcasted_iota(jnp.int32, (C2, C2), 0) == lax.broadcasted_iota(jnp.int32, (C2, C2), 1)
    eye = unit[0:C1, 0:C1]
    unit = unit.astype(BF16)
    stem_ref[...] = mm(unit[0:C1, 0:C1], v_stem[...], NT).astype(BF16)
    for dy in range(3):
        starts = [(j * 3 + dy) * C1 for j in range(9)]
        part = jnp.concatenate([v_down[r : r + C1, :] for r in starts], axis=0)
        down_ref[dy * C2 : (dy + 1) * C2, :] = mm(unit, part, NT).astype(BF16)
    for j in range(9):
        down_back[:, j * C2 : (j + 1) * C2] = v_down[j * 3 * C1 : (j + 1) * 3 * C1, :]

    def turned(x):
        return x.astype(F32).T.astype(BF16)

    lift_t[...] = turned(lift_ref[...])
    slot_tile[...] = jnp.full((16, GY), slot_ref[0].astype(F32)).astype(BF16)
    deep_t[...] = turned(deep_ref[...])
    fine = v_merge[:, 0:C1]
    coarse = v_merge[:, C1 : C1 + C2]
    fine_ref[...] = fine
    fine_t[...] = turned(fine)
    coarse_ref[...] = coarse
    coarse_t[...] = turned(coarse)
    row64 = v_proj[...].astype(F32)
    column = jnp.sum(jnp.where(eye, jnp.broadcast_to(row64, (C1, C1)), 0.0), axis=1, keepdims=True)
    proj_col[...] = jnp.broadcast_to(column, proj_col.shape)

    @pl.when(below)
    def _():
        for copy in upward:
            copy.wait_recv()

    @pl.when(above)
    def _():
        for copy in downward:
            copy.wait_recv()

    has_lo = (me > 0).astype(F32)
    has_hi = (me < total - 1).astype(F32)
    ul, kl, uh, kh = ulo, klo, uhi, khi
    end = depth - 1
    h1[0] = has_lo * step(ul[0], ul[1], u_ref[0], kl[0], kl[1], k_ref[0])
    h1[1] = step(ul[1], u_ref[0], u_ref[1], kl[1], k_ref[0], k_ref[1])
    h1[depth] = step(u_ref[end - 1], u_ref[end], uh[0], k_ref[end - 1], k_ref[end], kh[0])
    h1[depth + 1] = has_hi * step(u_ref[end], uh[0], uh[1], k_ref[end], kh[0], kh[1])

    out_ref[0] = step(h1[0], h1[1], h1[2], kl[1], k_ref[0], k_ref[1])
    out_ref[end] = step(h1[end], h1[depth], h1[depth + 1], k_ref[end - 1], k_ref[end], kh[0])
    second(1)
    second(end - 1)
    pz = pz_ref[0]
    px = px_ref[0]
    for z in range(PZ):
        patch_ref[0, z] = h1[1 + pz + z, pl.ds(px, PX), :]
        patch_ref[1, z] = k_ref[pz + z, pl.ds(px, PX), :]
        patch_ref[2, z] = out_ref[pz + z, pl.ds(px, PX), :]

    @pl.when(above)
    def _():
        for copy in upward:
            copy.wait_send()

    @pl.when(below)
    def _():
        for copy in downward:
            copy.wait_send()


def silu_and_slope(z):
    s = 0.5 * jnp.tanh(0.5 * z) + 0.5
    value = z * s
    return value, s + value * (1.0 - s)


def block(x, b):
    return x[:, b * GY : (b + 1) * GY]


def train_part(
    scale,
    n_sec,
    n_hi,
    n_lo,
    slot_tile,
    patch_ref,
    w_stem,
    w_lift,
    w_lift_t,
    w_down,
    wback,
    w_deep,
    w_deep_t,
    w_fine,
    w_fine_t,
    w_coarse,
    w_coarse_t,
    w_proj_col,
    pred_out,
    buf2,
    tall,
    cols,
    l1,
    l2,
    g1,
    g2,
    dz_ref,
    dz2_ref,
    colsd,
    colsz,
    pack,
    pair,
    grads,
    packet,
    buf1,
    acc,
    pbuf,
    q_ref,
    qbuf,
    s1,
    r1,
    s2,
    r2,
    s3,
    r3,
    s4,
    r4,
):
    sec = lax.axis_index("section")
    dp = lax.axis_index("dp")
    hi = lax.div(dp, n_lo)
    lo = lax.rem(dp, n_lo)
    across = n_sec * n_hi
    mine = sec * n_hi + hi

    def in_line(d):
        peer = lax.rem(lo + d, n_lo)
        return peer, (sec, hi * n_lo + peer)

    def in_column(d):
        peer = lax.rem(mine + d, across)
        return peer, (lax.div(peer, n_hi), lax.rem(peer, n_hi) * n_lo + lo)

    def in_part(d):
        peer = lax.rem(hi + d, n_hi)
        return peer, (sec, peer * n_lo + lo)

    def send(src, dst, ssem, rsem, device):
        copy = pltpu.make_async_remote_copy(
            src_ref=src, dst_ref=dst, send_sem=ssem, recv_sem=rsem, device_id=device, device_id_type=MESH
        )
        copy.start()
        return copy

    def group(like, ssem, rsem, device):
        return pltpu.make_async_remote_copy(
            src_ref=like, dst_ref=like, send_sem=ssem, recv_sem=rsem, device_id=device, device_id_type=MESH
        )

    plane = PX * GY
    cells = PZ * plane
    small = cells // 4
    row8 = lax.broadcasted_iota(jnp.int32, (PX, GY), 0)
    lane8 = lax.broadcasted_iota(jnp.int32, (PX, GY), 1)
    lane64 = lax.broadcasted_iota(jnp.int32, (C1, GY), 1)

    tall[...] = jnp.zeros_like(tall)
    for channel in range(2):
        for dx in range(3):
            for dy in range(3):
                shifted = []
                for z in range(PZ):
                    v = rounded(patch_ref[channel, z])
                    if dx == 0:
                        v = jnp.where(row8 == 0, 0.0, pltpu.roll(v, 1, 0))
                    elif dx == 2:
                        v = jnp.where(row8 == PX - 1, 0.0, pltpu.roll(v, PX - 1, 0))
                    if dy == 0:
                        v = jnp.where(lane8 == 0, 0.0, pltpu.roll(v, 1, 1))
                    elif dy == 2:
                        v = jnp.where(lane8 == GY - 1, 0.0, pltpu.roll(v, GY - 1, 1))
                    shifted.append(v)
                for dz in range(3):
                    r = ((dz * 3 + dx) * 3 + dy) * 2 + channel
                    for z in range(PZ):
                        if 0 <= z + dz - 1 < PZ:
                            tall[pl.ds(z * PX * C1 + r, PX, stride=C1), :] = shifted[z + dz - 1]
    for b in range(PZ * PX):
        cols[:, b * GY : (b + 1) * GY] = tall[b * C1 : (b + 1) * C1, :].astype(BF16)

    taps = w_stem.shape[1]
    stem = w_stem[...]
    lift = w_lift[...]
    pooled = []
    for zz in range(PZ // 2):
        rows = []
        for z in (2 * zz, 2 * zz + 1):
            here = slice(z * plane, (z + 1) * plane)
            value, slope = silu_and_slope(mm(stem, cols[0:taps, here]))
            g1[:, here] = slope
            one = value.astype(BF16)
            l1[:, here] = one
            value, slope = silu_and_slope(mm(lift, one))
            g2[:, here] = slope
            two = value.astype(BF16)
            l2[:, here] = two
            rows.append(two.astype(F32))
        both = rows[0] + rows[1]
        for xx in range(PX // 2):
            pooled.append(rounded((block(both, 2 * xx) + block(both, 2 * xx + 1)) * 0.25))

    hz, hx = PZ // 2, PX // 2
    nothing = jnp.zeros((C1, GY), BF16)
    pooled = [v.astype(BF16) for v in pooled]
    for dz in range(3):
        for dx in range(3):
            r = (dz * 3 + dx) * C1
            for z in range(hz):
                for x in range(hx):
                    sz, sx = z + dz - 1, x + dx - 1
                    inside = 0 <= sz < hz and 0 <= sx < hx
                    b = z * hx + x
                    colsd[r : r + C1, b * GY : (b + 1) * GY] = pooled[sz * hx + sx] if inside else nothing
    depth = 9 * C1
    colsd[depth : depth + C1, :] = jnp.zeros((C1, small), BF16)
    products = mm(w_down[...], colsd[0:depth, :])
    lane128 = lax.broadcasted_iota(jnp.int32, (C2, GY), 1)

    def later(v):
        return jnp.where(lane128 == 0, 0.0, pltpu.roll(v, 1, 1))

    def sooner(v):
        return jnp.where(lane128 == GY - 1, 0.0, pltpu.roll(v, GY - 1, 1))

    summed = []
    for b in range(hz * hx):
        v = block(products, b)
        summed.append(later(v[0:C2]) + v[C2 : 2 * C2] + sooner(v[2 * C2 : 3 * C2]))
    value, slope_down = silu_and_slope(jnp.concatenate(summed, axis=1))
    coarse = value.astype(BF16)
    value, slope_deep = silu_and_slope(mm(w_deep[...], coarse))
    deeper = value.astype(BF16)
    merge_fine = w_fine[...]
    lifted = mm(w_coarse[...], deeper)

    out_col = w_proj_col[...]
    fine_t = w_fine_t[...]
    d_out = jnp.zeros((C1, GY), F32)
    gathered = [None] * (hz * hx)
    forecast = []
    for z in range(PZ):
        here = slice(z * plane, (z + 1) * plane)
        two = l2[:, here]
        added = [block(lifted, (z // 2) * hx + x // 2) for x in range(PX)]
        value, slope = silu_and_slope(mm(merge_fine, two) + jnp.concatenate(added, axis=1))
        merged = value.astype(BF16)
        held = merged.astype(F32)
        predicted = jnp.zeros((PX, GY), F32)
        for x in range(PX):
            summed = jnp.sum(block(held, x) * out_col, axis=0, keepdims=True)
            predicted = jnp.where(row8 == x, summed, predicted)
        forecast.append(predicted)
        misfit = (predicted - rounded(patch_ref[2, z])) * scale
        for x in range(PX):
            d_out = d_out + block(held, x) * misfit[x : x + 1, :]
        d_merged = jnp.concatenate([out_col * misfit[x : x + 1, :] for x in range(PX)], axis=1)
        dz = rounded(d_merged) * slope
        for x in range(PX):
            b = (z // 2) * hx + x // 2
            gathered[b] = block(dz, x) if gathered[b] is None else gathered[b] + block(dz, x)
        dz = dz.astype(BF16)
        dz_ref[:, here] = dz

    half = PZ * PX // 2
    packet[0:half, :] = jnp.concatenate(forecast[0 : PZ // 2], axis=0).astype(BF16)
    packet[half : 2 * half, :] = jnp.concatenate(forecast[PZ // 2 : PZ], axis=0).astype(BF16)
    packet[2 * half : 2 * half + 16, :] = slot_tile[...]
    for d in range(1, n_hi):
        peer, device = in_part(d)
        send(packet, pbuf.at[d], s3, r3, device)
    packets = group(pbuf.at[pl.ds(1, n_hi - 1)], s3, r3, device)
    pbuf[0] = packet[...]

    d_lifted = jnp.concatenate(gathered, axis=1).astype(BF16)
    d_deeper = mm(w_coarse_t[...], d_lifted)
    dz_deep = (rounded(d_deeper) * slope_deep).astype(BF16)
    d_coarse = mm(w_deep_t[...], dz_deep)
    dz_down = (rounded(d_coarse) * slope_down).astype(BF16)

    r_ = lax.broadcasted_iota(jnp.int32, (C2, C2), 0)
    c_ = lax.broadcasted_iota(jnp.int32, (C2, C2), 1)
    parted = jnp.where(r_ < C1, 2 * r_, 2 * r_ - (C2 - 1)) == c_
    dz_parted = mm(parted.astype(BF16), dz_down)
    blocks = [block(dz_parted, b) for b in range(hz * hx)]
    dz_shifts = jnp.concatenate(
        [
            jnp.concatenate([f(v) for v in blocks], axis=1).astype(BF16)
            for f in (sooner, lambda v: v, later)
        ],
        axis=0,
    )
    d_down = mm(dz_shifts, colsd[...], NT)
    low = lane64 < C1
    turned_chunks = {}

    def piece(h, lanes_low):
        odd, h = divmod(h, 27)
        zx, dy = divmod(h, 3)
        q, high = divmod(zx, 2)
        r = dy * C2 + odd * C1
        chunk = d_down[r : r + C1, q * GY : (q + 1) * GY]
        if bool(high) != lanes_low:
            return chunk
        if (r, q) not in turned_chunks:
            turned_chunks[r, q] = pltpu.roll(chunk, C1, 1)
        return turned_chunks[r, q]

    base = 27 + 32
    for j in range(27):
        pack[pl.ds(base + j, C1, stride=27), :] = jnp.where(
            low, piece(2 * j, True), piece(2 * j + 1, False)
        )

    per = grads.shape[2]
    first = -(-(27 + 32) // (per * n_lo))
    top = n_hi - (27 + 32 + 27 * C1) // (per * n_lo)
    tail = first + top

    def emit(hi_):
        for lo_ in range(n_lo):
            start = (hi_ * n_lo + lo_) * per
            grads[lo_, (hi_ + top) % n_hi] = pack[start : start + per, :].astype(BF16)

    for h in range(first, n_hi - top):
        emit(h)

    def scatter(begin, count, i):
        part = pl.ds(begin, count)
        for d in range(1, n_lo):
            peer, device = in_line(d)
            send(grads.at[peer, part], buf1.at[d - 1, part], s1.at[i], r1.at[i], device)
        return group(buf1.at[:, part], s1.at[i], r1.at[i], device)

    early = scatter(tail, n_hi - tail, 0)

    def twice(x):
        pair[:, 0:C1] = x
        pair[:, C1:GY] = jnp.zeros((C1, GY - C1), F32)
        once = pair[...]
        return once + pltpu.roll(once, C1, 1)

    d_coarse_merge = mm(d_lifted, deeper, NT)
    d_deep = mm(dz_deep, coarse, NT)
    d_fine = twice(mm(dz_ref[...], l2[...], NT))
    low32 = lax.broadcasted_iota(jnp.int32, (32, GY), 1) < C1
    base = 27 + 32 + 27 * C1
    pack[base : base + C2, :] = d_deep
    base = base + C2
    pair[...] = d_fine
    fine_even_odd = [pair[pl.ds(i, 32, stride=2), :] for i in range(2)]
    pair[...] = d_coarse_merge
    coarse_even_odd = [pair[pl.ds(i, 32, stride=2), :] for i in range(2)]
    turn = pltpu.roll(coarse_even_odd[0], C1, 1)
    pack[pl.ds(base, 32, stride=3), :] = jnp.where(low32, fine_even_odd[0], turn)
    pack[pl.ds(base + 1, 32, stride=3), :] = jnp.where(low32, turn, fine_even_odd[1])
    pack[pl.ds(base + 2, 32, stride=3), :] = coarse_even_odd[1]
    base = base + 96
    column = jnp.sum(d_out, axis=1, keepdims=True)
    across_ = lane64 == lax.broadcasted_iota(jnp.int32, (C1, GY), 0)
    pack[base : base + 1, :] = jnp.sum(
        jnp.where(across_, jnp.broadcast_to(column, (C1, GY)), 0.0), axis=0, keepdims=True
    )
    pack[base + 1 : GROWS, :] = jnp.zeros((GROWS - base - 1, GY), F32)


    blank = jnp.zeros((C2, GY), BF16)
    for dz in range(3):
        for dx in range(3):
            j = dz * 3 + dx
            for z in range(hz):
                for x in range(hx):
                    sz, sx = z - (dz - 1), x - (dx - 1)
                    inside = 0 <= sz < hz and 0 <= sx < hx
                    b = z * hx + x
                    colsz[j * C2 : (j + 1) * C2, b * GY : (b + 1) * GY] = (
                        block(dz_down, sz * hx + sx) if inside else blank
                    )
    d_shifted = mm(wback[...], colsz[...])
    d_pooled = []
    for b in range(hz * hx):
        whole = block(d_shifted, b)
        total = whole[C1 : 2 * C1]
        total = total + jnp.where(lane64 == GY - 1, 0.0, pltpu.roll(whole[0:C1], GY - 1, 1))
        total = total + jnp.where(lane64 == 0, 0.0, pltpu.roll(whole[2 * C1 : 3 * C1], 1, 1))
        d_pooled.append(rounded(total) * 0.25)

    lift_t = w_lift_t[...]
    d_stem = jnp.zeros((C1, C1), F32)
    for z in range(PZ):
        here = slice(z * plane, (z + 1) * plane)
        spread = jnp.concatenate([d_pooled[(z // 2) * hx + x // 2] for x in range(PX)], axis=1)
        dz = ((rounded(mm(fine_t, dz_ref[:, here])) + spread) * g2[:, here]).astype(BF16)
        dz2_ref[:, here] = dz
        d_one = rounded(mm(lift_t, dz))
        dz = (d_one * g1[:, here]).astype(BF16)
        d_stem = d_stem + mm(dz, cols[:, here], NT)

    d_lift = twice(mm(dz2_ref[...], l1[...], NT))

    pair[:, 0:C1] = d_stem
    pair[:, C1:GY] = jnp.zeros((C1, GY - C1), F32)
    turned = pair[...]
    source = lax.broadcasted_iota(jnp.int32, (C1, GY), 0)
    for bit in range(6):
        moved = pltpu.roll(turned, (taps << bit) % GY, 1)
        turned = jnp.where((source >> bit) % 2 == 1, moved, turned)
    begin = source * taps
    wraps = lane64 < begin % GY
    stay = jnp.where(wraps, 0.0, turned).astype(BF16)
    over = jnp.where(wraps, turned, 0.0).astype(BF16)
    target_row = lax.broadcasted_iota(jnp.int32, (32, C1), 0)
    owner = lax.broadcasted_iota(jnp.int32, (32, C1), 1) * taps // GY
    stem_rows = mm((target_row == owner).astype(BF16), stay)
    stem_rows = stem_rows + mm((target_row == owner + 1).astype(BF16), over)
    pack[0:27, :] = stem_rows[0:27, :]

    low32 = lax.broadcasted_iota(jnp.int32, (32, GY), 1) < C1
    pair[...] = d_lift
    pack[27 : 27 + 32, :] = jnp.where(low32, pair[pl.ds(0, 32, stride=2), :], pair[pl.ds(1, 32, stride=2), :])


    for h in list(range(first)) + list(range(n_hi - top, n_hi)):
        emit(h)
    late = scatter(0, tail, 1)

    def line_sum(h):
        at = (h + top) % n_hi
        value = grads[lo, at].astype(F32)
        for d in range(n_lo - 1):
            value = value + buf1[d, at].astype(F32)
        acc[h] = value.astype(BF16)

    early.wait_recv()
    for h in range(first, n_hi - top):
        line_sum(h)
    late.wait_recv()
    for h in list(range(first)) + list(range(n_hi - top, n_hi)):
        line_sum(h)
    ring = 8
    far_first = sorted(range(1, n_hi + 1), key=lambda e: (e == n_hi, -min(e % ring, ring - e % ring)))
    for e in far_first:
        h = lax.rem(hi + e, n_hi)
        for q in range(n_sec):
            if e == n_hi and q == 0:
                buf2[mine] = acc[h]
                continue
            owner = lax.rem(sec + q, n_sec)
            device = (owner, h * n_lo + lo)
            send(acc.at[h], buf2.at[mine], s2, r2, device)
    partials = group(buf2.at[pl.ds(0, across - 1)], s2, r2, device)

    packets.wait_recv()
    rows = PZ * PX

    def route(q, carry):
        wanted = (hi * (2 * n_lo) + q).astype(F32)
        value = jnp.zeros((rows, GY), F32)
        for src in range(n_hi):
            named = pbuf[src, rows : rows + 16, :].astype(F32)
            named = jnp.concatenate([named] * (rows // 16), axis=0)
            value = value + jnp.where(named == wanted, pbuf[src, 0:rows, :].astype(F32), 0.0)
        q_ref[q] = value.astype(BF16)
        return carry

    lax.fori_loop(0, 2 * n_lo, route, 0)
    for d in range(1, n_lo):
        peer, device = in_line(d)
        send(q_ref.at[pl.ds(2 * peer, 2)], qbuf.at[d - 1], s4, r4, device)
    routed = group(qbuf, s4, r4, device)

    routed.wait_recv()
    for s in range(2):
        value = q_ref[2 * lo + s].astype(F32)
        for d in range(n_lo - 1):
            value = value + qbuf[d, s].astype(F32)
        pred_out[s] = value

    partials.wait_recv()
    for copy in (packets, early, late, routed, partials):
        copy.wait_send()


def whole_kernel(n_sec, n_hi, n_lo, scale, *refs):
    ins, refs = refs[:11], refs[11:]
    (heat_out, pred_out, buf2), refs = refs[:3], refs[3:]
    made, refs = refs[:14], refs[14:]
    heat_scratch, train_scratch = refs[:14], refs[14:]
    sec = lax.axis_index("section")
    dp = lax.axis_index("dp")
    hi = lax.div(dp, n_lo)
    lo = lax.rem(dp, n_lo)
    across = n_sec * n_hi
    mine = sec * n_hi + hi
    n_dp = n_hi * n_lo
    total = n_sec * n_dp
    me = sec * n_dp + dp
    barrier = pltpu.get_barrier_semaphore()
    at_start = jnp.logical_and(lo == 0, me > 0)
    at_end = jnp.logical_and(lo == n_lo - 1, me < total - 1)
    outside = jnp.logical_or(at_start, at_end)

    def signal(section, index):
        pl.semaphore_signal(barrier, inc=1, device_id=(section, index), device_id_type=MESH)

    def enter():
        @pl.when(at_start)
        def _():
            signal(lax.div(me - 1, n_dp), lax.rem(me - 1, n_dp))

        @pl.when(at_end)
        def _():
            signal(lax.div(me + 1, n_dp), lax.rem(me + 1, n_dp))

        for d in sorted(range(1, across), key=lambda d: (d % 8 == 0, d % 8)):
            peer = lax.rem(mine + d, across)
            signal(lax.div(peer, n_hi), lax.rem(peer, n_hi) * n_lo + lo)
        for d in range(1, n_lo):
            signal(sec, hi * n_lo + lax.rem(lo + d, n_lo))

    def ready():
        peers = n_lo - 1 + across - 1

        @pl.when(outside)
        def _():
            pl.semaphore_wait(barrier, peers + 1)

        @pl.when(jnp.logical_not(outside))
        def _():
            pl.semaphore_wait(barrier, peers)

    heat_part(enter, ready, n_sec, n_dp, *ins, heat_out, *made, *heat_scratch)
    patch, *weights, slot_tile = made
    train_part(scale, n_sec, n_hi, n_lo, slot_tile, patch, *weights, pred_out, buf2, *train_scratch)


def whole(scale, n_sec, n_hi, n_lo, heat, cond, patch_z, patch_x, slot, weights):
    layers = (2,) + heat.shape[1:]
    taps = weights[0].shape[0]
    cells = PZ * PX * GY
    small = cells // 4
    per = GROWS // (n_lo * n_hi)
    across = n_sec * n_hi
    dma = pltpu.SemaphoreType.DMA
    operands = (heat, cond, *weights)
    operands = [pltpu.with_memory_space_constraint(x, pltpu.HBM) for x in operands]
    return pl.pallas_call(
        functools.partial(whole_kernel, n_sec, n_hi, n_lo, scale),
        out_shape=(
            jax.ShapeDtypeStruct(heat.shape, F32),
            jax.ShapeDtypeStruct((2, PZ * PX, GY), F32),
            jax.ShapeDtypeStruct((across, per, GY), BF16),
        ),
        in_specs=[SMEM] * 3 + [HBM] * 8,
        out_specs=(VMEM,) * 3,
        scratch_shapes=[
            pltpu.VMEM((3, PZ, PX, GY), F32),
            pltpu.VMEM((C1, taps), BF16),
            pltpu.VMEM((C1, C1), BF16),
            pltpu.VMEM((C1, C1), BF16),
            pltpu.VMEM((3 * C2, 9 * C1), BF16),
            pltpu.VMEM((3 * C1, 9 * C2), BF16),
            pltpu.VMEM((C2, C2), BF16),
            pltpu.VMEM((C2, C2), BF16),
            pltpu.VMEM((C1, C1), BF16),
            pltpu.VMEM((C1, C1), BF16),
            pltpu.VMEM((C1, C2), BF16),
            pltpu.VMEM((C2, C1), BF16),
            pltpu.VMEM((C1, GY), F32),
            pltpu.VMEM((16, GY), BF16),
            pltpu.VMEM(weights[0].shape, BF16),
            pltpu.VMEM(weights[2].shape, BF16),
            pltpu.VMEM(weights[4].shape, BF16),
            pltpu.VMEM(weights[5].shape, BF16),
            pltpu.VMEM(heat.shape, F32),
            pltpu.VMEM(heat.shape, F32),
            pltpu.VMEM(layers, F32),
            pltpu.VMEM(layers, F32),
            pltpu.VMEM(layers, F32),
            pltpu.VMEM(layers, F32),
            pltpu.VMEM((heat.shape[0] + 2,) + heat.shape[1:], F32),
            dma((8,)),
            dma((4,)),
            dma((4,)),
            pltpu.VMEM((PZ * PX * C1, GY), F32),
            pltpu.VMEM((C1, cells), BF16),
            pltpu.VMEM((C1, cells), BF16),
            pltpu.VMEM((C1, cells), BF16),
            pltpu.VMEM((C1, cells), F32),
            pltpu.VMEM((C1, cells), F32),
            pltpu.VMEM((C1, cells), BF16),
            pltpu.VMEM((C1, cells), BF16),
            pltpu.VMEM((10 * C1, small), BF16),
            pltpu.VMEM((9 * C2, small), BF16),
            pltpu.VMEM((GROWS, GY), F32),
            pltpu.VMEM((C1, GY), F32),
            pltpu.VMEM((n_lo, n_hi, per, GY), BF16),
            pltpu.VMEM((PZ * PX + 16, GY), BF16),
            pltpu.VMEM((n_lo - 1, n_hi, per, GY), BF16),
            pltpu.VMEM((n_hi, per, GY), BF16),
            pltpu.VMEM((n_hi, PZ * PX + 16, GY), BF16),
            pltpu.VMEM((2 * n_lo, PZ * PX, GY), BF16),
            pltpu.VMEM((n_lo - 1, 2, PZ * PX, GY), BF16),
            dma((2,)),
            dma((2,)),
            dma,
            dma,
            dma,
            dma,
            dma,
            dma,
        ],
        compiler_params=pltpu.CompilerParams(
            collective_id=0, has_side_effects=True, vmem_limit_bytes=48 * 2**20
        ),
        name="whole",
    )(patch_z, patch_x, slot, *operands)


def finish_kernel(heat_in, pred_in, grad_in, heat_out, pred_out, grad_out, done):
    copy = pltpu.make_async_copy(heat_in, heat_out, done)
    copy.start()
    total = grad_in[0].astype(F32)
    for t in range(1, grad_in.shape[0]):
        total = total + grad_in[t].astype(F32)
    grad_out[...] = total
    for s in range(2):
        for z in range(PZ):
            pred_out[s, z] = pred_in[s, z * PX : (z + 1) * PX, :].astype(BF16)
    copy.wait()


def finish(heat, preds, partials):
    return pl.pallas_call(
        finish_kernel,
        out_shape=(
            jax.ShapeDtypeStruct(heat.shape, F32),
            jax.ShapeDtypeStruct((2, PZ, PX, GY), BF16),
            jax.ShapeDtypeStruct(partials.shape[1:], F32),
        ),
        in_specs=[pl.BlockSpec(memory_space=pl.ANY), VMEM, VMEM],
        out_specs=(HBM, VMEM, VMEM),
        scratch_shapes=[pltpu.SemaphoreType.DMA],
        compiler_params=pltpu.CompilerParams(vmem_limit_bytes=8 * 2**20),
        name="finish",
    )(heat, preds, partials)


def local(
    n_sec,
    n_dp,
    heat_start,
    conductivity,
    patch_z,
    patch_x,
    slot_table,
    w_stem,
    w_lift,
    w_down,
    w_deep,
    w_merge,
    w_out,
):
    n_lo = LINE
    n_hi = n_dp // n_lo
    weights = (w_stem.T, w_lift, w_down.T, w_deep, w_merge, w_out)
    scale = 1.0 / (n_sec * n_dp * PZ * PX * GY)
    heat_two, preds, partials = whole(
        scale, n_sec, n_hi, n_lo, heat_start, conductivity, patch_z, patch_x, slot_table, weights
    )
    return finish(heat_two, preds, partials)


def solution(mesh):
    n_sec, n_dp = mesh.shape["section"], mesh.shape["dp"]
    both = ("section", "dp")
    return jax.shard_map(
        functools.partial(local, n_sec, n_dp),
        mesh=mesh,
        in_specs=(P(both, None, None), P(both, None, None), P(both), P(both), P(both)) + (P(),) * 6,
        out_specs=(P(both, None, None), P(both, None, None, None), P("dp", None)),
        check_vma=False,
    )
```

```python
import functools

import jax
import jax.numpy as jnp
from jax import lax
from jax.experimental import pallas as pl
from jax.experimental.pallas import tpu as pltpu
from jax.sharding import PartitionSpec as P

MESH = pl.DeviceIdType.MESH
TIME_STEP = 0.15
GY = 128
PZ = 4
PX = 8
C1 = 64
C2 = 128
GROWS = 2048
LINE = 8
F32 = jnp.float32
BF16 = jnp.bfloat16
VMEM = pl.BlockSpec(memory_space=pltpu.VMEM)
SMEM = pl.BlockSpec(memory_space=pltpu.SMEM)
HBM = pl.BlockSpec(memory_space=pltpu.HBM)


def rounded(x):
    return x.astype(BF16).astype(F32)


NT = (((1,), (1,)), ((), ()))
NN = (((1,), (0,)), ((), ()))


def mm(a, b, dims=NN):
    return lax.dot_general(a, b, dims, preferred_element_type=F32)


def heat_part(
    enter,
    ready,
    meanwhile,
    n_sec,
    n_dp,
    pz_ref,
    px_ref,
    slot_ref,
    u_hbm,
    k_hbm,
    stem_hbm,
    lift_hbm,
    down_hbm,
    deep_hbm,
    merge_hbm,
    proj_hbm,
    out_ref,
    patch_ref,
    stem_ref,
    lift_ref,
    lift_t,
    down_ref,
    down_back,
    deep_ref,
    deep_t,
    fine_ref,
    fine_t,
    coarse_ref,
    coarse_t,
    proj_col,
    slot_tile,
    v_stem,
    v_down,
    v_merge,
    v_proj,
    u_ref,
    k_ref,
    ulo,
    klo,
    uhi,
    khi,
    h1,
    load,
    send,
    recv,
):
    total = n_sec * n_dp
    depth = u_ref.shape[0]
    me = lax.axis_index("section") * n_dp + lax.axis_index("dp")
    after = lax.rem(me + 1, total)
    before = lax.rem(me + total - 1, total)

    def place(i):
        return (lax.div(i, n_dp), lax.rem(i, n_dp))

    below, above = me > 0, me < total - 1
    enter()
    loads = [
        pltpu.make_async_copy(u_hbm, u_ref, load.at[0]),
        pltpu.make_async_copy(k_hbm, k_ref, load.at[1]),
        pltpu.make_async_copy(down_hbm, v_down, load.at[2]),
        pltpu.make_async_copy(stem_hbm, v_stem, load.at[3]),
        pltpu.make_async_copy(lift_hbm, lift_ref, load.at[4]),
        pltpu.make_async_copy(deep_hbm, deep_ref, load.at[5]),
        pltpu.make_async_copy(merge_hbm, v_merge, load.at[6]),
        pltpu.make_async_copy(proj_hbm, v_proj, load.at[7]),
    ]
    for copy in loads:
        copy.start()
    ready()
    plan = (
        (u_hbm.at[pl.ds(depth - 2, 2)], ulo, after),
        (k_hbm.at[pl.ds(depth - 2, 2)], klo, after),
        (u_hbm.at[pl.ds(0, 2)], uhi, before),
        (k_hbm.at[pl.ds(0, 2)], khi, before),
    )
    copies = [
        pltpu.make_async_remote_copy(
            src_ref=src,
            dst_ref=dst,
            send_sem=send.at[i],
            recv_sem=recv.at[i],
            device_id=place(peer),
            device_id_type=MESH,
        )
        for i, (src, dst, peer) in enumerate(plan)
    ]
    upward, downward = copies[0:2], copies[2:4]

    @pl.when(above)
    def _():
        for copy in upward:
            copy.start()

    @pl.when(below)
    def _():
        for copy in downward:
            copy.start()

    @pl.when(me == 0)
    def _():
        ulo[...] = jnp.zeros_like(ulo)
        klo[...] = jnp.zeros_like(klo)

    @pl.when(me == total - 1)
    def _():
        uhi[...] = jnp.zeros_like(uhi)
        khi[...] = jnp.zeros_like(khi)

    rows, lanes = u_ref.shape[1:]
    row = lax.broadcasted_iota(jnp.int32, (rows, lanes), 0)
    lane = lax.broadcasted_iota(jnp.int32, (rows, lanes), 1)

    def step(up, uc, un, kp, kc, kn):
        flux = (kc + kn) * (un - uc) + (kc + kp) * (up - uc)
        for axis, place_, size in ((0, row, rows), (1, lane, lanes)):
            last = place_ == size - 1
            first = place_ == 0
            u_next = jnp.where(last, 0.0, pltpu.roll(uc, size - 1, axis))
            k_next = jnp.where(last, 0.0, pltpu.roll(kc, size - 1, axis))
            face = (kc + k_next) * (u_next - uc)
            back = jnp.where(first, kc * uc, pltpu.roll(face, 1, axis))
            flux = flux + (face - back)
        return uc + (0.5 * TIME_STEP) * flux

    for copy in loads:
        copy.wait()
    group = 7

    def interior(i, carry):
        for j in range(group):
            z = 1 + i * group + j
            h1[z + 1] = step(
                u_ref[z - 1], u_ref[z], u_ref[z + 1], k_ref[z - 1], k_ref[z], k_ref[z + 1]
            )
        return carry

    lax.fori_loop(0, (depth - 2) // group, interior, 0)

    def second(z):
        out_ref[z] = step(h1[z], h1[z + 1], h1[z + 2], k_ref[z - 1], k_ref[z], k_ref[z + 1])

    pack = 6

    def inner(i, carry):
        for j in range(pack):
            second(2 + i * pack + j)
        return carry

    lax.fori_loop(0, (depth - 4) // pack, inner, 0)
    unit = lax.broadcasted_iota(jnp.int32, (C2, C2), 0) == lax.broadcasted_iota(jnp.int32, (C2, C2), 1)
    eye = unit[0:C1, 0:C1]
    unit = unit.astype(BF16)
    stem_ref[...] = mm(unit[0:C1, 0:C1], v_stem[...], NT).astype(BF16)
    for dy in range(3):
        starts = [(j * 3 + dy) * C1 for j in range(9)]
        part = jnp.concatenate([v_down[r : r + C1, :] for r in starts], axis=0)
        down_ref[dy * C2 : (dy + 1) * C2, :] = mm(unit, part, NT).astype(BF16)
    for j in range(9):
        down_back[:, j * C2 : (j + 1) * C2] = v_down[j * 3 * C1 : (j + 1) * 3 * C1, :]

    def turned(x):
        return x.astype(F32).T.astype(BF16)

    lift_t[...] = turned(lift_ref[...])
    slot_tile[...] = jnp.full((16, GY), slot_ref[0].astype(F32)).astype(BF16)
    deep_t[...] = turned(deep_ref[...])
    fine = v_merge[:, 0:C1]
    coarse = v_merge[:, C1 : C1 + C2]
    fine_ref[...] = fine
    fine_t[...] = turned(fine)
    coarse_ref[...] = coarse
    coarse_t[...] = turned(coarse)
    row64 = v_proj[...].astype(F32)
    column = jnp.sum(jnp.where(eye, jnp.broadcast_to(row64, (C1, C1)), 0.0), axis=1, keepdims=True)
    proj_col[...] = jnp.broadcast_to(column, proj_col.shape)

    pz = pz_ref[0]
    px = px_ref[0]
    for z in range(PZ):
        patch_ref[1, z] = k_ref[pz + z, pl.ds(px, PX), :]
    meanwhile()

    @pl.when(below)
    def _():
        for copy in upward:
            copy.wait_recv()

    @pl.when(above)
    def _():
        for copy in downward:
            copy.wait_recv()

    has_lo = (me > 0).astype(F32)
    has_hi = (me < total - 1).astype(F32)
    ul, kl, uh, kh = ulo, klo, uhi, khi
    end = depth - 1
    h1[0] = has_lo * step(ul[0], ul[1], u_ref[0], kl[0], kl[1], k_ref[0])
    h1[1] = step(ul[1], u_ref[0], u_ref[1], kl[1], k_ref[0], k_ref[1])
    h1[depth] = step(u_ref[end - 1], u_ref[end], uh[0], k_ref[end - 1], k_ref[end], kh[0])
    h1[depth + 1] = has_hi * step(u_ref[end], uh[0], uh[1], k_ref[end], kh[0], kh[1])

    out_ref[0] = step(h1[0], h1[1], h1[2], kl[1], k_ref[0], k_ref[1])
    out_ref[end] = step(h1[end], h1[depth], h1[depth + 1], k_ref[end - 1], k_ref[end], kh[0])
    second(1)
    second(end - 1)
    for z in range(PZ):
        patch_ref[0, z] = h1[1 + pz + z, pl.ds(px, PX), :]
        patch_ref[2, z] = out_ref[pz + z, pl.ds(px, PX), :]

    @pl.when(above)
    def _():
        for copy in upward:
            copy.wait_send()

    @pl.when(below)
    def _():
        for copy in downward:
            copy.wait_send()


def silu_and_slope(z):
    s = 0.5 * jnp.tanh(0.5 * z) + 0.5
    value = z * s
    return value, s + value * (1.0 - s)


def block(x, b):
    return x[:, b * GY : (b + 1) * GY]


def stem_columns(patch_ref, tall, channel):
    row8 = lax.broadcasted_iota(jnp.int32, (PX, GY), 0)
    lane8 = lax.broadcasted_iota(jnp.int32, (PX, GY), 1)
    for dx in range(3):
        for dy in range(3):
            shifted = []
            for z in range(PZ):
                v = rounded(patch_ref[channel, z])
                if dx == 0:
                    v = jnp.where(row8 == 0, 0.0, pltpu.roll(v, 1, 0))
                elif dx == 2:
                    v = jnp.where(row8 == PX - 1, 0.0, pltpu.roll(v, PX - 1, 0))
                if dy == 0:
                    v = jnp.where(lane8 == 0, 0.0, pltpu.roll(v, 1, 1))
                elif dy == 2:
                    v = jnp.where(lane8 == GY - 1, 0.0, pltpu.roll(v, GY - 1, 1))
                shifted.append(v)
            for dz in range(3):
                r = ((dz * 3 + dx) * 3 + dy) * 2 + channel
                for z in range(PZ):
                    if 0 <= z + dz - 1 < PZ:
                        tall[pl.ds(z * PX * C1 + r, PX, stride=C1), :] = shifted[z + dz - 1]


def train_part(
    scale,
    n_sec,
    n_hi,
    n_lo,
    slot_tile,
    patch_ref,
    w_stem,
    w_lift,
    w_lift_t,
    w_down,
    wback,
    w_deep,
    w_deep_t,
    w_fine,
    w_fine_t,
    w_coarse,
    w_coarse_t,
    w_proj_col,
    pred_out,
    buf2,
    tall,
    cols,
    l1,
    l2,
    g1,
    g2,
    dz_ref,
    dz2_ref,
    colsd,
    colsz,
    pack,
    pair,
    grads,
    packet,
    buf1,
    acc,
    pbuf,
    q_ref,
    qbuf,
    s1,
    r1,
    s2,
    r2,
    s3,
    r3,
    s4,
    r4,
):
    sec = lax.axis_index("section")
    dp = lax.axis_index("dp")
    hi = lax.div(dp, n_lo)
    lo = lax.rem(dp, n_lo)
    across = n_sec * n_hi
    mine = sec * n_hi + hi

    def in_line(d):
        peer = lax.rem(lo + d, n_lo)
        return peer, (sec, hi * n_lo + peer)

    def in_column(d):
        peer = lax.rem(mine + d, across)
        return peer, (lax.div(peer, n_hi), lax.rem(peer, n_hi) * n_lo + lo)

    def in_part(d):
        peer = lax.rem(hi + d, n_hi)
        return peer, (sec, peer * n_lo + lo)

    def send(src, dst, ssem, rsem, device):
        copy = pltpu.make_async_remote_copy(
            src_ref=src, dst_ref=dst, send_sem=ssem, recv_sem=rsem, device_id=device, device_id_type=MESH
        )
        copy.start()
        return copy

    def group(like, ssem, rsem, device):
        return pltpu.make_async_remote_copy(
            src_ref=like, dst_ref=like, send_sem=ssem, recv_sem=rsem, device_id=device, device_id_type=MESH
        )

    plane = PX * GY
    cells = PZ * plane
    small = cells // 4
    row8 = lax.broadcasted_iota(jnp.int32, (PX, GY), 0)
    lane8 = lax.broadcasted_iota(jnp.int32, (PX, GY), 1)
    lane64 = lax.broadcasted_iota(jnp.int32, (C1, GY), 1)

    stem_columns(patch_ref, tall, 0)
    for b in range(PZ * PX):
        cols[:, b * GY : (b + 1) * GY] = tall[b * C1 : (b + 1) * C1, :].astype(BF16)

    taps = w_stem.shape[1]
    stem = w_stem[...]
    lift = w_lift[...]
    pooled = []
    for zz in range(PZ // 2):
        rows = []
        for z in (2 * zz, 2 * zz + 1):
            here = slice(z * plane, (z + 1) * plane)
            value, slope = silu_and_slope(mm(stem, cols[0:taps, here]))
            g1[:, here] = slope
            one = value.astype(BF16)
            l1[:, here] = one
            value, slope = silu_and_slope(mm(lift, one))
            g2[:, here] = slope
            two = value.astype(BF16)
            l2[:, here] = two
            rows.append(two.astype(F32))
        both = rows[0] + rows[1]
        for xx in range(PX // 2):
            pooled.append(rounded((block(both, 2 * xx) + block(both, 2 * xx + 1)) * 0.25))

    hz, hx = PZ // 2, PX // 2
    pooled = [v.astype(BF16) for v in pooled]
    for dz in range(3):
        for dx in range(3):
            r = (dz * 3 + dx) * C1
            for z in range(hz):
                for x in range(hx):
                    sz, sx = z + dz - 1, x + dx - 1
                    inside = 0 <= sz < hz and 0 <= sx < hx
                    b = z * hx + x
                    if inside:
                        colsd[r : r + C1, b * GY : (b + 1) * GY] = pooled[sz * hx + sx]
    depth = 9 * C1
    products = mm(w_down[...], colsd[0:depth, :])
    lane128 = lax.broadcasted_iota(jnp.int32, (C2, GY), 1)

    def later(v):
        return jnp.where(lane128 == 0, 0.0, pltpu.roll(v, 1, 1))

    def sooner(v):
        return jnp.where(lane128 == GY - 1, 0.0, pltpu.roll(v, GY - 1, 1))

    summed = []
    for b in range(hz * hx):
        v = block(products, b)
        summed.append(later(v[0:C2]) + v[C2 : 2 * C2] + sooner(v[2 * C2 : 3 * C2]))
    value, slope_down = silu_and_slope(jnp.concatenate(summed, axis=1))
    coarse = value.astype(BF16)
    value, slope_deep = silu_and_slope(mm(w_deep[...], coarse))
    deeper = value.astype(BF16)
    merge_fine = w_fine[...]
    lifted = mm(w_coarse[...], deeper)

    out_col = w_proj_col[...]
    fine_t = w_fine_t[...]
    d_out = jnp.zeros((C1, GY), F32)
    gathered = [None] * (hz * hx)
    forecast = []
    for z in range(PZ):
        here = slice(z * plane, (z + 1) * plane)
        two = l2[:, here]
        added = [block(lifted, (z // 2) * hx + x // 2) for x in range(PX)]
        value, slope = silu_and_slope(mm(merge_fine, two) + jnp.concatenate(added, axis=1))
        merged = value.astype(BF16)
        held = merged.astype(F32)
        predicted = jnp.zeros((PX, GY), F32)
        for x in range(PX):
            summed = jnp.sum(block(held, x) * out_col, axis=0, keepdims=True)
            predicted = jnp.where(row8 == x, summed, predicted)
        forecast.append(predicted)
        misfit = (predicted - rounded(patch_ref[2, z])) * scale
        for x in range(PX):
            d_out = d_out + block(held, x) * misfit[x : x + 1, :]
        d_merged = jnp.concatenate([out_col * misfit[x : x + 1, :] for x in range(PX)], axis=1)
        dz = rounded(d_merged) * slope
        for x in range(PX):
            b = (z // 2) * hx + x // 2
            gathered[b] = block(dz, x) if gathered[b] is None else gathered[b] + block(dz, x)
        dz = dz.astype(BF16)
        dz_ref[:, here] = dz

    half = PZ * PX // 2
    packet[0:half, :] = jnp.concatenate(forecast[0 : PZ // 2], axis=0).astype(BF16)
    packet[half : 2 * half, :] = jnp.concatenate(forecast[PZ // 2 : PZ], axis=0).astype(BF16)
    packet[2 * half : 2 * half + 16, :] = slot_tile[...]
    for d in range(1, n_hi):
        peer, device = in_part(d)
        send(packet, pbuf.at[d], s3, r3, device)
    packets = group(pbuf.at[pl.ds(1, n_hi - 1)], s3, r3, device)
    pbuf[0] = packet[...]

    d_lifted = jnp.concatenate(gathered, axis=1).astype(BF16)
    d_deeper = mm(w_coarse_t[...], d_lifted)
    dz_deep = (rounded(d_deeper) * slope_deep).astype(BF16)
    d_coarse = mm(w_deep_t[...], dz_deep)
    dz_down = (rounded(d_coarse) * slope_down).astype(BF16)

    r_ = lax.broadcasted_iota(jnp.int32, (C2, C2), 0)
    c_ = lax.broadcasted_iota(jnp.int32, (C2, C2), 1)
    parted = jnp.where(r_ < C1, 2 * r_, 2 * r_ - (C2 - 1)) == c_
    dz_parted = mm(parted.astype(BF16), dz_down)
    blocks = [block(dz_parted, b) for b in range(hz * hx)]
    dz_shifts = jnp.concatenate(
        [
            jnp.concatenate([f(v) for v in blocks], axis=1).astype(BF16)
            for f in (sooner, lambda v: v, later)
        ],
        axis=0,
    )
    d_down = mm(dz_shifts, colsd[...], NT)
    low = lane64 < C1
    turned_chunks = {}

    def piece(h, lanes_low):
        odd, h = divmod(h, 27)
        zx, dy = divmod(h, 3)
        q, high = divmod(zx, 2)
        r = dy * C2 + odd * C1
        chunk = d_down[r : r + C1, q * GY : (q + 1) * GY]
        if bool(high) != lanes_low:
            return chunk
        if (r, q) not in turned_chunks:
            turned_chunks[r, q] = pltpu.roll(chunk, C1, 1)
        return turned_chunks[r, q]

    base = 27 + 32
    for j in range(27):
        pack[pl.ds(base + j, C1, stride=27), :] = jnp.where(
            low, piece(2 * j, True), piece(2 * j + 1, False)
        )

    per = grads.shape[2]
    first = -(-(27 + 32) // (per * n_lo))
    top = n_hi - (27 + 32 + 27 * C1) // (per * n_lo)
    tail = first + top

    def emit(hi_):
        for lo_ in range(n_lo):
            start = (hi_ * n_lo + lo_) * per
            grads[lo_, (hi_ + top) % n_hi] = pack[start : start + per, :].astype(BF16)

    for h in range(first, n_hi - top):
        emit(h)

    def scatter(begin, count, i):
        part = pl.ds(begin, count)
        for d in range(1, n_lo):
            peer, device = in_line(d)
            send(grads.at[peer, part], buf1.at[d - 1, part], s1.at[i], r1.at[i], device)
        return group(buf1.at[:, part], s1.at[i], r1.at[i], device)

    early = scatter(tail, n_hi - tail, 0)

    def twice(x):
        pair[:, 0:C1] = x
        pair[:, C1:GY] = jnp.zeros((C1, GY - C1), F32)
        once = pair[...]
        return once + pltpu.roll(once, C1, 1)

    d_coarse_merge = mm(d_lifted, deeper, NT)
    d_deep = mm(dz_deep, coarse, NT)
    d_fine = twice(mm(dz_ref[...], l2[...], NT))
    low32 = lax.broadcasted_iota(jnp.int32, (32, GY), 1) < C1
    base = 27 + 32 + 27 * C1
    pack[base : base + C2, :] = d_deep
    base = base + C2
    pair[...] = d_fine
    fine_even_odd = [pair[pl.ds(i, 32, stride=2), :] for i in range(2)]
    pair[...] = d_coarse_merge
    coarse_even_odd = [pair[pl.ds(i, 32, stride=2), :] for i in range(2)]
    turn = pltpu.roll(coarse_even_odd[0], C1, 1)
    pack[pl.ds(base, 32, stride=3), :] = jnp.where(low32, fine_even_odd[0], turn)
    pack[pl.ds(base + 1, 32, stride=3), :] = jnp.where(low32, turn, fine_even_odd[1])
    pack[pl.ds(base + 2, 32, stride=3), :] = coarse_even_odd[1]
    base = base + 96
    column = jnp.sum(d_out, axis=1, keepdims=True)
    across_ = lane64 == lax.broadcasted_iota(jnp.int32, (C1, GY), 0)
    pack[base : base + 1, :] = jnp.sum(
        jnp.where(across_, jnp.broadcast_to(column, (C1, GY)), 0.0), axis=0, keepdims=True
    )
    pack[base + 1 : GROWS, :] = jnp.zeros((GROWS - base - 1, GY), F32)


    for dz in range(3):
        for dx in range(3):
            j = dz * 3 + dx
            for z in range(hz):
                for x in range(hx):
                    sz, sx = z - (dz - 1), x - (dx - 1)
                    inside = 0 <= sz < hz and 0 <= sx < hx
                    b = z * hx + x
                    if inside:
                        colsz[j * C2 : (j + 1) * C2, b * GY : (b + 1) * GY] = block(
                            dz_down, sz * hx + sx
                        )
    d_shifted = mm(wback[...], colsz[...])
    d_pooled = []
    for b in range(hz * hx):
        whole = block(d_shifted, b)
        total = whole[C1 : 2 * C1]
        total = total + jnp.where(lane64 == GY - 1, 0.0, pltpu.roll(whole[0:C1], GY - 1, 1))
        total = total + jnp.where(lane64 == 0, 0.0, pltpu.roll(whole[2 * C1 : 3 * C1], 1, 1))
        d_pooled.append(rounded(total) * 0.25)

    lift_t = w_lift_t[...]
    d_stem = jnp.zeros((C1, C1), F32)
    for z in range(PZ):
        here = slice(z * plane, (z + 1) * plane)
        spread = jnp.concatenate([d_pooled[(z // 2) * hx + x // 2] for x in range(PX)], axis=1)
        dz = ((rounded(mm(fine_t, dz_ref[:, here])) + spread) * g2[:, here]).astype(BF16)
        dz2_ref[:, here] = dz
        d_one = rounded(mm(lift_t, dz))
        dz = (d_one * g1[:, here]).astype(BF16)
        d_stem = d_stem + mm(dz, cols[:, here], NT)

    d_lift = twice(mm(dz2_ref[...], l1[...], NT))

    pair[:, 0:C1] = d_stem
    pair[:, C1:GY] = jnp.zeros((C1, GY - C1), F32)
    turned = pair[...]
    source = lax.broadcasted_iota(jnp.int32, (C1, GY), 0)
    for bit in range(6):
        moved = pltpu.roll(turned, (taps << bit) % GY, 1)
        turned = jnp.where((source >> bit) % 2 == 1, moved, turned)
    begin = source * taps
    wraps = lane64 < begin % GY
    stay = jnp.where(wraps, 0.0, turned).astype(BF16)
    over = jnp.where(wraps, turned, 0.0).astype(BF16)
    target_row = lax.broadcasted_iota(jnp.int32, (32, C1), 0)
    owner = lax.broadcasted_iota(jnp.int32, (32, C1), 1) * taps // GY
    stem_rows = mm((target_row == owner).astype(BF16), stay)
    stem_rows = stem_rows + mm((target_row == owner + 1).astype(BF16), over)
    pack[0:27, :] = stem_rows[0:27, :]

    low32 = lax.broadcasted_iota(jnp.int32, (32, GY), 1) < C1
    pair[...] = d_lift
    pack[27 : 27 + 32, :] = jnp.where(low32, pair[pl.ds(0, 32, stride=2), :], pair[pl.ds(1, 32, stride=2), :])


    for h in list(range(first)) + list(range(n_hi - top, n_hi)):
        emit(h)
    late = scatter(0, tail, 1)

    def line_sum(h):
        at = (h + top) % n_hi
        value = grads[lo, at].astype(F32)
        for d in range(n_lo - 1):
            value = value + buf1[d, at].astype(F32)
        acc[h] = value.astype(BF16)

    early.wait_recv()
    for h in range(first, n_hi - top):
        line_sum(h)
    late.wait_recv()
    for h in list(range(first)) + list(range(n_hi - top, n_hi)):
        line_sum(h)
    ring = 8
    far_first = sorted(range(1, n_hi + 1), key=lambda e: (e == n_hi, -min(e % ring, ring - e % ring)))
    for e in far_first:
        h = lax.rem(hi + e, n_hi)
        for q in range(n_sec):
            if e == n_hi and q == 0:
                buf2[mine] = acc[h]
                continue
            owner = lax.rem(sec + q, n_sec)
            device = (owner, h * n_lo + lo)
            send(acc.at[h], buf2.at[mine], s2, r2, device)
    partials = group(buf2.at[pl.ds(0, across - 1)], s2, r2, device)

    packets.wait_recv()
    rows = PZ * PX

    def route(q, carry):
        wanted = (hi * (2 * n_lo) + q).astype(F32)
        value = jnp.zeros((rows, GY), F32)
        for src in range(n_hi):
            named = pbuf[src, rows : rows + 16, :].astype(F32)
            named = jnp.concatenate([named] * (rows // 16), axis=0)
            value = value + jnp.where(named == wanted, pbuf[src, 0:rows, :].astype(F32), 0.0)
        q_ref[q] = value.astype(BF16)
        return carry

    lax.fori_loop(0, 2 * n_lo, route, 0)
    for d in range(1, n_lo):
        peer, device = in_line(d)
        send(q_ref.at[pl.ds(2 * peer, 2)], qbuf.at[d - 1], s4, r4, device)
    routed = group(qbuf, s4, r4, device)

    routed.wait_recv()
    for s in range(2):
        value = q_ref[2 * lo + s].astype(F32)
        for d in range(n_lo - 1):
            value = value + qbuf[d, s].astype(F32)
        pred_out[s] = value

    partials.wait_recv()
    for copy in (packets, early, late, routed, partials):
        copy.wait_send()


def whole_kernel(n_sec, n_hi, n_lo, scale, *refs):
    ins, refs = refs[:11], refs[11:]
    (heat_out, pred_out, buf2), refs = refs[:3], refs[3:]
    made, refs = refs[:14], refs[14:]
    heat_scratch, train_scratch = refs[:14], refs[14:]
    sec = lax.axis_index("section")
    dp = lax.axis_index("dp")
    hi = lax.div(dp, n_lo)
    lo = lax.rem(dp, n_lo)
    across = n_sec * n_hi
    mine = sec * n_hi + hi
    n_dp = n_hi * n_lo
    total = n_sec * n_dp
    me = sec * n_dp + dp
    barrier = pltpu.get_barrier_semaphore()
    at_start = jnp.logical_and(lo == 0, me > 0)
    at_end = jnp.logical_and(lo == n_lo - 1, me < total - 1)
    outside = jnp.logical_or(at_start, at_end)

    def signal(section, index):
        pl.semaphore_signal(barrier, inc=1, device_id=(section, index), device_id_type=MESH)

    def enter():
        @pl.when(at_start)
        def _():
            signal(lax.div(me - 1, n_dp), lax.rem(me - 1, n_dp))

        @pl.when(at_end)
        def _():
            signal(lax.div(me + 1, n_dp), lax.rem(me + 1, n_dp))

        for d in sorted(range(1, across), key=lambda d: (d % 8 == 0, d % 8)):
            peer = lax.rem(mine + d, across)
            signal(lax.div(peer, n_hi), lax.rem(peer, n_hi) * n_lo + lo)
        for d in range(1, n_lo):
            signal(sec, hi * n_lo + lax.rem(lo + d, n_lo))

    def ready():
        peers = n_lo - 1 + across - 1

        @pl.when(outside)
        def _():
            pl.semaphore_wait(barrier, peers + 1)

        @pl.when(jnp.logical_not(outside))
        def _():
            pl.semaphore_wait(barrier, peers)

    patch, *weights, slot_tile = made
    tall, colsd, colsz = train_scratch[0], train_scratch[8], train_scratch[9]

    def meanwhile():
        for cleared in (tall, colsd, colsz):
            cleared[...] = jnp.zeros_like(cleared)
        stem_columns(patch, tall, 1)

    heat_part(enter, ready, meanwhile, n_sec, n_dp, *ins, heat_out, *made, *heat_scratch)
    train_part(scale, n_sec, n_hi, n_lo, slot_tile, patch, *weights, pred_out, buf2, *train_scratch)


def whole(scale, n_sec, n_hi, n_lo, heat, cond, patch_z, patch_x, slot, weights):
    layers = (2,) + heat.shape[1:]
    taps = weights[0].shape[0]
    cells = PZ * PX * GY
    small = cells // 4
    per = GROWS // (n_lo * n_hi)
    across = n_sec * n_hi
    dma = pltpu.SemaphoreType.DMA
    operands = (heat, cond, *weights)
    operands = [pltpu.with_memory_space_constraint(x, pltpu.HBM) for x in operands]
    return pl.pallas_call(
        functools.partial(whole_kernel, n_sec, n_hi, n_lo, scale),
        out_shape=(
            jax.ShapeDtypeStruct(heat.shape, F32),
            jax.ShapeDtypeStruct((2, PZ * PX, GY), F32),
            jax.ShapeDtypeStruct((across, per, GY), BF16),
        ),
        in_specs=[SMEM] * 3 + [HBM] * 8,
        out_specs=(VMEM,) * 3,
        scratch_shapes=[
            pltpu.VMEM((3, PZ, PX, GY), F32),
            pltpu.VMEM((C1, taps), BF16),
            pltpu.VMEM((C1, C1), BF16),
            pltpu.VMEM((C1, C1), BF16),
            pltpu.VMEM((3 * C2, 9 * C1), BF16),
            pltpu.VMEM((3 * C1, 9 * C2), BF16),
            pltpu.VMEM((C2, C2), BF16),
            pltpu.VMEM((C2, C2), BF16),
            pltpu.VMEM((C1, C1), BF16),
            pltpu.VMEM((C1, C1), BF16),
            pltpu.VMEM((C1, C2), BF16),
            pltpu.VMEM((C2, C1), BF16),
            pltpu.VMEM((C1, GY), F32),
            pltpu.VMEM((16, GY), BF16),
            pltpu.VMEM(weights[0].shape, BF16),
            pltpu.VMEM(weights[2].shape, BF16),
            pltpu.VMEM(weights[4].shape, BF16),
            pltpu.VMEM(weights[5].shape, BF16),
            pltpu.VMEM(heat.shape, F32),
            pltpu.VMEM(heat.shape, F32),
            pltpu.VMEM(layers, F32),
            pltpu.VMEM(layers, F32),
            pltpu.VMEM(layers, F32),
            pltpu.VMEM(layers, F32),
            pltpu.VMEM((heat.shape[0] + 2,) + heat.shape[1:], F32),
            dma((8,)),
            dma((4,)),
            dma((4,)),
            pltpu.VMEM((PZ * PX * C1, GY), F32),
            pltpu.VMEM((C1, cells), BF16),
            pltpu.VMEM((C1, cells), BF16),
            pltpu.VMEM((C1, cells), BF16),
            pltpu.VMEM((C1, cells), F32),
            pltpu.VMEM((C1, cells), F32),
            pltpu.VMEM((C1, cells), BF16),
            pltpu.VMEM((C1, cells), BF16),
            pltpu.VMEM((10 * C1, small), BF16),
            pltpu.VMEM((9 * C2, small), BF16),
            pltpu.VMEM((GROWS, GY), F32),
            pltpu.VMEM((C1, GY), F32),
            pltpu.VMEM((n_lo, n_hi, per, GY), BF16),
            pltpu.VMEM((PZ * PX + 16, GY), BF16),
            pltpu.VMEM((n_lo - 1, n_hi, per, GY), BF16),
            pltpu.VMEM((n_hi, per, GY), BF16),
            pltpu.VMEM((n_hi, PZ * PX + 16, GY), BF16),
            pltpu.VMEM((2 * n_lo, PZ * PX, GY), BF16),
            pltpu.VMEM((n_lo - 1, 2, PZ * PX, GY), BF16),
            dma((2,)),
            dma((2,)),
            dma,
            dma,
            dma,
            dma,
            dma,
            dma,
        ],
        compiler_params=pltpu.CompilerParams(
            collective_id=0, has_side_effects=True, vmem_limit_bytes=48 * 2**20
        ),
        name="whole",
    )(patch_z, patch_x, slot, *operands)


def finish_kernel(heat_in, pred_in, grad_in, heat_out, pred_out, grad_out, done):
    copy = pltpu.make_async_copy(heat_in, heat_out, done)
    copy.start()
    total = grad_in[0].astype(F32)
    for t in range(1, grad_in.shape[0]):
        total = total + grad_in[t].astype(F32)
    grad_out[...] = total
    for s in range(2):
        for z in range(PZ):
            pred_out[s, z] = pred_in[s, z * PX : (z + 1) * PX, :].astype(BF16)
    copy.wait()


def finish(heat, preds, partials):
    return pl.pallas_call(
        finish_kernel,
        out_shape=(
            jax.ShapeDtypeStruct(heat.shape, F32),
            jax.ShapeDtypeStruct((2, PZ, PX, GY), BF16),
            jax.ShapeDtypeStruct(partials.shape[1:], F32),
        ),
        in_specs=[pl.BlockSpec(memory_space=pl.ANY), VMEM, VMEM],
        out_specs=(HBM, VMEM, VMEM),
        scratch_shapes=[pltpu.SemaphoreType.DMA],
        compiler_params=pltpu.CompilerParams(vmem_limit_bytes=8 * 2**20),
        name="finish",
    )(heat, preds, partials)


def local(
    n_sec,
    n_dp,
    heat_start,
    conductivity,
    patch_z,
    patch_x,
    slot_table,
    w_stem,
    w_lift,
    w_down,
    w_deep,
    w_merge,
    w_out,
):
    n_lo = LINE
    n_hi = n_dp // n_lo
    weights = (w_stem.T, w_lift, w_down.T, w_deep, w_merge, w_out)
    scale = 1.0 / (n_sec * n_dp * PZ * PX * GY)
    heat_two, preds, partials = whole(
        scale, n_sec, n_hi, n_lo, heat_start, conductivity, patch_z, patch_x, slot_table, weights
    )
    return finish(heat_two, preds, partials)


def solution(mesh):
    n_sec, n_dp = mesh.shape["section"], mesh.shape["dp"]
    both = ("section", "dp")
    return jax.shard_map(
        functools.partial(local, n_sec, n_dp),
        mesh=mesh,
        in_specs=(P(both, None, None), P(both, None, None), P(both), P(both), P(both)) + (P(),) * 6,
        out_specs=(P(both, None, None), P(both, None, None, None), P("dp", None)),
        check_vma=False,
    )
```

```python
import functools

import jax
import jax.numpy as jnp
from jax import lax
from jax.experimental import pallas as pl
from jax.experimental.pallas import tpu as pltpu
from jax.sharding import PartitionSpec as P

MESH = pl.DeviceIdType.MESH
TIME_STEP = 0.15
GY = 128
PZ = 4
PX = 8
C1 = 64
C2 = 128
GROWS = 2048
LINE = 8
F32 = jnp.float32
BF16 = jnp.bfloat16
VMEM = pl.BlockSpec(memory_space=pltpu.VMEM)
SMEM = pl.BlockSpec(memory_space=pltpu.SMEM)
HBM = pl.BlockSpec(memory_space=pltpu.HBM)


def rounded(x):
    return x.astype(BF16).astype(F32)


NT = (((1,), (1,)), ((), ()))
NN = (((1,), (0,)), ((), ()))


def mm(a, b, dims=NN):
    return lax.dot_general(a, b, dims, preferred_element_type=F32)


def heat_part(
    enter,
    ready,
    meanwhile,
    n_sec,
    n_dp,
    pz_ref,
    px_ref,
    slot_ref,
    u_hbm,
    k_hbm,
    stem_hbm,
    lift_hbm,
    down_hbm,
    deep_hbm,
    merge_hbm,
    proj_hbm,
    out_ref,
    patch_ref,
    stem_ref,
    lift_ref,
    lift_t,
    down_ref,
    down_back,
    deep_ref,
    deep_t,
    fine_ref,
    fine_t,
    coarse_ref,
    coarse_t,
    proj_col,
    slot_tile,
    v_stem,
    v_down,
    v_merge,
    v_proj,
    u_ref,
    k_ref,
    ulo,
    klo,
    uhi,
    khi,
    h1,
    load,
    send,
    recv,
):
    total = n_sec * n_dp
    depth = u_ref.shape[0]
    me = lax.axis_index("section") * n_dp + lax.axis_index("dp")
    after = lax.rem(me + 1, total)
    before = lax.rem(me + total - 1, total)

    def place(i):
        return (lax.div(i, n_dp), lax.rem(i, n_dp))

    below, above = me > 0, me < total - 1
    enter()
    loads = [
        pltpu.make_async_copy(u_hbm, u_ref, load.at[0]),
        pltpu.make_async_copy(k_hbm, k_ref, load.at[1]),
        pltpu.make_async_copy(down_hbm, v_down, load.at[2]),
        pltpu.make_async_copy(stem_hbm, v_stem, load.at[3]),
        pltpu.make_async_copy(lift_hbm, lift_ref, load.at[4]),
        pltpu.make_async_copy(deep_hbm, deep_ref, load.at[5]),
        pltpu.make_async_copy(merge_hbm, v_merge, load.at[6]),
        pltpu.make_async_copy(proj_hbm, v_proj, load.at[7]),
    ]
    for copy in loads:
        copy.start()
    ready()
    plan = (
        (u_hbm.at[pl.ds(depth - 2, 2)], ulo, after),
        (k_hbm.at[pl.ds(depth - 2, 2)], klo, after),
        (u_hbm.at[pl.ds(0, 2)], uhi, before),
        (k_hbm.at[pl.ds(0, 2)], khi, before),
    )
    copies = [
        pltpu.make_async_remote_copy(
            src_ref=src,
            dst_ref=dst,
            send_sem=send.at[i],
            recv_sem=recv.at[i],
            device_id=place(peer),
            device_id_type=MESH,
        )
        for i, (src, dst, peer) in enumerate(plan)
    ]
    upward, downward = copies[0:2], copies[2:4]

    @pl.when(above)
    def _():
        for copy in upward:
            copy.start()

    @pl.when(below)
    def _():
        for copy in downward:
            copy.start()

    @pl.when(me == 0)
    def _():
        ulo[...] = jnp.zeros_like(ulo)
        klo[...] = jnp.zeros_like(klo)

    @pl.when(me == total - 1)
    def _():
        uhi[...] = jnp.zeros_like(uhi)
        khi[...] = jnp.zeros_like(khi)

    rows, lanes = u_ref.shape[1:]
    row = lax.broadcasted_iota(jnp.int32, (rows, lanes), 0)
    lane = lax.broadcasted_iota(jnp.int32, (rows, lanes), 1)

    def step(up, uc, un, kp, kc, kn):
        flux = (kc + kn) * (un - uc) + (kc + kp) * (up - uc)
        for axis, place_, size in ((0, row, rows), (1, lane, lanes)):
            last = place_ == size - 1
            first = place_ == 0
            u_next = jnp.where(last, 0.0, pltpu.roll(uc, size - 1, axis))
            k_next = jnp.where(last, 0.0, pltpu.roll(kc, size - 1, axis))
            face = (kc + k_next) * (u_next - uc)
            back = jnp.where(first, kc * uc, pltpu.roll(face, 1, axis))
            flux = flux + (face - back)
        return uc + (0.5 * TIME_STEP) * flux

    for copy in loads:
        copy.wait()
    group = 7

    def interior(i, carry):
        for j in range(group):
            z = 1 + i * group + j
            h1[z + 1] = step(
                u_ref[z - 1], u_ref[z], u_ref[z + 1], k_ref[z - 1], k_ref[z], k_ref[z + 1]
            )
        return carry

    lax.fori_loop(0, (depth - 2) // group, interior, 0)

    def second(z):
        out_ref[z] = step(h1[z], h1[z + 1], h1[z + 2], k_ref[z - 1], k_ref[z], k_ref[z + 1])

    pack = 6

    def inner(i, carry):
        for j in range(pack):
            second(2 + i * pack + j)
        return carry

    lax.fori_loop(0, (depth - 4) // pack, inner, 0)
    unit = lax.broadcasted_iota(jnp.int32, (C2, C2), 0) == lax.broadcasted_iota(jnp.int32, (C2, C2), 1)
    eye = unit[0:C1, 0:C1]
    unit = unit.astype(BF16)
    stem_ref[...] = mm(unit[0:C1, 0:C1], v_stem[...], NT).astype(BF16)
    for dy in range(3):
        starts = [(j * 3 + dy) * C1 for j in range(9)]
        part = jnp.concatenate([v_down[r : r + C1, :] for r in starts], axis=0)
        down_ref[dy * C2 : (dy + 1) * C2, :] = mm(unit, part, NT).astype(BF16)
    for j in range(9):
        down_back[:, j * C2 : (j + 1) * C2] = v_down[j * 3 * C1 : (j + 1) * 3 * C1, :]

    def turned(x):
        return x.astype(F32).T.astype(BF16)

    lift_t[...] = turned(lift_ref[...])
    slot_tile[...] = jnp.full((16, GY), slot_ref[0].astype(F32)).astype(BF16)
    deep_t[...] = turned(deep_ref[...])
    fine = v_merge[:, 0:C1]
    coarse = v_merge[:, C1 : C1 + C2]
    fine_ref[...] = fine
    fine_t[...] = turned(fine)
    coarse_ref[...] = coarse
    coarse_t[...] = turned(coarse)
    row64 = v_proj[...].astype(F32)
    column = jnp.sum(jnp.where(eye, jnp.broadcast_to(row64, (C1, C1)), 0.0), axis=1, keepdims=True)
    proj_col[...] = jnp.broadcast_to(column, proj_col.shape)

    pz = pz_ref[0]
    px = px_ref[0]
    for z in range(PZ):
        patch_ref[1, z] = k_ref[pz + z, pl.ds(px, PX), :]
    meanwhile()

    @pl.when(below)
    def _():
        for copy in upward:
            copy.wait_recv()

    @pl.when(above)
    def _():
        for copy in downward:
            copy.wait_recv()

    has_lo = (me > 0).astype(F32)
    has_hi = (me < total - 1).astype(F32)
    ul, kl, uh, kh = ulo, klo, uhi, khi
    end = depth - 1
    h1[0] = has_lo * step(ul[0], ul[1], u_ref[0], kl[0], kl[1], k_ref[0])
    h1[1] = step(ul[1], u_ref[0], u_ref[1], kl[1], k_ref[0], k_ref[1])
    h1[depth] = step(u_ref[end - 1], u_ref[end], uh[0], k_ref[end - 1], k_ref[end], kh[0])
    h1[depth + 1] = has_hi * step(u_ref[end], uh[0], uh[1], k_ref[end], kh[0], kh[1])

    out_ref[0] = step(h1[0], h1[1], h1[2], kl[1], k_ref[0], k_ref[1])
    out_ref[end] = step(h1[end], h1[depth], h1[depth + 1], k_ref[end - 1], k_ref[end], kh[0])
    second(1)
    second(end - 1)
    for z in range(PZ):
        patch_ref[0, z] = h1[1 + pz + z, pl.ds(px, PX), :]
        patch_ref[2, z] = out_ref[pz + z, pl.ds(px, PX), :]

    @pl.when(above)
    def _():
        for copy in upward:
            copy.wait_send()

    @pl.when(below)
    def _():
        for copy in downward:
            copy.wait_send()


def silu_and_slope(z):
    s = 0.5 * jnp.tanh(0.5 * z) + 0.5
    value = z * s
    return value, s + value * (1.0 - s)


def block(x, b):
    return x[:, b * GY : (b + 1) * GY]


def stem_columns(patch_ref, tall, channel):
    row8 = lax.broadcasted_iota(jnp.int32, (PX, GY), 0)
    lane8 = lax.broadcasted_iota(jnp.int32, (PX, GY), 1)
    for dx in range(3):
        for dy in range(3):
            shifted = []
            for z in range(PZ):
                v = rounded(patch_ref[channel, z])
                if dx == 0:
                    v = jnp.where(row8 == 0, 0.0, pltpu.roll(v, 1, 0))
                elif dx == 2:
                    v = jnp.where(row8 == PX - 1, 0.0, pltpu.roll(v, PX - 1, 0))
                if dy == 0:
                    v = jnp.where(lane8 == 0, 0.0, pltpu.roll(v, 1, 1))
                elif dy == 2:
                    v = jnp.where(lane8 == GY - 1, 0.0, pltpu.roll(v, GY - 1, 1))
                shifted.append(v)
            for dz in range(3):
                r = ((dz * 3 + dx) * 3 + dy) * 2 + channel
                for z in range(PZ):
                    if 0 <= z + dz - 1 < PZ:
                        tall[pl.ds(z * PX * C1 + r, PX, stride=C1), :] = shifted[z + dz - 1]


def train_part(
    scale,
    n_sec,
    n_hi,
    n_lo,
    slot_tile,
    patch_ref,
    w_stem,
    w_lift,
    w_lift_t,
    w_down,
    wback,
    w_deep,
    w_deep_t,
    w_fine,
    w_fine_t,
    w_coarse,
    w_coarse_t,
    w_proj_col,
    pred_out,
    buf2,
    tall,
    cols,
    l1,
    l2,
    g1,
    g2,
    dz_ref,
    dz2_ref,
    colsd,
    colsz,
    pack,
    pair,
    grads,
    packet,
    buf1,
    acc,
    pbuf,
    q_ref,
    qbuf,
    s1,
    r1,
    s2,
    r2,
    s3,
    r3,
    s4,
    r4,
):
    sec = lax.axis_index("section")
    dp = lax.axis_index("dp")
    hi = lax.div(dp, n_lo)
    lo = lax.rem(dp, n_lo)
    across = n_sec * n_hi
    mine = sec * n_hi + hi

    def in_line(d):
        peer = lax.rem(lo + d, n_lo)
        return peer, (sec, hi * n_lo + peer)

    def in_column(d):
        peer = lax.rem(mine + d, across)
        return peer, (lax.div(peer, n_hi), lax.rem(peer, n_hi) * n_lo + lo)

    def in_part(d):
        peer = lax.rem(hi + d, n_hi)
        return peer, (sec, peer * n_lo + lo)

    def send(src, dst, ssem, rsem, device):
        copy = pltpu.make_async_remote_copy(
            src_ref=src, dst_ref=dst, send_sem=ssem, recv_sem=rsem, device_id=device, device_id_type=MESH
        )
        copy.start()
        return copy

    def group(like, ssem, rsem, device):
        return pltpu.make_async_remote_copy(
            src_ref=like, dst_ref=like, send_sem=ssem, recv_sem=rsem, device_id=device, device_id_type=MESH
        )

    plane = PX * GY
    cells = PZ * plane
    small = cells // 4
    row8 = lax.broadcasted_iota(jnp.int32, (PX, GY), 0)
    lane8 = lax.broadcasted_iota(jnp.int32, (PX, GY), 1)
    lane64 = lax.broadcasted_iota(jnp.int32, (C1, GY), 1)

    stem_columns(patch_ref, tall, 0)
    for b in range(PZ * PX):
        cols[:, b * GY : (b + 1) * GY] = tall[b * C1 : (b + 1) * C1, :].astype(BF16)

    taps = w_stem.shape[1]
    stem = w_stem[...]
    lift = w_lift[...]
    pooled = []
    for zz in range(PZ // 2):
        rows = []
        for z in (2 * zz, 2 * zz + 1):
            here = slice(z * plane, (z + 1) * plane)
            value, slope = silu_and_slope(mm(stem, cols[0:taps, here]))
            g1[:, here] = slope
            one = value.astype(BF16)
            l1[:, here] = one
            value, slope = silu_and_slope(mm(lift, one))
            g2[:, here] = slope
            two = value.astype(BF16)
            l2[:, here] = two
            rows.append(two.astype(F32))
        both = rows[0] + rows[1]
        for xx in range(PX // 2):
            pooled.append(rounded((block(both, 2 * xx) + block(both, 2 * xx + 1)) * 0.25))

    hz, hx = PZ // 2, PX // 2
    pooled = [v.astype(BF16) for v in pooled]
    for dz in range(3):
        for dx in range(3):
            r = (dz * 3 + dx) * C1
            for z in range(hz):
                for x in range(hx):
                    sz, sx = z + dz - 1, x + dx - 1
                    inside = 0 <= sz < hz and 0 <= sx < hx
                    b = z * hx + x
                    if inside:
                        colsd[r : r + C1, b * GY : (b + 1) * GY] = pooled[sz * hx + sx]
    depth = 9 * C1
    products = mm(w_down[...], colsd[0:depth, :])
    lane128 = lax.broadcasted_iota(jnp.int32, (C2, GY), 1)

    def later(v):
        return jnp.where(lane128 == 0, 0.0, pltpu.roll(v, 1, 1))

    def sooner(v):
        return jnp.where(lane128 == GY - 1, 0.0, pltpu.roll(v, GY - 1, 1))

    summed = []
    for b in range(hz * hx):
        v = block(products, b)
        summed.append(later(v[0:C2]) + v[C2 : 2 * C2] + sooner(v[2 * C2 : 3 * C2]))
    value, slope_down = silu_and_slope(jnp.concatenate(summed, axis=1))
    coarse = value.astype(BF16)
    value, slope_deep = silu_and_slope(mm(w_deep[...], coarse))
    deeper = value.astype(BF16)
    merge_fine = w_fine[...]
    lifted = mm(w_coarse[...], deeper)

    out_col = w_proj_col[...]
    fine_t = w_fine_t[...]
    d_out = jnp.zeros((C1, GY), F32)
    gathered = [None] * (hz * hx)
    forecast = []
    for z in range(PZ):
        here = slice(z * plane, (z + 1) * plane)
        two = l2[:, here]
        added = [block(lifted, (z // 2) * hx + x // 2) for x in range(PX)]
        value, slope = silu_and_slope(mm(merge_fine, two) + jnp.concatenate(added, axis=1))
        merged = value.astype(BF16)
        held = merged.astype(F32)
        predicted = jnp.zeros((PX, GY), F32)
        for x in range(PX):
            summed = jnp.sum(block(held, x) * out_col, axis=0, keepdims=True)
            predicted = jnp.where(row8 == x, summed, predicted)
        forecast.append(predicted)
        misfit = (predicted - rounded(patch_ref[2, z])) * scale
        for x in range(PX):
            d_out = d_out + block(held, x) * misfit[x : x + 1, :]
        d_merged = jnp.concatenate([out_col * misfit[x : x + 1, :] for x in range(PX)], axis=1)
        dz = rounded(d_merged) * slope
        for x in range(PX):
            b = (z // 2) * hx + x // 2
            gathered[b] = block(dz, x) if gathered[b] is None else gathered[b] + block(dz, x)
        dz = dz.astype(BF16)
        dz_ref[:, here] = dz

    half = PZ * PX // 2
    packet[0:half, :] = jnp.concatenate(forecast[0 : PZ // 2], axis=0).astype(BF16)
    packet[half : 2 * half, :] = jnp.concatenate(forecast[PZ // 2 : PZ], axis=0).astype(BF16)
    packet[2 * half : 2 * half + 16, :] = slot_tile[...]
    d_lifted = jnp.concatenate(gathered, axis=1).astype(BF16)
    d_deeper = mm(w_coarse_t[...], d_lifted)
    dz_deep = (rounded(d_deeper) * slope_deep).astype(BF16)
    d_coarse = mm(w_deep_t[...], dz_deep)
    dz_down = (rounded(d_coarse) * slope_down).astype(BF16)

    r_ = lax.broadcasted_iota(jnp.int32, (C2, C2), 0)
    c_ = lax.broadcasted_iota(jnp.int32, (C2, C2), 1)
    parted = jnp.where(r_ < C1, 2 * r_, 2 * r_ - (C2 - 1)) == c_
    dz_parted = mm(parted.astype(BF16), dz_down)
    blocks = [block(dz_parted, b) for b in range(hz * hx)]
    dz_shifts = jnp.concatenate(
        [
            jnp.concatenate([f(v) for v in blocks], axis=1).astype(BF16)
            for f in (sooner, lambda v: v, later)
        ],
        axis=0,
    )
    d_down = mm(dz_shifts, colsd[...], NT)
    low = lane64 < C1
    turned_chunks = {}

    def piece(h, lanes_low):
        odd, h = divmod(h, 27)
        zx, dy = divmod(h, 3)
        q, high = divmod(zx, 2)
        r = dy * C2 + odd * C1
        chunk = d_down[r : r + C1, q * GY : (q + 1) * GY]
        if bool(high) != lanes_low:
            return chunk
        if (r, q) not in turned_chunks:
            turned_chunks[r, q] = pltpu.roll(chunk, C1, 1)
        return turned_chunks[r, q]

    base = 27 + 32
    for j in range(27):
        pack[pl.ds(base + j, C1, stride=27), :] = jnp.where(
            low, piece(2 * j, True), piece(2 * j + 1, False)
        )

    per = grads.shape[2]
    first = -(-(27 + 32) // (per * n_lo))
    top = n_hi - (27 + 32 + 27 * C1) // (per * n_lo)
    tail = first + top

    def emit(hi_):
        for lo_ in range(n_lo):
            start = (hi_ * n_lo + lo_) * per
            grads[lo_, (hi_ + top) % n_hi] = pack[start : start + per, :].astype(BF16)

    for h in range(first, n_hi - top):
        emit(h)

    def scatter(begin, count, i):
        part = pl.ds(begin, count)
        for d in range(1, n_lo):
            peer, device = in_line(d)
            send(grads.at[peer, part], buf1.at[d - 1, part], s1.at[i], r1.at[i], device)
        return group(buf1.at[:, part], s1.at[i], r1.at[i], device)

    early = scatter(tail, n_hi - tail, 0)
    for d in range(1, n_hi):
        peer, device = in_part(d)
        send(packet, pbuf.at[d], s3, r3, device)
    packets = group(pbuf.at[pl.ds(1, n_hi - 1)], s3, r3, device)
    pbuf[0] = packet[...]

    def twice(x):
        pair[:, 0:C1] = x
        pair[:, C1:GY] = jnp.zeros((C1, GY - C1), F32)
        once = pair[...]
        return once + pltpu.roll(once, C1, 1)

    d_coarse_merge = mm(d_lifted, deeper, NT)
    d_deep = mm(dz_deep, coarse, NT)
    d_fine = twice(mm(dz_ref[...], l2[...], NT))
    low32 = lax.broadcasted_iota(jnp.int32, (32, GY), 1) < C1
    base = 27 + 32 + 27 * C1
    pack[base : base + C2, :] = d_deep
    base = base + C2
    pair[...] = d_fine
    fine_even_odd = [pair[pl.ds(i, 32, stride=2), :] for i in range(2)]
    pair[...] = d_coarse_merge
    coarse_even_odd = [pair[pl.ds(i, 32, stride=2), :] for i in range(2)]
    turn = pltpu.roll(coarse_even_odd[0], C1, 1)
    pack[pl.ds(base, 32, stride=3), :] = jnp.where(low32, fine_even_odd[0], turn)
    pack[pl.ds(base + 1, 32, stride=3), :] = jnp.where(low32, turn, fine_even_odd[1])
    pack[pl.ds(base + 2, 32, stride=3), :] = coarse_even_odd[1]
    base = base + 96
    column = jnp.sum(d_out, axis=1, keepdims=True)
    across_ = lane64 == lax.broadcasted_iota(jnp.int32, (C1, GY), 0)
    pack[base : base + 1, :] = jnp.sum(
        jnp.where(across_, jnp.broadcast_to(column, (C1, GY)), 0.0), axis=0, keepdims=True
    )
    pack[base + 1 : GROWS, :] = jnp.zeros((GROWS - base - 1, GY), F32)


    for dz in range(3):
        for dx in range(3):
            j = dz * 3 + dx
            for z in range(hz):
                for x in range(hx):
                    sz, sx = z - (dz - 1), x - (dx - 1)
                    inside = 0 <= sz < hz and 0 <= sx < hx
                    b = z * hx + x
                    if inside:
                        colsz[j * C2 : (j + 1) * C2, b * GY : (b + 1) * GY] = block(
                            dz_down, sz * hx + sx
                        )
    d_shifted = mm(wback[...], colsz[...])
    d_pooled = []
    for b in range(hz * hx):
        whole = block(d_shifted, b)
        total = whole[C1 : 2 * C1]
        total = total + jnp.where(lane64 == GY - 1, 0.0, pltpu.roll(whole[0:C1], GY - 1, 1))
        total = total + jnp.where(lane64 == 0, 0.0, pltpu.roll(whole[2 * C1 : 3 * C1], 1, 1))
        d_pooled.append(rounded(total) * 0.25)

    lift_t = w_lift_t[...]
    d_stem = jnp.zeros((C1, C1), F32)
    for z in range(PZ):
        here = slice(z * plane, (z + 1) * plane)
        spread = jnp.concatenate([d_pooled[(z // 2) * hx + x // 2] for x in range(PX)], axis=1)
        dz = ((rounded(mm(fine_t, dz_ref[:, here])) + spread) * g2[:, here]).astype(BF16)
        dz2_ref[:, here] = dz
        d_one = rounded(mm(lift_t, dz))
        dz = (d_one * g1[:, here]).astype(BF16)
        d_stem = d_stem + mm(dz, cols[:, here], NT)

    d_lift = twice(mm(dz2_ref[...], l1[...], NT))

    pair[:, 0:C1] = d_stem
    pair[:, C1:GY] = jnp.zeros((C1, GY - C1), F32)
    turned = pair[...]
    source = lax.broadcasted_iota(jnp.int32, (C1, GY), 0)
    for bit in range(6):
        moved = pltpu.roll(turned, (taps << bit) % GY, 1)
        turned = jnp.where((source >> bit) % 2 == 1, moved, turned)
    begin = source * taps
    wraps = lane64 < begin % GY
    stay = jnp.where(wraps, 0.0, turned).astype(BF16)
    over = jnp.where(wraps, turned, 0.0).astype(BF16)
    target_row = lax.broadcasted_iota(jnp.int32, (32, C1), 0)
    owner = lax.broadcasted_iota(jnp.int32, (32, C1), 1) * taps // GY
    stem_rows = mm((target_row == owner).astype(BF16), stay)
    stem_rows = stem_rows + mm((target_row == owner + 1).astype(BF16), over)
    pack[0:27, :] = stem_rows[0:27, :]

    low32 = lax.broadcasted_iota(jnp.int32, (32, GY), 1) < C1
    pair[...] = d_lift
    pack[27 : 27 + 32, :] = jnp.where(low32, pair[pl.ds(0, 32, stride=2), :], pair[pl.ds(1, 32, stride=2), :])


    for h in list(range(first)) + list(range(n_hi - top, n_hi)):
        emit(h)
    late = scatter(0, tail, 1)

    def line_sum(h):
        at = (h + top) % n_hi
        value = grads[lo, at].astype(F32)
        for d in range(n_lo - 1):
            value = value + buf1[d, at].astype(F32)
        acc[h] = value.astype(BF16)

    early.wait_recv()
    for h in range(first, n_hi - top):
        line_sum(h)
    late.wait_recv()
    for h in list(range(first)) + list(range(n_hi - top, n_hi)):
        line_sum(h)
    ring = 8
    far_first = sorted(range(1, n_hi + 1), key=lambda e: (e == n_hi, -min(e % ring, ring - e % ring)))
    for e in far_first:
        h = lax.rem(hi + e, n_hi)
        for q in range(n_sec):
            if e == n_hi and q == 0:
                buf2[mine] = acc[h]
                continue
            owner = lax.rem(sec + q, n_sec)
            device = (owner, h * n_lo + lo)
            send(acc.at[h], buf2.at[mine], s2, r2, device)
    partials = group(buf2.at[pl.ds(0, across - 1)], s2, r2, device)

    packets.wait_recv()
    rows = PZ * PX

    def route(q, carry):
        wanted = (hi * (2 * n_lo) + q).astype(F32)
        value = jnp.zeros((rows, GY), F32)
        for src in range(n_hi):
            named = pbuf[src, rows : rows + 16, :].astype(F32)
            named = jnp.concatenate([named] * (rows // 16), axis=0)
            value = value + jnp.where(named == wanted, pbuf[src, 0:rows, :].astype(F32), 0.0)
        q_ref[q] = value.astype(BF16)
        return carry

    lax.fori_loop(0, 2 * n_lo, route, 0)
    for d in range(1, n_lo):
        peer, device = in_line(d)
        send(q_ref.at[pl.ds(2 * peer, 2)], qbuf.at[d - 1], s4, r4, device)
    routed = group(qbuf, s4, r4, device)

    routed.wait_recv()
    for s in range(2):
        value = q_ref[2 * lo + s].astype(F32)
        for d in range(n_lo - 1):
            value = value + qbuf[d, s].astype(F32)
        pred_out[s] = value

    partials.wait_recv()
    for copy in (packets, early, late, routed, partials):
        copy.wait_send()


def whole_kernel(n_sec, n_hi, n_lo, scale, *refs):
    ins, refs = refs[:11], refs[11:]
    (heat_out, pred_out, buf2), refs = refs[:3], refs[3:]
    made, refs = refs[:14], refs[14:]
    heat_scratch, train_scratch = refs[:14], refs[14:]
    sec = lax.axis_index("section")
    dp = lax.axis_index("dp")
    hi = lax.div(dp, n_lo)
    lo = lax.rem(dp, n_lo)
    across = n_sec * n_hi
    mine = sec * n_hi + hi
    n_dp = n_hi * n_lo
    total = n_sec * n_dp
    me = sec * n_dp + dp
    barrier = pltpu.get_barrier_semaphore()
    at_start = jnp.logical_and(lo == 0, me > 0)
    at_end = jnp.logical_and(lo == n_lo - 1, me < total - 1)
    outside = jnp.logical_or(at_start, at_end)

    def signal(section, index):
        pl.semaphore_signal(barrier, inc=1, device_id=(section, index), device_id_type=MESH)

    def enter():
        @pl.when(at_start)
        def _():
            signal(lax.div(me - 1, n_dp), lax.rem(me - 1, n_dp))

        @pl.when(at_end)
        def _():
            signal(lax.div(me + 1, n_dp), lax.rem(me + 1, n_dp))

        for d in sorted(range(1, across), key=lambda d: (d % 8 == 0, d % 8)):
            peer = lax.rem(mine + d, across)
            signal(lax.div(peer, n_hi), lax.rem(peer, n_hi) * n_lo + lo)
        for d in range(1, n_lo):
            signal(sec, hi * n_lo + lax.rem(lo + d, n_lo))

    def ready():
        peers = n_lo - 1 + across - 1

        @pl.when(outside)
        def _():
            pl.semaphore_wait(barrier, peers + 1)

        @pl.when(jnp.logical_not(outside))
        def _():
            pl.semaphore_wait(barrier, peers)

    patch, *weights, slot_tile = made
    tall, colsd, colsz = train_scratch[0], train_scratch[8], train_scratch[9]

    def meanwhile():
        for cleared in (tall, colsd, colsz):
            cleared[...] = jnp.zeros_like(cleared)
        stem_columns(patch, tall, 1)

    heat_part(enter, ready, meanwhile, n_sec, n_dp, *ins, heat_out, *made, *heat_scratch)
    train_part(scale, n_sec, n_hi, n_lo, slot_tile, patch, *weights, pred_out, buf2, *train_scratch)


def whole(scale, n_sec, n_hi, n_lo, heat, cond, patch_z, patch_x, slot, weights):
    layers = (2,) + heat.shape[1:]
    taps = weights[0].shape[0]
    cells = PZ * PX * GY
    small = cells // 4
    per = GROWS // (n_lo * n_hi)
    across = n_sec * n_hi
    dma = pltpu.SemaphoreType.DMA
    operands = (heat, cond, *weights)
    operands = [pltpu.with_memory_space_constraint(x, pltpu.HBM) for x in operands]
    return pl.pallas_call(
        functools.partial(whole_kernel, n_sec, n_hi, n_lo, scale),
        out_shape=(
            jax.ShapeDtypeStruct(heat.shape, F32),
            jax.ShapeDtypeStruct((2, PZ * PX, GY), F32),
            jax.ShapeDtypeStruct((across, per, GY), BF16),
        ),
        in_specs=[SMEM] * 3 + [HBM] * 8,
        out_specs=(VMEM,) * 3,
        scratch_shapes=[
            pltpu.VMEM((3, PZ, PX, GY), F32),
            pltpu.VMEM((C1, taps), BF16),
            pltpu.VMEM((C1, C1), BF16),
            pltpu.VMEM((C1, C1), BF16),
            pltpu.VMEM((3 * C2, 9 * C1), BF16),
            pltpu.VMEM((3 * C1, 9 * C2), BF16),
            pltpu.VMEM((C2, C2), BF16),
            pltpu.VMEM((C2, C2), BF16),
            pltpu.VMEM((C1, C1), BF16),
            pltpu.VMEM((C1, C1), BF16),
            pltpu.VMEM((C1, C2), BF16),
            pltpu.VMEM((C2, C1), BF16),
            pltpu.VMEM((C1, GY), F32),
            pltpu.VMEM((16, GY), BF16),
            pltpu.VMEM(weights[0].shape, BF16),
            pltpu.VMEM(weights[2].shape, BF16),
            pltpu.VMEM(weights[4].shape, BF16),
            pltpu.VMEM(weights[5].shape, BF16),
            pltpu.VMEM(heat.shape, F32),
            pltpu.VMEM(heat.shape, F32),
            pltpu.VMEM(layers, F32),
            pltpu.VMEM(layers, F32),
            pltpu.VMEM(layers, F32),
            pltpu.VMEM(layers, F32),
            pltpu.VMEM((heat.shape[0] + 2,) + heat.shape[1:], F32),
            dma((8,)),
            dma((4,)),
            dma((4,)),
            pltpu.VMEM((PZ * PX * C1, GY), F32),
            pltpu.VMEM((C1, cells), BF16),
            pltpu.VMEM((C1, cells), BF16),
            pltpu.VMEM((C1, cells), BF16),
            pltpu.VMEM((C1, cells), F32),
            pltpu.VMEM((C1, cells), F32),
            pltpu.VMEM((C1, cells), BF16),
            pltpu.VMEM((C1, cells), BF16),
            pltpu.VMEM((10 * C1, small), BF16),
            pltpu.VMEM((9 * C2, small), BF16),
            pltpu.VMEM((GROWS, GY), F32),
            pltpu.VMEM((C1, GY), F32),
            pltpu.VMEM((n_lo, n_hi, per, GY), BF16),
            pltpu.VMEM((PZ * PX + 16, GY), BF16),
            pltpu.VMEM((n_lo - 1, n_hi, per, GY), BF16),
            pltpu.VMEM((n_hi, per, GY), BF16),
            pltpu.VMEM((n_hi, PZ * PX + 16, GY), BF16),
            pltpu.VMEM((2 * n_lo, PZ * PX, GY), BF16),
            pltpu.VMEM((n_lo - 1, 2, PZ * PX, GY), BF16),
            dma((2,)),
            dma((2,)),
            dma,
            dma,
            dma,
            dma,
            dma,
            dma,
        ],
        compiler_params=pltpu.CompilerParams(
            collective_id=0, has_side_effects=True, vmem_limit_bytes=48 * 2**20
        ),
        name="whole",
    )(patch_z, patch_x, slot, *operands)


def finish_kernel(heat_in, pred_in, grad_in, heat_out, pred_out, grad_out, done):
    copy = pltpu.make_async_copy(heat_in, heat_out, done)
    copy.start()
    total = grad_in[0].astype(F32)
    for t in range(1, grad_in.shape[0]):
        total = total + grad_in[t].astype(F32)
    grad_out[...] = total
    for s in range(2):
        for z in range(PZ):
            pred_out[s, z] = pred_in[s, z * PX : (z + 1) * PX, :].astype(BF16)
    copy.wait()


def finish(heat, preds, partials):
    return pl.pallas_call(
        finish_kernel,
        out_shape=(
            jax.ShapeDtypeStruct(heat.shape, F32),
            jax.ShapeDtypeStruct((2, PZ, PX, GY), BF16),
            jax.ShapeDtypeStruct(partials.shape[1:], F32),
        ),
        in_specs=[pl.BlockSpec(memory_space=pl.ANY), VMEM, VMEM],
        out_specs=(HBM, VMEM, VMEM),
        scratch_shapes=[pltpu.SemaphoreType.DMA],
        compiler_params=pltpu.CompilerParams(vmem_limit_bytes=8 * 2**20),
        name="finish",
    )(heat, preds, partials)


def local(
    n_sec,
    n_dp,
    heat_start,
    conductivity,
    patch_z,
    patch_x,
    slot_table,
    w_stem,
    w_lift,
    w_down,
    w_deep,
    w_merge,
    w_out,
):
    n_lo = LINE
    n_hi = n_dp // n_lo
    weights = (w_stem.T, w_lift, w_down.T, w_deep, w_merge, w_out)
    scale = 1.0 / (n_sec * n_dp * PZ * PX * GY)
    heat_two, preds, partials = whole(
        scale, n_sec, n_hi, n_lo, heat_start, conductivity, patch_z, patch_x, slot_table, weights
    )
    return finish(heat_two, preds, partials)


def solution(mesh):
    n_sec, n_dp = mesh.shape["section"], mesh.shape["dp"]
    both = ("section", "dp")
    return jax.shard_map(
        functools.partial(local, n_sec, n_dp),
        mesh=mesh,
        in_specs=(P(both, None, None), P(both, None, None), P(both), P(both), P(both)) + (P(),) * 6,
        out_specs=(P(both, None, None), P(both, None, None, None), P("dp", None)),
        check_vma=False,
    )
```
